32 devices in a mesh: dp: 4 (over y, x), ctx: 8 (over z, core).
Axes of the slice: x: 2, y: 2, z: 4, core: 2. Of those that a mesh axis runs over, the one named last changes fastest.
Arguments:
- layer_input: bfloat16 [4, 1024, 2048], P('dp', 'ctx'), may hold values from -6 to 6
- prefix: int32 [4], P('dp'), may hold values from 102 to 512
- wq: bfloat16 [2048, 2048], P(('dp', 'ctx')), may hold values from -0.125 to 0.125
- wk: bfloat16 [2048, 1024], P(('dp', 'ctx')), may hold values from -0.125 to 0.125
- wv: bfloat16 [2048, 1024], P(('dp', 'ctx')), may hold values from -0.125 to 0.125
- wo: bfloat16 [2048, 2048], P(('dp', 'ctx')), may hold values from -2 to 2
- w_gate: bfloat16 [2048, 6144], P(('dp', 'ctx')), may hold values from -0.125 to 0.125
- w_up: bfloat16 [2048, 6144], P(('dp', 'ctx')), may hold values from -0.125 to 0.125
- w_down: bfloat16 [6144, 2048], P(('dp', 'ctx')), may hold values from -0.078125 to 0.078125
- gains: bfloat16 [4352], P(('dp', 'ctx')), may hold values from 0.5 to 1.5
- cotangent: bfloat16 [4, 1024, 2048], P('dp', 'ctx'), may hold values from -6 to 6
Outputs:
- layer_output: bfloat16 [4, 1024, 2048], P('dp', 'ctx')
- x_grad: bfloat16 [4, 1024, 2048], P('dp', 'ctx')
- wq_grad: float32 [2048, 2048], P(('dp', 'ctx'))
- wk_grad: float32 [2048, 1024], P(('dp', 'ctx'))
- wv_grad: float32 [2048, 1024], P(('dp', 'ctx'))
- wo_grad: float32 [2048, 2048], P(('dp', 'ctx'))
- gate_grad: float32 [2048, 6144], P(('dp', 'ctx'))
- up_grad: float32 [2048, 6144], P(('dp', 'ctx'))
- down_grad: float32 [6144, 2048], P(('dp', 'ctx'))
- gains_grad: float32 [4352], P(('dp', 'ctx'))
The draws below stay inside these ranges and needn't reach their ends.
Inputs may be any that keep to these rules, and one draw needn't show every extreme that they name: prefix[s] keys at the start of sequence s are seen by every query of that sequence.
All inputs are finite; a program needn't handle non-finite values.
Results may differ from the reference program's by a relative error of at most 0.015.
Values may be sent and summed in bfloat16 or wider, within the bound.
A program may use at most 512 MiB of HBM per device.

```python
import math
import jax
import jax.numpy as jnp
from jax import lax

MODEL_WIDTH = 2048
FF = 6144
QUERY_HEADS = 16
KEY_VALUE_HEADS = 8
HEAD_SIZE = 128
SEQS = 4
SEQ_LEN = 1024
GAINS = 4352


def place_ends(entries, own_key, low, high):
    longest = entries.shape.index(max(entries.shape))
    spots = []
    for shift in (0, 1):
        where = [jax.random.randint(jax.random.fold_in(own_key, axis), (), 0, length) for axis, length in enumerate(entries.shape)]
        where[longest] = (where[longest] + shift) % entries.shape[longest]
        spots.append(tuple(where))
    return entries.at[spots[0]].set(low).at[spots[1]].set(high)


def levels(key, dims, shards, low, largest):
    level = 1.0
    for position, parts in shards:
        draws = jax.random.uniform(jax.random.fold_in(jax.random.fold_in(key, 6), position), (parts,), jnp.float32, low / len(shards), largest / len(shards))
        level = level * jnp.repeat(jnp.exp(draws), dims[position] // parts).reshape((-1,) + (1,) * (len(dims) - 1 - position))
    return level


def gaussian(rng, dims, width, bound, pieces=(), kind=jnp.bfloat16):
    values = width * jax.random.normal(rng, dims, jnp.float32)
    if pieces:
        values = values * levels(rng, dims, pieces, -0.22, 0.18)
    return jnp.clip(values, -bound, bound).astype(kind)


def setup_inputs(seed: int = 0) -> dict:
    seeds = jax.random.split(jax.random.key(seed), 12)
    return {
        "layer_input": gaussian(seeds[0], (SEQS, SEQ_LEN, MODEL_WIDTH), 1.0, 6.0, ((0, 4), (1, 8))),
        "prefix": place_ends(jax.random.randint(seeds[1], (SEQS,), SEQ_LEN // 10, SEQ_LEN // 2 + 1), jax.random.fold_in(seeds[1], 1), SEQ_LEN // 10, (SEQ_LEN // 2 + 1) - 1).astype(jnp.int32),
        "wq": gaussian(seeds[2], (MODEL_WIDTH, QUERY_HEADS * HEAD_SIZE), MODEL_WIDTH ** -0.5, 0.125, ((0, 32),)),
        "wk": gaussian(seeds[3], (MODEL_WIDTH, KEY_VALUE_HEADS * HEAD_SIZE), MODEL_WIDTH ** -0.5, 0.125, ((0, 32),)),
        "wv": gaussian(seeds[4], (MODEL_WIDTH, KEY_VALUE_HEADS * HEAD_SIZE), MODEL_WIDTH ** -0.5, 0.125, ((0, 32),)),
        "wo": gaussian(seeds[5], (QUERY_HEADS * HEAD_SIZE, MODEL_WIDTH), (max(1, QUERY_HEADS * HEAD_SIZE * 4 // SEQ_LEN)) ** -0.5, 2.0, ((0, 32),)),
        "w_gate": gaussian(seeds[6], (MODEL_WIDTH, FF), MODEL_WIDTH ** -0.5, 0.125, ((0, 32),)),
        "w_up": gaussian(seeds[7], (MODEL_WIDTH, FF), MODEL_WIDTH ** -0.5, 0.125, ((0, 32),)),
        "w_down": gaussian(seeds[8], (FF, MODEL_WIDTH), FF ** -0.5, 0.078125, ((0, 32),)),
        "gains": jnp.clip(1.0 + 0.1 * jax.random.normal(seeds[9], (GAINS,), jnp.float32), 0.5, 1.5).astype(jnp.bfloat16),
        "cotangent": gaussian(seeds[10], (SEQS, SEQ_LEN, MODEL_WIDTH), 1.0, 6.0, ((0, 4), (1, 8))),
    }


EPSILON = 1e-06
ROPE_BASE = 1000000.0
HIGH = lax.Precision.HIGHEST

@jax.custom_vjp
def lower_precision(v):
    return lax.optimization_barrier(v.astype(jnp.bfloat16)).astype(jnp.float32)

@jax.custom_vjp
def lower_precision_backward(v):
    return v

def low_keep(v):
    return (lower_precision(v), None)

def low_pass(kept, grad):
    return (grad,)

def back_keep(v):
    return (v, None)

def back_low(kept, grad):
    return (lower_precision(grad),)
lower_precision.defvjp(low_keep, low_pass)
lower_precision_backward.defvjp(back_keep, back_low)

def rms_scale(value, gain):
    return value * lax.rsqrt(lax.optimization_barrier(jnp.mean(value * value, -1, keepdims=True)) + EPSILON) * gain

def rotate(value, cosine, sine):
    half = value.shape[-1] // 2
    first = value[..., :half]
    second = value[..., half:]
    return jnp.concatenate([first * cosine - second * sine, second * cosine + first * sine], -1)

def matrix_product(left, right):
    return jnp.dot(left, right, precision=HIGH, preferred_element_type=jnp.float32)

def layer(inputs, limit, wq, wk, wv, wo, w_gate, w_up, w_down, gains):
    sequence_length = inputs.shape[0]
    query_group_size = QUERY_HEADS // KEY_VALUE_HEADS
    scale = 1.0 / math.sqrt(HEAD_SIZE)
    gain_one = gains[:MODEL_WIDTH]
    gain_two = gains[MODEL_WIDTH:2 * MODEL_WIDTH]
    gain_q = gains[2 * MODEL_WIDTH:2 * MODEL_WIDTH + HEAD_SIZE]
    gain_k = gains[2 * MODEL_WIDTH + HEAD_SIZE:]
    positions = jnp.arange(sequence_length, dtype=jnp.int32)
    freqs = ROPE_BASE ** (-(jnp.arange(HEAD_SIZE // 2, dtype=jnp.float32) * 2.0 / HEAD_SIZE))
    angles = positions.astype(jnp.float32)[:, None] * freqs[None, :]
    cosine = jnp.cos(angles)[:, None, :]
    sine = jnp.sin(angles)[:, None, :]
    normalized_rows = lower_precision(rms_scale(inputs, gain_one))
    query_rows = lower_precision_backward(matrix_product(normalized_rows, wq)).reshape(sequence_length, QUERY_HEADS, HEAD_SIZE)
    key_rows = lower_precision_backward(matrix_product(normalized_rows, wk)).reshape(sequence_length, KEY_VALUE_HEADS, HEAD_SIZE)
    value_rows = lower_precision(lower_precision_backward(matrix_product(normalized_rows, wv))).reshape(sequence_length, KEY_VALUE_HEADS, HEAD_SIZE)
    query_rows = lower_precision(rotate(rms_scale(query_rows, gain_q), cosine, sine))
    key_rows = lower_precision(rotate(rms_scale(key_rows, gain_k), cosine, sine))
    rows_per_block = math.gcd(sequence_length, 512)
    block_list = sequence_length // rows_per_block
    query_block_list = query_rows.reshape(block_list, rows_per_block, KEY_VALUE_HEADS, query_group_size, HEAD_SIZE)
    starts = jnp.arange(block_list, dtype=jnp.int32) * rows_per_block

    def attend(item):
        block, start = item
        qpos = start + jnp.arange(rows_per_block, dtype=jnp.int32)
        visible = (positions[None, :] <= qpos[:, None]) | (positions[None, :] < limit)
        scores = lower_precision_backward(scale * jnp.einsum('thgd,shd->hgts', block, key_rows, precision=HIGH))
        scores = jnp.where(visible[None, None], scores, -1e+30)
        probs = lower_precision(jax.nn.softmax(scores, -1))
        return jnp.einsum('hgts,shd->thgd', probs, value_rows, precision=HIGH)
    attended = lax.map(jax.checkpoint(attend), (query_block_list, starts))
    attended = lower_precision(lower_precision_backward(attended.reshape(sequence_length, QUERY_HEADS * HEAD_SIZE)))
    hidden = inputs + lower_precision_backward(matrix_product(attended, wo))
    normed_two = lower_precision(rms_scale(hidden, gain_two))
    gate = lower_precision_backward(matrix_product(normed_two, w_gate))
    up = lower_precision_backward(matrix_product(normed_two, w_up))
    active = lower_precision(jax.nn.silu(gate) * up)
    return hidden + lower_precision_backward(matrix_product(active, w_down))

def reference(layer_input, prefix, wq, wk, wv, wo, w_gate, w_up, w_down, gains, cotangent):
    weights = tuple((a.astype(jnp.float32) for a in (wq, wk, wv, wo, w_gate, w_up, w_down, gains)))

    def step(carry, item):
        inputs, limit, upstream = item

        def apply(value, *params):
            return layer(value, limit, *params)
        output, back = jax.vjp(apply, inputs.astype(jnp.float32), *weights)
        grads = back(upstream.astype(jnp.float32))
        summed = tuple((c + g for c, g in zip(carry, grads[1:])))
        return (summed, (output.astype(jnp.bfloat16), grads[0].astype(jnp.bfloat16)))
    zeros = tuple((jnp.zeros(w.shape, jnp.float32) for w in weights))
    totals, (outputs, input_grads) = lax.scan(step, zeros, (layer_input, prefix, cotangent))
    return (outputs, input_grads, totals[0], totals[1], totals[2], totals[3], totals[4], totals[5], totals[6], totals[7])
```

```python
import jax
import jax.numpy as jnp
from jax import lax
from jax.sharding import PartitionSpec as P

QUERY_HEADS = 16
KEY_VALUE_HEADS = 8
HEAD_SIZE = 128
EPSILON = 1e-06
ROPE_BASE = 1000000.0
BF = jnp.bfloat16
F32 = jnp.float32


def rms_scale(value, gain):
    return value * lax.rsqrt(jnp.mean(value * value, -1, keepdims=True) + EPSILON) * gain


def rotate(value, cosine, sine):
    half = value.shape[-1] // 2
    first = value[..., :half]
    second = value[..., half:]
    return jnp.concatenate([first * cosine - second * sine, second * cosine + first * sine], -1)


def mm(left, right):
    return jnp.dot(left, right, preferred_element_type=F32)


def mm_tn(left, right):
    return lax.dot_general(left, right, (((0,), (0,)), ((), ())), preferred_element_type=F32)


def mm_nt(left, right):
    return lax.dot_general(left, right, (((1,), (1,)), ((), ())), preferred_element_type=F32)


def gated_unit(gate, up):
    return jax.nn.silu(gate) * up


def swap_ctx(pieces):
    return lax.all_to_all(pieces, "ctx", 0, 0)


def general(layer_input, prefix, wq, wk, wv, wo, w_gate, w_up, w_down, gains, cotangent):
    nd, nc = lax.axis_size("dp"), lax.axis_size("ctx")
    me = lax.axis_index("ctx")
    rows = layer_input.shape[1]
    seq = rows * nc
    depth, width = wq.shape[0], layer_input.shape[2]
    heads = QUERY_HEADS // nc
    copies = max(1, nc // KEY_VALUE_HEADS)
    kv_heads = max(1, KEY_VALUE_HEADS // nc)
    unit = w_down.shape[0]
    scale = HEAD_SIZE ** (-0.5)

    def columns_to(weight, parts):
        return jnp.moveaxis(weight.reshape(depth, parts, -1), 1, 0)

    def by_head(weight, repeat):
        parts = columns_to(weight, nc // repeat)
        return jnp.repeat(parts, repeat, 0) if repeat > 1 else parts

    def by_unit(weight):
        return jnp.transpose(weight.reshape(depth, nd, nc, unit), (2, 0, 1, 3)).reshape(
            nc, depth, nd * unit
        )

    def everywhere(array):
        return lax.all_gather(array, "dp", axis=0, tiled=True)

    qkv_piece = jnp.concatenate([by_head(wq, 1), by_head(wk, copies), by_head(wv, copies)], 2)
    w_qkv = everywhere(swap_ctx(qkv_piece).reshape(nc * depth, -1))
    plane = nc * wo.shape[0]
    span = QUERY_HEADS * HEAD_SIZE // nc
    need = span // wo.shape[0]
    by_plane = everywhere(wo).reshape(nd, wo.shape[0], width)
    wanted = jnp.stack([by_plane[i * span // plane] for i in range(nc)])
    arrived = swap_ctx(wanted)
    first_source = (me * span % plane) // wo.shape[0]
    w_o = lax.dynamic_slice_in_dim(arrived, first_source, need, 0).reshape(span, width)
    w_gu = everywhere(
        swap_ctx(jnp.concatenate([by_unit(w_gate), by_unit(w_up)], 2)).reshape(nc * depth, -1)
    )
    w_d = everywhere(w_down)
    gain_all = lax.all_gather(gains, ("dp", "ctx"), axis=0, tiled=True).astype(F32)
    gain_one = gain_all[:width]
    gain_two = gain_all[width : 2 * width]
    gain_q = gain_all[2 * width : 2 * width + HEAD_SIZE]
    gain_k = gain_all[2 * width + HEAD_SIZE :]

    def whole(array):
        return lax.all_gather(array, "ctx", axis=0, tiled=True)

    def own_sum(partial):
        return lax.psum_scatter(partial.astype(BF), "ctx", scatter_dimension=0, tiled=True).astype(
            F32
        )

    pos = jnp.arange(seq, dtype=jnp.int32)
    visible = (pos[None, :] <= pos[:, None]) | (pos[None, :] < prefix[0])
    freqs = ROPE_BASE ** (-(jnp.arange(HEAD_SIZE // 2, dtype=F32) * 2.0 / HEAD_SIZE))
    angles = pos.astype(F32)[:, None] * freqs[None, :]
    cosine = jnp.cos(angles)[:, None, :]
    sine = jnp.sin(angles)[:, None, :]

    def prepare_heads(raw, gain):
        return rotate(rms_scale(raw, gain), cosine, sine)

    inputs = layer_input[0].astype(F32)
    n1, back_one = jax.vjp(rms_scale, inputs, gain_one)
    n1_all = whole(n1.astype(BF))
    dy_all = whole(cotangent[0])
    qkv = mm(n1_all, w_qkv)
    q_raw = qkv[:, : heads * HEAD_SIZE].reshape(seq, heads, HEAD_SIZE)
    k_raw = qkv[:, heads * HEAD_SIZE : (heads + kv_heads) * HEAD_SIZE].reshape(
        seq, kv_heads, HEAD_SIZE
    )
    v = qkv[:, (heads + kv_heads) * HEAD_SIZE :].astype(BF).reshape(seq, kv_heads, HEAD_SIZE)
    q_rot, back_q = jax.vjp(prepare_heads, q_raw, gain_q)
    k_rot, back_k = jax.vjp(prepare_heads, k_raw, gain_k)
    q_rot = q_rot.astype(BF).reshape(seq, kv_heads, -1, HEAD_SIZE)
    k_rot = k_rot.astype(BF)
    scores = jnp.einsum("tkgd,skd->kgts", q_rot, k_rot, preferred_element_type=F32) * scale
    scores = jnp.where(visible[None, None], scores, -1e30)
    top = jnp.max(scores, -1, keepdims=True)
    expo = jnp.exp(scores - top)
    total = jnp.sum(expo, -1, keepdims=True)
    probs = expo / total
    probs_bf = probs.astype(BF)
    o = jnp.einsum("kgts,skd->tkgd", probs_bf, v, preferred_element_type=F32).astype(BF)
    o = o.reshape(seq, heads * HEAD_SIZE)
    hidden = inputs + own_sum(mm(o, w_o))
    n2, back_two = jax.vjp(rms_scale, hidden, gain_two)
    n2_all = whole(n2.astype(BF))
    gu = mm(n2_all, w_gu)
    gate, up = gu[:, : nd * unit], gu[:, nd * unit :]
    active, back_gated = jax.vjp(gated_unit, gate, up)
    active = active.astype(BF)
    output = (hidden + own_sum(mm(active, w_d))).astype(BF)
    def row_sum(term):
        return lax.psum_scatter(term.astype(BF), "dp", scatter_dimension=0, tiled=True)

    down_grad = row_sum(mm_tn(active, dy_all)).astype(F32)
    d_gate, d_up = back_gated(mm_nt(dy_all, w_d))
    d_gu = jnp.concatenate([d_gate.astype(BF), d_up.astype(BF)], 1)
    gu_sum = swap_ctx(row_sum(mm_tn(n2_all, d_gu)).reshape(nc, depth, -1)).astype(F32)
    gu_sum = gu_sum.reshape(nc, depth, 2, nd, unit)
    gu_sum = jnp.transpose(gu_sum, (2, 1, 3, 0, 4)).reshape(2, depth, -1)
    gate_grad, up_grad = gu_sum[0], gu_sum[1]
    upstream = cotangent[0].astype(F32)
    d_hidden_part, d_gain_two = back_two(own_sum(mm_nt(d_gu, w_gu)))
    d_hidden = upstream + d_hidden_part
    d_attn = whole(d_hidden.astype(BF))
    wo_term = mm_tn(o, d_attn).astype(BF).reshape(need, wo.shape[0], width)
    slots = jnp.zeros((nc, wo.shape[0], width), BF)
    slots = lax.dynamic_update_slice_in_dim(slots, wo_term, first_source, 0)
    back_home = swap_ctx(slots)
    mine = []
    for plane_index in range(nd):
        total_plane = 0
        for i in range(nc):
            if i * span // plane == plane_index:
                total_plane = total_plane + back_home[i].astype(F32)
        mine.append(total_plane)
    wo_grad = lax.psum_scatter(
        jnp.stack(mine).astype(BF), "dp", scatter_dimension=0, tiled=True
    )[0].astype(F32)
    d_o = mm_nt(d_attn, w_o).astype(BF).reshape(seq, kv_heads, -1, HEAD_SIZE)
    d_probs = jnp.einsum("tkgd,skd->kgts", d_o, v, preferred_element_type=F32)
    d_v = jnp.einsum("kgts,tkgd->skd", probs_bf, d_o, preferred_element_type=F32).astype(BF)
    d_scores = (probs * (d_probs - jnp.sum(d_probs * probs, -1, keepdims=True))).astype(BF)
    d_q = jnp.einsum("kgts,skd->tkgd", d_scores, k_rot, preferred_element_type=F32) * scale
    d_k = jnp.einsum("kgts,tkgd->skd", d_scores, q_rot, preferred_element_type=F32) * scale
    d_q, d_gain_q = back_q(d_q.reshape(seq, heads, HEAD_SIZE))
    d_k, d_gain_k = back_k(d_k)
    d_qkv = jnp.concatenate(
        [a.reshape(seq, -1).astype(BF) for a in (d_q, d_k, d_v)], 1
    )
    qkv_sum = swap_ctx(row_sum(mm_tn(n1_all, d_qkv)).reshape(nc, depth, -1)).astype(F32)
    at_k, at_v = heads * HEAD_SIZE, (heads + kv_heads) * HEAD_SIZE

    def columns_back(part, repeat):
        part = part.reshape(nc // repeat, repeat, depth, -1).sum(1)
        return jnp.moveaxis(part, 0, 1).reshape(depth, -1)

    wq_grad = columns_back(qkv_sum[:, :, :at_k], 1)
    wk_grad = columns_back(qkv_sum[:, :, at_k:at_v], copies)
    wv_grad = columns_back(qkv_sum[:, :, at_v:], copies)
    d_input_part, d_gain_one = back_one(own_sum(mm_nt(d_qkv, w_qkv)))
    x_grad = (d_hidden + d_input_part).astype(BF)
    gain_term = jnp.concatenate([d_gain_one, d_gain_two, d_gain_q, d_gain_k])
    gains_grad = lax.psum_scatter(gain_term, ("dp", "ctx"), scatter_dimension=0, tiled=True)
    return (
        output[None], x_grad[None], wq_grad, wk_grad, wv_grad, wo_grad,
        gate_grad, up_grad, down_grad, gains_grad,
    )


def solution(mesh):
    tokens = P("dp", "ctx", None)
    matrix = P(("dp", "ctx"), None)
    vector = P(("dp", "ctx"))
    return jax.shard_map(
        general,
        mesh=mesh,
        in_specs=(tokens, P("dp")) + (matrix,) * 7 + (vector, tokens),
        out_specs=(tokens, tokens) + (matrix,) * 7 + (vector,),
        check_vma=False,
    )
```

```python
import jax
import jax.numpy as jnp
import numpy as np
from jax import lax
from jax.experimental import pallas as pl
from jax.experimental.pallas import tpu as pltpu
from jax.sharding import PartitionSpec as P

QUERY_HEADS = 16
KEY_VALUE_HEADS = 8
HEAD_SIZE = 128
EPSILON = 1e-06
ROPE_BASE = 1000000.0
BF = jnp.bfloat16
F32 = jnp.float32


def rms_scale(value, gain):
    return value * lax.rsqrt(jnp.mean(value * value, -1, keepdims=True) + EPSILON) * gain


def rotate(value, cosine, sine):
    half = value.shape[-1] // 2
    first = value[..., :half]
    second = value[..., half:]
    return jnp.concatenate([first * cosine - second * sine, second * cosine + first * sine], -1)


def mm(left, right):
    return jnp.dot(left, right, preferred_element_type=F32)


def mm_tn(left, right):
    return lax.dot_general(left, right, (((0,), (0,)), ((), ())), preferred_element_type=F32)


def mm_nt(left, right):
    return lax.dot_general(left, right, (((1,), (1,)), ((), ())), preferred_element_type=F32)


def gated_unit(gate, up):
    return jax.nn.silu(gate) * up


def swap_ctx(pieces):
    return lax.all_to_all(pieces, "ctx", 0, 0)


def general(layer_input, prefix, wq, wk, wv, wo, w_gate, w_up, w_down, gains, cotangent):
    nd, nc = lax.axis_size("dp"), lax.axis_size("ctx")
    me = lax.axis_index("ctx")
    rows = layer_input.shape[1]
    seq = rows * nc
    depth, width = wq.shape[0], layer_input.shape[2]
    heads = QUERY_HEADS // nc
    copies = max(1, nc // KEY_VALUE_HEADS)
    kv_heads = max(1, KEY_VALUE_HEADS // nc)
    unit = w_down.shape[0]
    scale = HEAD_SIZE ** (-0.5)

    def columns_to(weight, parts):
        return jnp.moveaxis(weight.reshape(depth, parts, -1), 1, 0)

    def by_head(weight, repeat):
        parts = columns_to(weight, nc // repeat)
        return jnp.repeat(parts, repeat, 0) if repeat > 1 else parts

    def by_unit(weight):
        return jnp.transpose(weight.reshape(depth, nd, nc, unit), (2, 0, 1, 3)).reshape(
            nc, depth, nd * unit
        )

    def everywhere(array):
        return lax.all_gather(array, "dp", axis=0, tiled=True)

    qkv_piece = jnp.concatenate([by_head(wq, 1), by_head(wk, copies), by_head(wv, copies)], 2)
    w_qkv = everywhere(swap_ctx(qkv_piece).reshape(nc * depth, -1))
    plane = nc * wo.shape[0]
    span = QUERY_HEADS * HEAD_SIZE // nc
    need = span // wo.shape[0]
    by_plane = everywhere(wo).reshape(nd, wo.shape[0], width)
    wanted = jnp.stack([by_plane[i * span // plane] for i in range(nc)])
    arrived = swap_ctx(wanted)
    first_source = (me * span % plane) // wo.shape[0]
    w_o = lax.dynamic_slice_in_dim(arrived, first_source, need, 0).reshape(span, width)
    w_gu = everywhere(
        swap_ctx(jnp.concatenate([by_unit(w_gate), by_unit(w_up)], 2)).reshape(nc * depth, -1)
    )
    w_d = everywhere(w_down)
    gain_all = lax.all_gather(gains, ("dp", "ctx"), axis=0, tiled=True).astype(F32)
    gain_one = gain_all[:width]
    gain_two = gain_all[width : 2 * width]
    gain_q = gain_all[2 * width : 2 * width + HEAD_SIZE]
    gain_k = gain_all[2 * width + HEAD_SIZE :]

    def whole(array):
        return lax.all_gather(array, "ctx", axis=0, tiled=True)

    def own_sum(partial):
        return lax.psum_scatter(partial.astype(BF), "ctx", scatter_dimension=0, tiled=True).astype(
            F32
        )

    pos = jnp.arange(seq, dtype=jnp.int32)
    visible = (pos[None, :] <= pos[:, None]) | (pos[None, :] < prefix[0])
    freqs = ROPE_BASE ** (-(jnp.arange(HEAD_SIZE // 2, dtype=F32) * 2.0 / HEAD_SIZE))
    angles = pos.astype(F32)[:, None] * freqs[None, :]
    cosine = jnp.cos(angles)[:, None, :]
    sine = jnp.sin(angles)[:, None, :]

    def prepare_heads(raw, gain):
        return rotate(rms_scale(raw, gain), cosine, sine)

    inputs = layer_input[0].astype(F32)
    n1, back_one = jax.vjp(rms_scale, inputs, gain_one)
    n1_all = whole(n1.astype(BF))
    dy_all = whole(cotangent[0])
    qkv = mm(n1_all, w_qkv)
    q_raw = qkv[:, : heads * HEAD_SIZE].reshape(seq, heads, HEAD_SIZE)
    k_raw = qkv[:, heads * HEAD_SIZE : (heads + kv_heads) * HEAD_SIZE].reshape(
        seq, kv_heads, HEAD_SIZE
    )
    v = qkv[:, (heads + kv_heads) * HEAD_SIZE :].astype(BF).reshape(seq, kv_heads, HEAD_SIZE)
    q_rot, back_q = jax.vjp(prepare_heads, q_raw, gain_q)
    k_rot, back_k = jax.vjp(prepare_heads, k_raw, gain_k)
    q_rot = q_rot.astype(BF).reshape(seq, kv_heads, -1, HEAD_SIZE)
    k_rot = k_rot.astype(BF)
    scores = jnp.einsum("tkgd,skd->kgts", q_rot, k_rot, preferred_element_type=F32) * scale
    scores = jnp.where(visible[None, None], scores, -1e30)
    top = jnp.max(scores, -1, keepdims=True)
    expo = jnp.exp(scores - top)
    total = jnp.sum(expo, -1, keepdims=True)
    probs = expo / total
    probs_bf = probs.astype(BF)
    o = jnp.einsum("kgts,skd->tkgd", probs_bf, v, preferred_element_type=F32).astype(BF)
    o = o.reshape(seq, heads * HEAD_SIZE)
    hidden = inputs + own_sum(mm(o, w_o))
    n2, back_two = jax.vjp(rms_scale, hidden, gain_two)
    n2_all = whole(n2.astype(BF))
    gu = mm(n2_all, w_gu)
    gate, up = gu[:, : nd * unit], gu[:, nd * unit :]
    active, back_gated = jax.vjp(gated_unit, gate, up)
    active = active.astype(BF)
    output = (hidden + own_sum(mm(active, w_d))).astype(BF)
    def row_sum(term):
        return lax.psum_scatter(term.astype(BF), "dp", scatter_dimension=0, tiled=True)

    down_grad = row_sum(mm_tn(active, dy_all)).astype(F32)
    d_gate, d_up = back_gated(mm_nt(dy_all, w_d))
    d_gu = jnp.concatenate([d_gate.astype(BF), d_up.astype(BF)], 1)
    gu_sum = swap_ctx(row_sum(mm_tn(n2_all, d_gu)).reshape(nc, depth, -1)).astype(F32)
    gu_sum = gu_sum.reshape(nc, depth, 2, nd, unit)
    gu_sum = jnp.transpose(gu_sum, (2, 1, 3, 0, 4)).reshape(2, depth, -1)
    gate_grad, up_grad = gu_sum[0], gu_sum[1]
    upstream = cotangent[0].astype(F32)
    d_hidden_part, d_gain_two = back_two(own_sum(mm_nt(d_gu, w_gu)))
    d_hidden = upstream + d_hidden_part
    d_attn = whole(d_hidden.astype(BF))
    wo_term = mm_tn(o, d_attn).astype(BF).reshape(need, wo.shape[0], width)
    slots = jnp.zeros((nc, wo.shape[0], width), BF)
    slots = lax.dynamic_update_slice_in_dim(slots, wo_term, first_source, 0)
    back_home = swap_ctx(slots)
    mine = []
    for plane_index in range(nd):
        total_plane = 0
        for i in range(nc):
            if i * span // plane == plane_index:
                total_plane = total_plane + back_home[i].astype(F32)
        mine.append(total_plane)
    wo_grad = lax.psum_scatter(
        jnp.stack(mine).astype(BF), "dp", scatter_dimension=0, tiled=True
    )[0].astype(F32)
    d_o = mm_nt(d_attn, w_o).astype(BF).reshape(seq, kv_heads, -1, HEAD_SIZE)
    d_probs = jnp.einsum("tkgd,skd->kgts", d_o, v, preferred_element_type=F32)
    d_v = jnp.einsum("kgts,tkgd->skd", probs_bf, d_o, preferred_element_type=F32).astype(BF)
    d_scores = (probs * (d_probs - jnp.sum(d_probs * probs, -1, keepdims=True))).astype(BF)
    d_q = jnp.einsum("kgts,skd->tkgd", d_scores, k_rot, preferred_element_type=F32) * scale
    d_k = jnp.einsum("kgts,tkgd->skd", d_scores, q_rot, preferred_element_type=F32) * scale
    d_q, d_gain_q = back_q(d_q.reshape(seq, heads, HEAD_SIZE))
    d_k, d_gain_k = back_k(d_k)
    d_qkv = jnp.concatenate(
        [a.reshape(seq, -1).astype(BF) for a in (d_q, d_k, d_v)], 1
    )
    qkv_sum = swap_ctx(row_sum(mm_tn(n1_all, d_qkv)).reshape(nc, depth, -1)).astype(F32)
    at_k, at_v = heads * HEAD_SIZE, (heads + kv_heads) * HEAD_SIZE

    def columns_back(part, repeat):
        part = part.reshape(nc // repeat, repeat, depth, -1).sum(1)
        return jnp.moveaxis(part, 0, 1).reshape(depth, -1)

    wq_grad = columns_back(qkv_sum[:, :, :at_k], 1)
    wk_grad = columns_back(qkv_sum[:, :, at_k:at_v], copies)
    wv_grad = columns_back(qkv_sum[:, :, at_v:], copies)
    d_input_part, d_gain_one = back_one(own_sum(mm_nt(d_qkv, w_qkv)))
    x_grad = (d_hidden + d_input_part).astype(BF)
    gain_term = jnp.concatenate([d_gain_one, d_gain_two, d_gain_q, d_gain_k])
    gains_grad = lax.psum_scatter(gain_term, ("dp", "ctx"), scatter_dimension=0, tiled=True)
    return (
        output[None], x_grad[None], wq_grad, wk_grad, wv_grad, wo_grad,
        gate_grad, up_grad, down_grad, gains_grad,
    )


MESH = pl.DeviceIdType.MESH
BLOCK = 128
VMEM_BYTES = 64 << 20


class Copies:
    def __init__(self, sends, receives):
        self.sends, self.receives = sends, receives
        self.used = 0

    def take(self, count=1):
        first = self.used
        self.used += count
        if self.used > SLOTS:
            raise ValueError("more semaphores")
        return first

    def to(self, src, dst, device, slot, receive_slot=None):
        receive_slot = slot if receive_slot is None else receive_slot
        return pltpu.make_async_remote_copy(
            src_ref=src,
            dst_ref=dst,
            send_sem=self.sends.at[slot],
            recv_sem=self.receives.at[receive_slot],
            device_id=device,
            device_id_type=MESH,
        )

    def here(self, src, dst, slot):
        return pltpu.make_async_copy(src, dst, self.sends.at[slot])


class Place:
    def __init__(self):
        self.d = lax.axis_index("dp")
        self.c = lax.axis_index("ctx")
        self.z = self.c // 2
        self.p = lax.rem(self.c, 2)

    def at(self, d, c):
        return (d, c)


def meet():
    barrier = pltpu.get_barrier_semaphore()
    d, c = lax.axis_index("dp"), lax.axis_index("ctx")
    partners = [(d, c ^ rel) for rel in range(1, 8)]
    partners += [(d ^ rel, c ^ twin) for rel in range(1, 4) for twin in range(2)]
    for partner in partners:
        pl.semaphore_signal(barrier, inc=1, device_id=partner, device_id_type=MESH)
    pl.semaphore_wait(barrier, len(partners))


def when(condition, then):
    if isinstance(condition, bool):
        if condition:
            then()
    else:
        pl.when(condition)(then)


def rows_at(start, size):
    return pl.ds(pl.multiple_of(start, 16), size)


class Gather:
    def __init__(self, copies, place, buf, parts=2):
        self.k, self.g, self.buf, self.parts = copies, place, buf, parts
        self.size = BLOCK // parts
        self.right = copies.take(3 * parts)
        self.left = copies.take(3 * parts)
        self.twin = copies.take(7 * parts)

    def piece(self, z, p, part):
        return self.buf.at[rows_at((2 * z + p) * BLOCK + part * self.size, self.size)]

    def line(self, step, part, rightwards):
        g = self.g
        z = g.z - step if rightwards else g.z + step
        slot = (self.right if rightwards else self.left) + step * self.parts + part
        piece = self.piece(z, g.p, part)
        to = g.c + 2 if rightwards else g.c - 2
        return self.k.to(piece, piece, (g.d, to), slot)

    def wait_line(self, step, part, rightwards):
        piece = self.piece(self.g.z, self.g.p, part)
        slot = (self.right if rightwards else self.left) + step * self.parts + part
        self.k.to(piece, piece, (self.g.d, self.g.c ^ 1), slot).wait_recv()

    def twins(self, order, z, part):
        piece = self.piece(z, self.g.p, part)
        return self.k.to(piece, piece, (self.g.d, self.g.c ^ 1), self.twin + order * self.parts + part)

    def can_send(self, step, rightwards):
        z = self.g.z
        return (z >= step) & (z < 3) if rightwards else (z + step <= 3) & (z > 0)

    def gets(self, step, rightwards):
        z = self.g.z
        return z >= step + 1 if rightwards else z + step + 1 <= 3

    def start(self):
        for part in range(self.parts):
            self.start_part(part)

    def start_part(self, part):
        for rightwards in (True, False):

            @pl.when(self.can_send(0, rightwards))
            def _():
                self.line(0, part, rightwards).start()

        self.twins(0, self.g.z, part).start()

    def start_line(self, right, left):
        for part in range(self.parts):
            for now, rightwards in ((right, True), (left, False)):

                @pl.when(now & self.can_send(0, rightwards))
                def _():
                    self.line(0, part, rightwards).start()

    def start_twin(self):
        for part in range(self.parts):
            self.twins(0, self.g.z, part).start()

    def step(self, step):
        for part in range(self.parts):
            self.step_part(step, part)

    def step_part(self, step, part):
        for side, rightwards in enumerate((True, False)):
            z = self.g.z - 1 - step if rightwards else self.g.z + 1 + step

            @pl.when(self.gets(step, rightwards))
            def _():
                self.wait_line(step, part, rightwards)

                def on():
                    @pl.when(self.can_send(step + 1, rightwards))
                    def _():
                        self.line(step + 1, part, rightwards).start()

                when(step < 2, on)
                self.twins(1 + 2 * step + side, z, part).start()

    def twin_own(self):
        for part in range(self.parts):
            self.twins(0, self.g.z, part).wait_recv()

    def twin_step(self, step):
        for part in range(self.parts):
            for side, rightwards in enumerate((True, False)):

                @pl.when(self.gets(step, rightwards))
                def _():
                    self.twins(1 + 2 * step + side, self.g.z, part).wait_recv()

    def drain(self):
        for part in range(self.parts):
            self.twins(0, self.g.z, part).wait_send()
            for step in range(3):
                for side, rightwards in enumerate((True, False)):

                    @pl.when(self.can_send(step, rightwards))
                    def _():
                        self.line(step, part, rightwards).wait_send()

                    @pl.when(self.gets(step, rightwards))
                    def _():
                        self.twins(1 + 2 * step + side, self.g.z, part).wait_send()


def add_rows(dst, dst_row, a, a_row, b, b_row, count):
    def body(i, carry):
        at = i * 32
        total = a[rows_at(a_row + at, 32), :].astype(F32) + b[rows_at(b_row + at, 32), :].astype(F32)
        dst[rows_at(dst_row + at, 32), :] = total.astype(dst.dtype)
        return carry

    lax.fori_loop(0, count // 32, body, 0)


class Scatter:
    def __init__(self, copies, place, partial, from_twin, from_left, from_right, parts=2):
        self.k, self.g = copies, place
        self.partial, self.from_twin = partial, from_twin
        self.from_line = {True: from_left, False: from_right}
        self.parts, self.size = parts, BLOCK // parts
        self.twin = copies.take(4)
        self.slots = {True: copies.take(3 * parts), False: copies.take(3 * parts)}

    def row(self, z, p):
        return (2 * z + p) * BLOCK

    def twins(self, z, slot):
        g = self.g
        src = self.partial.at[rows_at(self.row(z, 1 - g.p), BLOCK)]
        dst = self.from_twin.at[rows_at(z * BLOCK, BLOCK)]
        return self.k.to(src, dst, (g.d, g.c ^ 1), self.twin + slot)

    def send_twin(self, z):
        self.twins(z, z).start()

    def take_twin(self, z):
        self.twins(z, z).wait_recv()
        at = self.row(z, self.g.p)
        add_rows(self.partial, at, self.partial, at, self.from_twin, z * BLOCK, BLOCK)

    def target(self, step, rightwards):
        return self.g.z + 3 - step if rightwards else self.g.z - 3 + step

    def can_send(self, step, rightwards):
        z = self.g.z
        return z <= step if rightwards else 3 - z <= step

    def gets(self, step, rightwards):
        z = self.g.z
        return (z >= 1) & (z - 1 <= step) if rightwards else (z <= 2) & (2 - z <= step)

    def line(self, step, rightwards, part):
        g = self.g
        at = self.row(self.target(step, rightwards), g.p) + part * self.size
        src = self.partial.at[rows_at(at, self.size)]
        dst = self.from_line[rightwards].at[rows_at(step * BLOCK + part * self.size, self.size)]
        slot = self.slots[rightwards] + step * self.parts + part
        return self.k.to(src, dst, (g.d, g.c + 2 if rightwards else g.c - 2), slot)

    def wait_line(self, step, rightwards, part):
        src = self.partial.at[pl.ds(0, self.size)]
        dst = self.from_line[rightwards].at[rows_at(step * BLOCK + part * self.size, self.size)]
        slot = self.slots[rightwards] + step * self.parts + part
        self.k.to(src, dst, (self.g.d, self.g.c ^ 1), slot).wait_recv()

    def send(self, step, part):
        for rightwards in (True, False):

            @pl.when(self.can_send(step, rightwards))
            def _():
                self.line(step, rightwards, part).start()

    def start(self):
        for part in range(self.parts):
            self.send(0, part)

    def advance(self, step):
        for part in range(self.parts):
            for rightwards in (True, False):

                @pl.when(self.gets(step, rightwards))
                def _():
                    self.wait_line(step, rightwards, part)

                    def add():
                        z = self.g.z + 2 - step if rightwards else self.g.z - 2 + step
                        at = self.row(z, self.g.p) + part * self.size
                        add_rows(
                            self.partial, at, self.partial, at, self.from_line[rightwards],
                            step * BLOCK + part * self.size, self.size,
                        )

                    when(step < 2, add)

            when(step < 2, lambda: self.send(step + 1, part))

    def finish(self, done, slot=2, part=None):
        g = self.g
        own = self.row(g.z, g.p)
        first, count = (0, BLOCK) if part is None else (part * self.size, self.size)

        def body(i, carry):
            at = first + i * 16
            total = self.partial[rows_at(own + at, 16), :].astype(F32)
            a = self.from_line[True][rows_at(slot * BLOCK + at, 16), :].astype(F32)
            b = self.from_line[False][rows_at(slot * BLOCK + at, 16), :].astype(F32)
            total = total + jnp.where(g.z >= 1, a, 0.0) + jnp.where(g.z <= 2, b, 0.0)
            done(at, total)
            return carry

        lax.fori_loop(0, count // 16, body, 0)

    def send_ends(self, part, *steps):
        for rightwards in (True, False):

            @pl.when(self.g.z == (0 if rightwards else 3))
            def _():
                for step in steps:
                    self.line(step, rightwards, part).start()

    def relay(self, step, part):
        for rightwards in (True, False):

            @pl.when(self.gets(step, rightwards))
            def _():
                self.wait_line(step, rightwards, part)
                z = self.g.z + 2 - step if rightwards else self.g.z - 2 + step
                at = self.row(z, self.g.p) + part * self.size
                add_rows(
                    self.partial, at, self.partial, at, self.from_line[rightwards],
                    step * BLOCK + part * self.size, self.size,
                )
                self.line(step + 1, rightwards, part).start()

    def last(self, done, part):
        for rightwards in (True, False):

            @pl.when(self.gets(2, rightwards))
            def _():
                self.wait_line(2, rightwards, part)

        self.finish(done, part=part)

    def drain(self):
        for z in range(4):
            self.twins(z, z).wait_send()
        for step in range(3):
            for part in range(self.parts):
                for rightwards in (True, False):

                    @pl.when(self.can_send(step, rightwards))
                    def _():
                        self.line(step, rightwards, part).wait_send()


class Outwards(Scatter):
    def __init__(self, *args):
        super().__init__(*args, parts=1)

    def can_send(self, step, rightwards):
        return self.g.z + 1 + step <= 3 if rightwards else self.g.z - 1 - step >= 0

    def target(self, step, rightwards):
        return self.g.z + 1 + step if rightwards else self.g.z - 1 - step

    def send_ends(self, step):
        for rightwards in (True, False):

            @pl.when(self.g.z == (0 if rightwards else 3))
            def _():
                self.line(step, rightwards, 0).start()

    def relay(self, step, chip):
        for rightwards in (True, False):

            @pl.when(self.g.z == (chip if rightwards else 3 - chip))
            def _():
                self.wait_line(step, rightwards, 0)
                at = self.row(self.target(step - 1, rightwards), self.g.p)
                add_rows(
                    self.partial, at, self.partial, at, self.from_line[rightwards], step * BLOCK, BLOCK
                )
                self.line(step - 1, rightwards, 0).start()

    def take_own(self):
        for rightwards in (True, False):

            @pl.when(self.g.z >= 1 if rightwards else self.g.z <= 2)
            def _():
                self.wait_line(0, rightwards, 0)


class Spread:
    def __init__(self, copies, place, piece):
        self.k, self.g, self.piece = copies, place, piece
        self.slots = copies.take(6)

    def direct(self, half, rel):
        g = self.g
        piece = self.piece(g.d, half)
        return self.k.to(piece, piece, (g.d ^ rel, g.c), self.slots + 2 * (rel - 1) + half)

    def passed(self, rel):
        g = self.g
        piece = self.piece(g.d ^ (3 - rel), rel - 1)
        return self.k.to(piece, piece, (g.d ^ rel, g.c), self.slots + 4 + rel - 1)

    def start(self):
        for half, rel in ((0, 1), (1, 2), (1, 1), (0, 2)):
            self.direct(half, rel).start()

    def forward(self):
        self.direct(1, 1).wait_recv()
        self.passed(2).start()
        self.direct(0, 2).wait_recv()
        self.passed(1).start()

    def finish(self):
        self.direct(0, 1).wait_recv()
        self.direct(1, 2).wait_recv()
        self.passed(1).wait_recv()
        self.passed(2).wait_recv()

    def drain(self):
        for half, rel in ((0, 1), (1, 2), (1, 1), (0, 2)):
            self.direct(half, rel).wait_send()
        self.passed(1).wait_send()
        self.passed(2).wait_send()


class Direct:
    def __init__(self, copies, place, piece):
        self.k, self.g, self.piece = copies, place, piece
        self.slots = copies.take(3)

    def copy(self, rel):
        piece = self.piece(self.g.d)
        return self.k.to(piece, piece, (self.g.d ^ rel, self.g.c), self.slots + rel - 1)

    def start(self):
        for rel in (1, 2, 3):
            self.copy(rel).start()

    def finish(self):
        for rel in (1, 2, 3):
            self.copy(rel).wait_recv()

    def drain(self):
        for rel in (1, 2, 3):
            self.copy(rel).wait_send()


class Fold:
    def __init__(self, copies, place, piece, got, stage):
        self.k, self.g, self.piece, self.got, self.stage = copies, place, piece, got, stage
        self.slots = copies.take(6)
        self.loads = copies.take(6)

    def first(self, half, passed):
        g = self.g
        rel = 1 + half
        src = self.piece(g.d ^ (3 if passed else rel), half)
        i = 2 * half + passed
        return self.k.to(src, self.got(i), (g.d ^ rel, g.c), self.slots + i)

    def second(self, half):
        g = self.g
        rel = 2 - half
        return self.k.to(
            self.piece(g.d ^ rel, half), self.got(4 + half), (g.d ^ rel, g.c), self.slots + 4 + half
        )

    def load(self, i):
        return self.k.here(self.got(i), self.stage(i), self.loads + i)

    def start(self):
        for passed in (1, 0):
            for half in range(2):
                self.first(half, passed).start()

    def middle(self, add):
        for half in range(2):
            self.first(half, 1).wait_recv()
            self.load(2 * half + 1).start()
        for half in range(2):
            self.load(2 * half + 1).wait()
            add(self.piece(self.g.d ^ (2 - half), half), (self.stage(2 * half + 1),))
            self.second(half).start()

    def final(self, add):
        for half in range(2):
            self.first(half, 0).wait_recv()
            self.load(2 * half).start()
        for half in range(2):
            self.second(half).wait_recv()
            self.load(4 + half).start()
        for half in range(2):
            self.load(2 * half).wait()
            self.load(4 + half).wait()
            add(self.piece(self.g.d, half), (self.stage(2 * half), self.stage(4 + half)))

    def drain(self):
        for half in range(2):
            for passed in range(2):
                self.first(half, passed).wait_send()
            self.second(half).wait_send()


def down_to_units(place, copies, src, dst):
    g, p, d = place, place.p, place.d
    send, receive = copies.take(8), copies.take(12)
    odd = lax.rem(d, 2)
    wide = (src.at[rows_at(p * 64, 128)], dst.at[rows_at(wide_row(p, d), 128)])
    thin = (src.at[rows_at((1 - p) * 128, 64)], dst.at[rows_at(thin_row(d, p), 64)])
    stays = odd == p

    def thin_to(rel, core):
        return copies.to(
            *thin, (d ^ rel, 2 * g.z + odd), send + 4 + rel, receive + 4 + 2 * rel + core
        )

    def start_thin():
        for rel in (1, 2, 3):
            thin_to(rel, p).start()

        @pl.when(stays)
        def _():
            copies.here(*thin, send + 4).start()

        @pl.when(jnp.logical_not(stays))
        def _():
            thin_to(0, p).start()

    copies.here(*wide, send).start()
    spread = Spread(
        copies, g, lambda e, half: dst.at[rows_at(wide_row(p, e) + half * 64, 64)]
    )

    def start_wide():
        copies.here(*wide, send).wait()
        spread.start()

    def finish():
        spread.finish()

        @pl.when(stays)
        def _():
            copies.here(*thin, send + 4).wait()

        @pl.when(jnp.logical_not(stays))
        def _():
            thin_to(0, p).wait_send()

        for rel in (1, 2, 3):
            thin_to(rel, p).wait_send()
        for rel in range(4):

            @pl.when(lax.rem(d ^ rel, 2) == p)
            def _():
                if rel:
                    thin_to(rel, p).wait_recv()
                thin_to(rel, 1 - p).wait_recv()

    return start_thin, start_wide, spread, finish


def unit_row(core, plane):
    return (plane // 2) * 384 + (lax.rem(plane, 2) ^ core) * 256


def wide_row(core, plane):
    return unit_row(core, plane) + core * lax.rem(plane, 2) * 128


def thin_row(plane, core):
    odd = lax.rem(plane, 2)
    return unit_row(odd, plane) + (1 - odd) * 128 + core * 64


def down_to_owners(place, copies, src, dst):
    g, p, d = place, place.p, place.d
    send, receive = copies.take(12), copies.take(8)

    def wide(rel):
        plane = d ^ rel
        a = src.at[rows_at(wide_row(p, plane), 128)]
        b = dst.at[rel, rows_at(p * 64, 128)]
        if rel == 0:
            return copies.here(a, b, send)
        return copies.to(a, b, (plane, g.c), send + rel, receive + rel)

    def thin(rel, core):
        plane = d ^ rel
        a = src.at[rows_at(thin_row(plane, core), 64)]
        b = dst.at[rel, rows_at((1 - core) * 128, 64)]
        return copies.to(
            a, b, (plane, 2 * g.z + core), send + 4 + 2 * rel + core, receive + 4 + rel
        )

    def thin_own():
        a = src.at[rows_at(thin_row(d, p), 64)]
        return copies.here(a, dst.at[0, rows_at((1 - p) * 128, 64)], send + 4 + p)

    def holds(rel):
        return lax.rem(d ^ rel, 2) == p

    def start_wide():
        for rel in (1, 2, 3, 0):
            wide(rel).start()

    def start_thin():
        for rel in (1, 2, 3, 0):

            @pl.when(holds(rel))
            def _():
                if rel:
                    thin(rel, p).start()
                else:
                    thin_own().start()
                thin(rel, 1 - p).start()

    def finish():
        wide(0).wait()
        for rel in (1, 2, 3):
            wide(rel).wait()
        for rel in range(4):

            @pl.when(holds(rel))
            def _():
                if rel:
                    thin(rel, p).wait_send()
                else:
                    thin_own().wait()
                thin(rel, 1 - p).wait_send()

        @pl.when(jnp.logical_not(holds(0)))
        def _():
            thin(0, p).wait_recv()

        for rel in (1, 2, 3):
            thin(rel, p).wait_recv()

    return start_wide, start_thin, finish


UNIT_PARTS = ((0, 256), (256, 128), (384, 256), (640, 128))


def unit_column(j, z, core):
    plane = 2 * (j // 2) + (core if j % 2 == 0 else 1 - core)
    return plane * 1536 + z * 384 + core * (128 if j % 2 == 0 else 256)


def lanes(start, size):
    return pl.ds(pl.multiple_of(start, 128), size)


def nt(left, right):
    return lax.dot_general(left, right, (((1,), (1,)), ((), ())), preferred_element_type=F32)


def tn(left, right):
    return lax.dot_general(left, right, (((0,), (0,)), ((), ())), preferred_element_type=F32)


def layer_kernel(
    x, prefix, wq, wk, wv, wo, wg, wu, wd, gains, cosine, sine, dy,
    output, x_grad, gain_out, out_q, out_k, out_v, out_o, out_g, out_u, out_d,
    n1_kept, got_gu, got_d, got_qkv,
    xs, n1, ys, partial, partial2, from_twin, from_left, from_right, from_twin2, from_left2, from_right2,
    w_qkv, w_o, w_gu, w_d, qkv, raw, o, lse, act, d_gu, hidden, d_hidden, x_own, d_kv, d_qkv,
    wo_mid, wo_back, got_o, gain_buf, gain_acc, gain_one, gain_two, gain_qk, gain_vec, gain_ctx, gain_dp,
    sends, receives,
):
    g = Place()
    k = Copies(sends, receives)
    d, c, z, p = g.d, g.c, g.z, g.p
    meet()
    own = rows_at(c * BLOCK, BLOCK)
    shard = rows_at(d * 512, 512)
    mine = rows_at(d * 512 + c * 64, 64)

    gain_buf[d, c] = gains[...]
    gain_slots = k.take(12)

    def gain_over_ctx(rel):
        return k.to(gain_buf.at[d, c], gain_buf.at[d, c], (d, c ^ rel), gain_slots + rel)

    def gain_over_dp(rel):
        return k.to(gain_buf.at[d], gain_buf.at[d], (d ^ rel, c), gain_slots + 8 + rel)

    for rel in range(1, 8):
        gain_over_ctx(rel).start()

    own_slots = k.take(3)
    own_copies = [
        k.here(x, xs.at[own], own_slots),
        k.here(x, x_own, own_slots + 1),
        k.here(dy, ys.at[own], own_slots + 2),
    ]
    for copy in own_copies:
        copy.start()

    qkv_slots = k.take(24)

    def qkv_to(rel, j):
        other = c ^ rel
        width = 256 if j == 0 else 128
        src = (wq, wk, wv)[j].at[:, lanes(other * width, width)]
        dst = w_qkv.at[mine, pl.ds((0, 256, 384)[j], width)]
        slot = qkv_slots + 3 * rel + j
        return k.to(src, dst, (d, other), slot) if rel else k.here(src, dst, slot)

    for rel in range(8):
        for j in range(3):
            qkv_to(rel, j).start()
    own_copies[0].wait()
    tokens = Gather(k, g, xs)
    tokens.start()
    at_end = (z == 0) | (z == 3)
    gu_slots = k.take(64)

    def gu_to(which, rel, j):
        place, count = UNIT_PARTS[j]
        column = unit_column(j, z ^ (rel // 2), p ^ (rel % 2))
        src = (wg, wu)[which].at[:, lanes(column, count)]
        dst = w_gu.at[mine, pl.ds(which * 768 + place, count)]
        slot = gu_slots + which * 32 + rel * 4 + j
        return k.to(src, dst, (d, c ^ rel), slot) if rel else k.here(src, dst, slot)

    def gu_start(*groups):
        for which in range(2):
            for group in groups:
                for rel in (2 * group, 2 * group + 1):
                    for j in range(4):
                        gu_to(which, rel, j).start()

    @pl.when(at_end)
    def _():
        gu_start(1)


    wo_slots = k.take(20)
    far = c // 4

    def wo_over_dp(rel):
        src, dst = wo.at[rows_at((d ^ rel) * 16, 16)], wo_mid.at[d]
        slot = wo_slots + rel
        return k.to(src, dst, (d ^ rel, c), slot) if rel else k.here(src, dst, slot)

    def wo_over_ctx(rel):
        src, dst = wo_mid.at[z ^ rel], w_o.at[lax.rem(c, 4), rows_at(d * 16, 16)]
        return k.to(
            src, dst, (d, 2 * (z ^ rel) + far), wo_slots + 4 + rel, wo_slots + 8 + lax.rem(c, 4)
        )

    def wo_stay():
        return k.here(
            wo_mid.at[z], w_o.at[lax.rem(c, 4), rows_at(d * 16, 16)], wo_slots + 4
        )

    wo_stays = far == p
    for rel in range(4):
        wo_over_dp(rel).start()

    start_thin, start_wide, spread_wide, finish_down = down_to_units(g, k, wd, w_d)

    for rel in range(1, 8):
        gain_over_ctx(rel).wait_recv()
    for rel in range(1, 4):
        gain_over_dp(rel).start()
    start_thin()
    for rel in range(1, 4):
        gain_over_dp(rel).wait_recv()
    gain_acc[...] = jnp.zeros_like(gain_acc)
    for i in range(32):
        row = gain_buf[i // 8, i % 8][0:8, :].astype(F32)
        row = jnp.concatenate([row, jnp.zeros((8, 128), F32)], 1)
        shift = (8 * i) % 128
        if shift:
            row = pltpu.roll(row, shift, 1)
        first = 136 * i - shift
        gain_acc[:, first : first + 384] += row

    def normalize(block):
        def body(i, carry):
            at = rows_at(block * BLOCK + i * 16, 16)
            v = xs[at, :].astype(F32)
            r = lax.rsqrt(jnp.mean(v * v, -1, keepdims=True) + EPSILON)
            n1[at, :] = (v * r * gain_acc[0:1, 0:2048]).astype(BF)
            return carry

        lax.fori_loop(0, BLOCK // 16, body, 0)

    normalize(c)
    for j in range(3):
        qkv_to(0, j).wait()
        for rel in range(1, 8):
            qkv_to(rel, j).wait_recv()
    spread_qkv = Spread(k, g, lambda e, half: w_qkv.at[rows_at(e * 512 + half * 256, 256)])
    spread_qkv.start()
    tokens.twin_own()
    normalize(c ^ 1)

    def each_side(step, use):
        def side(i, carry):
            chip = jnp.where(i == 0, z - 1 - step, z + 1 + step)

            @pl.when((chip >= 0) & (chip <= 3))
            def _():
                use(chip)

            return carry

        lax.fori_loop(0, 2, side, 0)

    def normalize_chip(chip):
        normalize(2 * chip)
        normalize(2 * chip + 1)

    gain_q, gain_k = gain_acc[0:1, 4096:4224], gain_acc[0:1, 4224:4352]

    def rotated(value, gain, at):
        r = lax.rsqrt(jnp.mean(value * value, -1, keepdims=True) + EPSILON)
        value = value * r * gain
        return value * cosine[at, :] + pltpu.roll(value, 64, 1) * sine[at, :]

    def project(chip):
        at = rows_at(chip * 256, 256)
        product = jnp.dot(n1[at, :], w_qkv[...], preferred_element_type=F32)
        raw[at, :] = product[:, :384]
        for j, gain in ((0, gain_q), (1, gain_q), (2, gain_k)):
            qkv[at, j * 128 : j * 128 + 128] = rotated(
                product[:, j * 128 : j * 128 + 128], gain, at
            ).astype(BF)
        qkv[at, 384:512] = product[:, 384:].astype(BF)

    def project_all(first, last):
        def body(i, carry):
            step = first + i // 2
            chip = jnp.where(lax.rem(i, 2) == 0, z - 1 - step, z + 1 + step)

            @pl.when((chip >= 0) & (chip <= 3) & ((step >= 0) | (lax.rem(i, 2) == 0)))
            def _():
                project(chip)

            return carry

        lax.fori_loop(0, 2 * (last - first), body, 0)

    tokens.step(0)

    @pl.when(jnp.logical_not(at_end))
    def _():
        gu_start(3)

    for rel in range(4):
        if rel == 0:
            wo_over_dp(0).wait()
        else:
            wo_over_dp(rel).wait_recv()
    for rel in range(1, 4):
        wo_over_ctx(rel).start()

    @pl.when(wo_stays)
    def _():
        wo_stay().start()

    @pl.when(jnp.logical_not(wo_stays))
    def _():
        wo_over_ctx(0).start()

    tokens.twin_step(0)
    each_side(0, normalize_chip)
    tokens.step(1)
    spread_qkv.forward()
    tokens.twin_step(1)
    each_side(1, normalize_chip)
    for i in range(4):

        @pl.when(jnp.logical_not(c == 4 * p + i))
        def _():
            src, dst = wo_mid.at[0], w_o.at[0, rows_at(0, 16)]
            k.to(src, dst, (d, c ^ 1), wo_slots + 4, wo_slots + 8 + i).wait_recv()

    @pl.when(wo_stays)
    def _():
        wo_stay().wait()

    spread_o = Direct(k, g, lambda e: w_o.at[:, rows_at(e * 16, 16)])
    spread_o.start()
    start_wide()
    spread_qkv.finish()
    project_all(-1, 1)
    tokens.step(2)
    tokens.twin_step(2)
    each_side(2, normalize_chip)

    def gu_take(which):
        for rel in range(8):
            for j in range(4):
                if rel == 0:
                    gu_to(which, rel, j).wait()
                else:
                    gu_to(which, rel, j).wait_recv()

    @pl.when(at_end)
    def _():
        gu_start(0, 2, 3)

    project_all(1, 3)
    keep_slots = k.take(2)
    keep = k.here(n1, n1_kept, keep_slots)
    keep.start()

    limit = prefix[0]
    scale = HEAD_SIZE**-0.5

    def head_scores(head, at, first_row):
        scores = nt(qkv[at, head * 128 : head * 128 + 128], qkv[:, 256:384]) * scale
        row = first_row + lax.broadcasted_iota(jnp.int32, (256, 1), 0)
        column = lax.broadcasted_iota(jnp.int32, (1, 1024), 1)
        return jnp.where(column < jnp.maximum(row + 1, limit), scores, -1e30)

    def attend(head):
        def body(i, carry):
            at = rows_at(i * 256, 256)
            scores = head_scores(head, at, i * 256)
            top = jnp.max(scores, -1, keepdims=True)
            expo = jnp.exp(scores - top)
            total = jnp.sum(expo, -1, keepdims=True)
            probs = (expo * (1.0 / total)).astype(BF)
            value = jnp.dot(probs, qkv[:, 384:512], preferred_element_type=F32)
            o[at, head * 128 : head * 128 + 128] = value.astype(BF)
            lse[head, at, :] = jnp.broadcast_to(top + jnp.log(total), (256, 128))
            return carry

        lax.fori_loop(0, 4, body, 0)

    attend(0)
    attend(1)

    @pl.when(jnp.logical_not(at_end))
    def _():
        gu_start(0, 1, 2)

    spread_wide.forward()
    tokens.drain()
    spread_o.finish()
    sum_one = Scatter(k, g, partial, from_twin, from_left, from_right)
    for chip in (3, 0, 2, 1):

        def columns(j, carry):
            cols = lanes(j * 512, 512)
            rows = pl.ds(chip * 256, 256)
            value = jnp.dot(
                o[rows, :], w_o[:, :, cols].reshape(256, 512), preferred_element_type=F32
            )
            partial[rows, cols] = value.astype(BF)
            return carry

        lax.fori_loop(0, 4, columns, 0)
        sum_one.send_twin(chip)
    own_copies[2].wait()
    d_hidden[...] = ys[own, :].astype(F32)
    upstream = Gather(k, g, ys)

    def upstream_goes(step):
        upstream.start_line(step == z, step == 3 - z)


    sum_one.take_twin(3)
    sum_one.take_twin(0)
    sum_one.send_ends(0, 0)
    sum_one.take_twin(2)
    sum_one.take_twin(1)
    sum_one.send_ends(0, 1, 2)
    sum_one.send_ends(1, 0, 1, 2)
    gu_take(0)
    spread_gate = Spread(
        k, g, lambda e, half: w_gu.at[rows_at(e * 512 + half * 256, 256), pl.ds(0, 768)]
    )
    spread_gate.start()
    sum_one.relay(0, 0)
    gu_take(1)
    spread_up = Spread(
        k, g, lambda e, half: w_gu.at[rows_at(e * 512 + half * 256, 256), pl.ds(768, 768)]
    )
    spread_up.start()
    sum_one.relay(1, 0)
    own_copies[1].wait()

    def done_one(at, value):
        rows = rows_at(at, 16)
        h = x_own[rows, :].astype(F32) + value
        r = lax.rsqrt(jnp.mean(h * h, -1, keepdims=True) + EPSILON)
        hidden[rows, :] = h
        xs[rows_at(c * BLOCK + at, 16), :] = (h * r * gain_acc[0:1, 2048:4096]).astype(BF)

    seconds = Gather(k, g, xs)
    sum_one.last(done_one, 0)
    seconds.start_part(0)
    sum_one.relay(0, 1)
    spread_gate.forward()
    sum_one.relay(1, 1)
    seconds.step_part(0, 0)
    sum_one.last(done_one, 1)
    seconds.start_part(1)
    spread_up.forward()
    upstream_goes(0)
    upstream.start_twin()
    seconds.step_part(1, 0)
    seconds.step_part(0, 1)
    upstream_goes(1)
    spread_gate.finish()
    finish_down()
    sum_one.drain()
    keep.wait()
    spread_up.finish()
    sum_two = Scatter(k, g, partial2, from_twin, from_left, from_right)
    sum_out = Scatter(k, g, partial, from_twin2, from_left2, from_right2, parts=1)

    def feed_forward(chip):
        at = rows_at(chip * 256, 256)

        def units(j, carry):
            cols, up_cols = lanes(j * 256, 256), lanes(768 + j * 256, 256)
            gate = jnp.dot(xs[at, :], w_gu[:, cols], preferred_element_type=F32)
            up = jnp.dot(xs[at, :], w_gu[:, up_cols], preferred_element_type=F32)
            act[at, cols] = (gate * up * (1.0 / (1.0 + jnp.exp(-gate)))).astype(BF)
            d_gu[at, cols] = gate.astype(BF)
            d_gu[at, up_cols] = up.astype(BF)
            return carry

        lax.fori_loop(0, 3, units, 0)

        def columns(j, carry):
            cols = lanes(j * 512, 512)
            partial[at, cols] = jnp.dot(
                act[at, :], w_d[:, cols], preferred_element_type=F32
            ).astype(BF)
            return carry

        lax.fori_loop(0, 4, columns, 0)
        sum_out.send_twin(chip)

    def feed_back(chip):
        at = rows_at(chip * 256, 256)

        def units(j, carry):
            cols, up_cols = lanes(j * 256, 256), lanes(768 + j * 256, 256)
            d_act = nt(ys[at, :], w_d[rows_at(j * 256, 256), :])
            gate, up = d_gu[at, cols].astype(F32), d_gu[at, up_cols].astype(F32)
            sig = 1.0 / (1.0 + jnp.exp(-gate))
            d_gu[at, cols] = (d_act * up * sig * (1.0 + gate * (1.0 - sig))).astype(BF)
            d_gu[at, up_cols] = (d_act * gate * sig).astype(BF)
            return carry

        lax.fori_loop(0, 3, units, 0)

        def columns(j, carry):
            rows = rows_at(j * 512, 512)
            partial2[at, lanes(j * 512, 512)] = nt(d_gu[at, :], w_gu[rows, :]).astype(BF)
            return carry

        lax.fori_loop(0, 4, columns, 0)
        sum_two.send_twin(chip)

    def visit(gather, use, between=None, taken=(0, 0), used=None):
        inner = jnp.where(z <= 1, 1, -1)

        def body(step, carry):
            @pl.when(step == 0)
            def _():
                gather.twin_own()

            @pl.when(step > 0)
            @jax.named_scope("twin")
            def _():
                gather.twin_step(step - 1)

            def side(i, carry):
                chip = jnp.where(i == 0, z + inner * step, z - inner * step)

                @pl.when((chip >= 0) & (chip <= 3) & ((i == 0) | (step > 0)))
                @jax.named_scope("use")
                def _():
                    use(chip)

                if used is not None:

                    @pl.when(i == 0)
                    def _():
                        used(step)

                for part in range(gather.parts):

                    @pl.when((i == 0) & (step >= taken[part]) & (step < 3))
                    @jax.named_scope("arrive")
                    def _():
                        gather.step_part(step, part)

                if between is not None:

                    @pl.when(i == 0)
                    @jax.named_scope("between")
                    def _():
                        between(step)

                return carry

            lax.fori_loop(0, 2, side, 0)
            return carry

        lax.fori_loop(0, 4, body, 0)

    def upstream_passes(step):
        @pl.when(step == 1)
        def _():
            upstream_goes(2)

        @pl.when((step == 2) & jnp.logical_not(at_end))
        def _():
            upstream.step(0)

    visit(seconds, feed_forward, taken=(2, 1), between=upstream_passes)

    @pl.when(at_end)
    def _():
        upstream.step(0)

    for i in (3, 0):
        sum_out.take_twin(i)
    sum_out.start()
    for i in (2, 1):
        sum_out.take_twin(i)

    @pl.when(at_end)
    def _():
        sum_out.advance(0)

    def out_goes(step):
        @pl.when((step == 3) & jnp.logical_not(at_end))
        def _():
            sum_out.advance(0)

    visit(upstream, feed_back, taken=(1, 1), between=out_goes)
    sum_two.take_twin(3)
    sum_two.take_twin(0)
    sum_two.send_ends(0, 0)
    sum_two.take_twin(2)
    sum_two.take_twin(1)
    sum_two.send_ends(0, 1, 2)
    sum_two.send_ends(1, 0, 1)
    for spread in (spread_qkv, spread_o, spread_wide, spread_gate, spread_up):
        spread.drain()
    upstream.drain()
    seconds.drain()

    def fold_gu(which):
        cols = pl.ds(which * 768, 768)

        def stage(i):
            block = (0, 4, 1, 5, 2, 3)[i]
            return ys.at[pl.ds((block // 2) * 256, 256), pl.ds((block % 2) * 768, 768)]

        return Fold(
            k, g, lambda e, half: w_gu.at[rows_at(e * 512 + half * 256, 256), cols],
            lambda i: got_gu.at[i, :, cols], stage,
        )

    folds = [fold_gu(0), fold_gu(1)]

    def add_stages(piece, stages):
        def body(i, carry):
            rows = pl.ds(pl.multiple_of(i * 16, 16), 16)
            value = piece[rows, :].astype(F32)
            for stage in stages:
                value = value + stage[rows, :].astype(F32)
            piece[rows, :] = value.astype(BF)
            return carry

        lax.fori_loop(0, 16, body, 0)

    def gu_gradient(which):
        def body(j, carry):
            cols = lanes(j * 512, 512)
            w_gu[rows_at(j * 512, 512), which * 768 : which * 768 + 768] = tn(
                xs[:, cols], d_gu[:, which * 768 : which * 768 + 768]
            ).astype(BF)
            return carry

        lax.fori_loop(0, 4, body, 0)
        folds[which].start()

    def down_gradient(j, carry):
        rows = rows_at(j * 256, 256)
        for i in range(2):
            cols = slice(i * 1024, i * 1024 + 1024)
            w_d[rows, cols] = tn(act[:, lanes(j * 256, 256)], ys[:, cols]).astype(BF)
        return carry

    gu_gradient(0)
    gu_gradient(1)
    load = k.here(n1_kept, xs, keep_slots + 1)
    load.start()
    lax.fori_loop(0, 3, down_gradient, 0)
    start_wide_back, start_thin_back, finish_down_back = down_to_owners(g, k, w_d, got_d)
    start_wide_back()
    sum_two.relay(0, 0)
    folds[0].middle(add_stages)
    sum_two.relay(1, 0)
    gain_two[...] = jnp.zeros_like(gain_two)

    def done_two(at, value):
        rows = rows_at(at, 16)
        there = rows_at(c * BLOCK + at, 16)
        h = hidden[rows, :]
        r = lax.rsqrt(jnp.mean(h * h, -1, keepdims=True) + EPSILON)
        scaled = value * gain_acc[0:1, 2048:4096]
        mean = jnp.mean(h * scaled, -1, keepdims=True)
        d_h = d_hidden[rows, :] + r * scaled - h * (r * r * r * mean)
        part = value * h * r
        gain_two[...] += part[0:8, :] + part[8:16, :]
        d_hidden[rows, :] = d_h
        n1[there, :] = d_h.astype(BF)

    thirds = Gather(k, g, n1)
    sum_two.last(done_two, 0)
    thirds.start_part(0)
    sum_two.send_ends(1, 2)

    @pl.when(at_end)
    def _():
        sum_out.advance(1)

    sum_two.relay(0, 1)
    sum_two.relay(1, 1)
    thirds.step_part(0, 0)
    sum_two.last(done_two, 1)
    thirds.start_part(1)

    folds[1].middle(add_stages)
    thirds.step_part(1, 0)
    thirds.step_part(0, 1)

    sum_two.drain()
    d_kv[...] = jnp.zeros_like(d_kv)
    gain_qk[...] = jnp.zeros_like(gain_qk)

    def unrotated(gradient, value, gain, at):
        gradient = gradient * cosine[at, :] + pltpu.roll(gradient * sine[at, :], 64, 1)
        r = lax.rsqrt(jnp.mean(value * value, -1, keepdims=True) + EPSILON)
        part = gradient * value * r
        gradient = gradient * gain
        mean = jnp.mean(gradient * value, -1, keepdims=True)
        result = gradient * r - value * (r * r * r * mean)
        return result, jnp.sum(part.reshape(-1, 8, 128), 0)

    def attend_back(chip):
        at = rows_at(chip * 256, 256)
        d_o = nt(n1[at, :], w_o[...].reshape(256, 2048)).astype(BF)
        for head in range(2):
            cols = slice(head * 128, head * 128 + 128)
            probs = jnp.exp(head_scores(head, at, chip * 256) - lse[head, at, 0:1])
            d_probs = nt(d_o[:, cols], qkv[:, 384:512])
            delta = jnp.sum(d_probs * probs, -1, keepdims=True)
            d_scores = (probs * (d_probs - delta)).astype(BF)
            d_q = jnp.dot(d_scores, qkv[:, 256:384], preferred_element_type=F32) * scale
            d_kv[:, 0:128] += tn(d_scores, qkv[at, cols]) * scale
            d_kv[:, 128:256] += tn(probs.astype(BF), d_o[:, cols])
            d_q, part = unrotated(d_q, raw[at, cols], gain_q, at)
            d_qkv[at, cols] = d_q.astype(BF)
            gain_qk[:, 0:128] += part

    stage_slots = k.take(16)
    gu_back = k.take(64)

    def gu_home(which, rel, j):
        place, count = UNIT_PARTS[j]
        src = w_gu.at[rows_at(d * 512 + (c ^ rel) * 64, 64), pl.ds(which * 768 + place, count)]
        dst = (out_g, out_u)[which].at[:, lanes(unit_column(j, z, p), count)]
        slot = gu_back + which * 32 + rel * 4 + j
        return k.to(src, dst, (d, c ^ rel), slot) if rel else k.here(src, dst, slot)

    def sum_gu(which):
        folds[which].final(add_stages)
        for rel in range(8):
            for j in range(4):
                gu_home(which, rel, j).start()

    def meanwhile(step):
        @pl.when(step == 1)
        def _():
            @pl.when(jnp.logical_not(at_end))
            def _():
                sum_out.advance(1)

            sum_gu(0)

        @pl.when(step == 2)
        def _():
            sum_gu(1)

    visit(thirds, attend_back, taken=(2, 1), between=meanwhile)

    attn_slots = k.take(8)

    def qkv_rows(e, first, count):
        return d_gu.at[rows_at(lax.rem(e, 2) * 512 + first, count), lanes((e // 2) * 512, 512)]

    def qkv_over_dp(rel):
        return k.to(
            qkv_rows(d ^ rel, 0, 512), got_qkv.at[rel - 1], (d ^ rel, c), attn_slots + rel - 1
        )

    def wo_grad_over_dp(rel):
        src = w_o.at[:, rows_at((d ^ rel) * 16, 16)]
        return k.to(src, got_o.at[rel - 1], (d ^ rel, c), attn_slots + 3 + rel)

    def wo_gradient(j, carry):
        cols = lanes(j * 512, 512)
        w_o[:, :, cols] = tn(o[...], n1[:, cols]).astype(BF).reshape(4, 64, 512)
        return carry

    lax.fori_loop(0, 4, wo_gradient, 0)
    for rel in (1, 2, 3):
        wo_grad_over_dp(rel).start()

    def finish_keys(i, carry):
        at = rows_at(i * 256, 256)
        d_k, part = unrotated(d_kv[at, 0:128], raw[at, 256:384], gain_k, at)
        d_qkv[at, 256:384] = d_k.astype(BF)
        d_qkv[at, 384:512] = d_kv[at, 128:256].astype(BF)
        gain_qk[:, 128:256] += part
        return carry

    lax.fori_loop(0, 4, finish_keys, 0)
    load.wait()

    def qkv_gradient(e, carry):
        cols = lanes(e * 512, 512)
        rows, place = rows_at(lax.rem(e, 2) * 512, 512), lanes((e // 2) * 512, 512)
        d_gu[rows, place] = tn(xs[:, cols], d_qkv[...]).astype(BF)
        return carry

    lax.fori_loop(0, 4, qkv_gradient, 0)
    for rel in (1, 2, 3):
        qkv_over_dp(rel).start()
    start_thin_back()
    sum_three = Scatter(k, g, partial2, from_twin, from_left, from_right)
    for chip in (3, 0, 2, 1):

        def columns(j, carry):
            cols = lanes(j * 512, 512)
            rows = pl.ds(chip * 256, 256)
            value = nt(d_qkv[rows, :], w_qkv[rows_at(j * 512, 512), :])
            partial2[rows, cols] = value.astype(BF)
            return carry

        lax.fori_loop(0, 4, columns, 0)
        sum_three.send_twin(chip)
    sum_three.take_twin(3)
    sum_three.take_twin(0)
    sum_three.start()
    sum_three.take_twin(2)
    sum_three.take_twin(1)

    def gain_columns(e, carry):
        rows, place = rows_at(lax.rem(e, 2) * 512, 512), lanes((e // 2) * 512, 512)
        product = d_gu[rows, place].astype(F32) * w_qkv[rows_at(e * 512, 512), :].astype(F32)
        gain_one[:, lanes(e * 512, 512)] = nt(jnp.ones((8, 512), BF), product.astype(BF))
        return carry

    lax.fori_loop(0, 4, gain_columns, 0)
    gain_vec[:, 0:2048] = gain_one[0:1, :] / gain_acc[0:1, 0:2048]
    gain_vec[:, 2048:4096] = jnp.sum(gain_two[...], 0, keepdims=True)
    gain_vec[:, 4096:4352] = jnp.sum(gain_qk[...], 0, keepdims=True)
    sum_slots = k.take(12)

    def gain_sum_over_ctx(rel):
        return k.to(gain_vec, gain_ctx.at[rel - 1], (d, c ^ rel), sum_slots + rel)

    def gain_sum_over_dp(rel):
        return k.to(gain_out, gain_dp.at[rel - 1], (d ^ rel, c), sum_slots + 8 + rel)

    for rel in range(1, 8):
        gain_sum_over_ctx(rel).start()
    for rel in (1, 2, 3):
        wo_grad_over_dp(rel).wait()
    for i in range(4):
        rows = rows_at(d * 16, 16)
        value = w_o[i, rows, :].astype(F32)
        for j in range(3):
            value = value + got_o[j, i].astype(F32)
        w_o[i, rows, :] = value.astype(BF)
    back_slots = k.take(20)

    def wo_back_ctx(i):
        src, dst = w_o.at[i, rows_at(d * 16, 16)], wo_back.at[z]
        return k.to(src, dst, (d, 4 * p + i), back_slots + i, back_slots + 4 + z)

    def wo_back_here(i):
        return k.here(w_o.at[i, rows_at(d * 16, 16)], wo_back.at[z], back_slots + i)

    def wo_home(rel):
        src, dst = wo_back.at[d ^ rel], out_o.at[rows_at(d * 16, 16)]
        slot = back_slots + 8 + rel
        return k.to(src, dst, (d ^ rel, c), slot) if rel else k.here(src, dst, slot)

    for i in range(4):

        @pl.when(c == 4 * p + i)
        def _():
            wo_back_here(i).start()

        @pl.when(c != 4 * p + i)
        def _():
            wo_back_ctx(i).start()

    sum_three.advance(0)


    sum_three.advance(1)

    qkv_back = k.take(24)

    def qkv_home(rel, j):
        other = c ^ rel
        width = 256 if j == 0 else 128
        src = d_gu.at[
            rows_at(lax.rem(d, 2) * 512 + other * 64, 64),
            lanes((d // 2) * 512 + (0, 256, 384)[j], width),
        ]
        dst = (out_q, out_k, out_v)[j].at[:, lanes(c * width, width)]
        slot = qkv_back + 3 * rel + j
        return k.to(src, dst, (d, other), slot) if rel else k.here(src, dst, slot)

    for rel in (1, 2, 3):
        qkv_over_dp(rel).wait()
    qkv_stage = [
        k.here(
            got_qkv.at[i],
            ys.at[pl.ds(512, 512), pl.ds(i * 512, 512)],
            stage_slots + 11 + i,
        )
        for i in range(3)
    ]
    for copy in qkv_stage:
        copy.start()
    for copy in qkv_stage:
        copy.wait()

    def add_qkv(i, carry):
        at = i * 16
        rows, place = rows_at(lax.rem(d, 2) * 512 + at, 16), lanes((d // 2) * 512, 512)
        value = d_gu[rows, place].astype(F32)
        for j in range(3):
            value = value + ys[rows_at(512 + at, 16), j * 512 : j * 512 + 512].astype(F32)
        d_gu[rows, place] = value.astype(BF)
        return carry

    lax.fori_loop(0, 32, add_qkv, 0)
    for rel in range(8):
        for j in range(3):
            qkv_home(rel, j).start()
    for j in range(4):

        @pl.when(jnp.logical_not((j == z) & wo_stays))
        def _():
            src, dst = w_o.at[0, rows_at(0, 16)], wo_back.at[0]
            k.to(src, dst, (d, c ^ 1), back_slots, back_slots + 4 + j).wait_recv()

    for i in range(4):

        @pl.when(c == 4 * p + i)
        def _():
            wo_back_here(i).wait()

        @pl.when(c != 4 * p + i)
        def _():
            wo_back_ctx(i).wait_send()

    for rel in range(4):
        wo_home(rel).start()

    total = gain_vec[...]
    for rel in range(1, 8):
        gain_sum_over_ctx(rel).wait()
        total = total + gain_ctx[rel - 1]
    gain_out[...] = total
    for rel in range(1, 4):
        gain_sum_over_dp(rel).start()

    sum_out.advance(2)

    def done_out(at, value):
        rows = rows_at(at, 16)
        output[rows, :] = (hidden[rows, :] + value).astype(BF)

    sum_out.finish(done_out)

    finish_down_back()
    stages = [
        k.here(got_d.at[i], ys.at[pl.ds(i * 192, 192)], stage_slots + 6 + i) for i in range(4)
    ]
    for copy in stages:
        copy.start()
    for copy in stages:
        copy.wait()

    def add_down(i, carry):
        at = i * 16
        value = 0.0
        for j in range(4):
            value = value + ys[rows_at(j * 192 + at, 16), :].astype(F32)
        ys[rows_at(at, 16), :] = value.astype(BF)
        return carry

    lax.fori_loop(0, 12, add_down, 0)
    down_home = k.here(ys.at[pl.ds(0, 192)], out_d, stage_slots + 10)
    down_home.start()

    sum_three.advance(2)

    def done_three(at, value):
        rows = rows_at(at, 16)
        v = x_own[rows, :].astype(F32)
        r = lax.rsqrt(jnp.mean(v * v, -1, keepdims=True) + EPSILON)
        scaled = value * gain_acc[0:1, 0:2048]
        mean = jnp.mean(v * scaled, -1, keepdims=True)
        x_grad[rows, :] = (d_hidden[rows, :] + r * scaled - v * (r * r * r * mean)).astype(BF)

    sum_three.finish(done_three)
    total = gain_out[...]
    for rel in range(1, 4):
        gain_sum_over_dp(rel).wait()
        total = total + gain_dp[rel - 1]
    gain_out[...] = total

    for rel in range(8):
        for j in range(3):
            qkv_home(rel, j).wait()
            if rel:
                qkv_to(rel, j).wait_send()
        for which in range(2):
            for j in range(4):
                gu_home(which, rel, j).wait()
                if rel:
                    gu_to(which, rel, j).wait_send()
        if rel:
            gain_over_ctx(rel).wait_send()
    for rel in range(4):
        wo_home(rel).wait()
        if rel:
            gain_over_dp(rel).wait_send()
            wo_over_dp(rel).wait_send()
            wo_over_ctx(rel).wait_send()

    @pl.when(jnp.logical_not(wo_stays))
    def _():
        wo_over_ctx(0).wait_send()

    down_home.wait()
    for fold in folds:
        fold.drain()
    thirds.drain()
    sum_out.drain()
    sum_three.drain()


def run_layer(x, prefix, wq, wk, wv, wo, wg, wu, wd, gains, cosine, sine, dy):
    width = 2048
    any_space, vmem = pl.BlockSpec(memory_space=pl.ANY), pl.BlockSpec(memory_space=pltpu.VMEM)
    shape, hold = jax.ShapeDtypeStruct, pltpu.VMEM
    return pl.pallas_call(
        layer_kernel,
        out_shape=(
            shape((BLOCK, width), BF), shape((BLOCK, width), BF), shape((1, 4352), F32),
            shape((64, 2048), BF), shape((64, 1024), BF), shape((64, 1024), BF), shape((64, 2048), BF),
            shape((64, 6144), BF), shape((64, 6144), BF), shape((192, 2048), BF),
            shape((1024, width), BF), shape((6, 256, 1536), BF), shape((4, 192, 2048), BF),
            shape((3, 512, 512), BF),
        ),
        in_specs=[any_space, pl.BlockSpec(memory_space=pltpu.SMEM)] + [any_space] * 7 + [vmem] * 3 + [any_space],
        out_specs=(vmem,) * 3 + (any_space,) * 11,
        scratch_shapes=[
            hold((1024, width), BF), hold((1024, width), BF), hold((1024, width), BF),
            hold((1024, width), BF), hold((1024, width), BF),
            hold((512, width), BF), hold((384, width), BF), hold((384, width), BF),
            hold((512, width), BF), hold((384, width), BF), hold((384, width), BF),
            hold((width, 512), BF), hold((4, 64, width), BF), hold((width, 1536), BF), hold((768, width), BF),
            hold((1024, 512), BF), hold((1024, 384), F32), hold((1024, 256), BF), hold((2, 1024, 128), F32),
            hold((1024, 768), BF), hold((1024, 1536), BF),
            hold((BLOCK, width), F32), hold((BLOCK, width), F32), hold((BLOCK, width), BF),
            hold((1024, 256), F32), hold((1024, 512), BF),
            hold((4, 16, width), BF), hold((4, 16, width), BF), hold((3, 4, 16, width), BF),
            hold((4, 8, 16, 256), BF), hold((8, 4608), F32), hold((8, width), F32), hold((8, width), F32),
            hold((8, 256), F32), hold((1, 4352), F32), hold((7, 1, 4352), F32), hold((3, 1, 4352), F32),
            pltpu.SemaphoreType.DMA((SLOTS,)), pltpu.SemaphoreType.DMA((SLOTS,)),
        ],
        compiler_params=pltpu.CompilerParams(
            collective_id=0, has_side_effects=True, vmem_limit_bytes=VMEM_BYTES
        ),
        name="layer",
    )(x, prefix, wq, wk, wv, wo, wg, wu, wd, gains, cosine, sine, dy)


SLOTS = 640


def widen_kernel(*refs):
    narrow, wide = refs[:9], refs[9:18]
    held, turned, sems = refs[18:27], refs[27:34], refs[34]
    loads = [pltpu.make_async_copy(a, b, sems.at[i]) for i, (a, b) in enumerate(zip(narrow, held))]
    stores = [
        pltpu.make_async_copy(a, b, sems.at[9 + i])
        for i, (a, b) in enumerate(zip(turned + held[7:], wide))
    ]
    for copy in loads:
        copy.start()
    for load, store, a, b in zip(loads, stores, held, turned):
        load.wait()

        def body(i, carry):
            rows = rows_at(i * 32, 32)
            b[rows, :] = a[rows, :].astype(F32)
            return carry

        lax.fori_loop(0, a.shape[0] // 32, body, 0)
        store.start()
    for i in (7, 8):
        loads[i].wait()
        stores[i].start()
    for copy in stores:
        copy.wait()


def widen(narrow, same):
    place, shape, hold = pl.BlockSpec(memory_space=pltpu.HBM), jax.ShapeDtypeStruct, pltpu.VMEM
    return pl.pallas_call(
        widen_kernel,
        out_shape=tuple(shape(a.shape, F32) for a in narrow) + tuple(shape(a.shape, BF) for a in same),
        in_specs=[place] * 9,
        out_specs=(place,) * 9,
        scratch_shapes=[hold(a.shape, BF) for a in narrow + same]
        + [hold(a.shape, F32) for a in narrow]
        + [pltpu.SemaphoreType.DMA((18,))],
        compiler_params=pltpu.CompilerParams(vmem_limit_bytes=VMEM_BYTES),
        name="widen",
    )(*narrow, *same)


def rope_tables(length):
    freqs = ROPE_BASE ** (-(np.arange(HEAD_SIZE // 2, dtype=np.float32) * 2.0 / HEAD_SIZE))
    angles = np.arange(length, dtype=np.float32)[:, None] * freqs.astype(np.float32)[None, :]
    cosine, sine = np.cos(angles), np.sin(angles)
    return np.concatenate([cosine, cosine], 1), np.concatenate([-sine, sine], 1)


def with_kernel(layer_input, prefix, wq, wk, wv, wo, w_gate, w_up, w_down, gains, cotangent):
    cosine, sine = rope_tables(layer_input.shape[1] * 8)
    results = run_layer(
        layer_input[0], prefix, wq, wk, wv, wo, w_gate, w_up, w_down,
        jnp.pad(gains.reshape(1, 136), ((0, 15), (0, 120))),
        cosine, sine, cotangent[0],
    )
    output, x_grad, gain_sum = results[:3]
    first = (lax.axis_index("dp") * 8 + lax.axis_index("ctx")) * 136
    gains_grad = lax.dynamic_slice_in_dim(gain_sum[0], first, 136, 0)
    big_first = (8, 7, 9, 3, 6, 4, 5)
    final = widen([results[i] for i in big_first], [output, x_grad])
    wide = tuple(final[big_first.index(i)] for i in range(3, 10))
    return (final[7][None], final[8][None]) + wide + (gains_grad,)


def solution(mesh):
    tokens = P("dp", "ctx", None)
    matrix = P(("dp", "ctx"), None)
    vector = P(("dp", "ctx"))
    small = mesh.shape["dp"] == 4 and mesh.shape["ctx"] == 8
    return jax.shard_map(
        with_kernel if small else general,
        mesh=mesh,
        in_specs=(tokens, P("dp")) + (matrix,) * 7 + (vector, tokens),
        out_specs=(tokens, tokens) + (matrix,) * 7 + (vector,),
        check_vma=False,
    )
```

```python
import jax
import jax.numpy as jnp
import numpy as np
from jax import lax
from jax.experimental import pallas as pl
from jax.experimental.pallas import tpu as pltpu
from jax.sharding import PartitionSpec as P

QUERY_HEADS = 16
KEY_VALUE_HEADS = 8
HEAD_SIZE = 128
EPSILON = 1e-06
ROPE_BASE = 1000000.0
BF = jnp.bfloat16
F32 = jnp.float32


def rms_scale(value, gain):
    return value * lax.rsqrt(jnp.mean(value * value, -1, keepdims=True) + EPSILON) * gain


def rotate(value, cosine, sine):
    half = value.shape[-1] // 2
    first = value[..., :half]
    second = value[..., half:]
    return jnp.concatenate([first * cosine - second * sine, second * cosine + first * sine], -1)


def mm(left, right):
    return jnp.dot(left, right, preferred_element_type=F32)


def mm_tn(left, right):
    return lax.dot_general(left, right, (((0,), (0,)), ((), ())), preferred_element_type=F32)


def mm_nt(left, right):
    return lax.dot_general(left, right, (((1,), (1,)), ((), ())), preferred_element_type=F32)


def gated_unit(gate, up):
    return jax.nn.silu(gate) * up


def swap_ctx(pieces):
    return lax.all_to_all(pieces, "ctx", 0, 0)


def general(layer_input, prefix, wq, wk, wv, wo, w_gate, w_up, w_down, gains, cotangent):
    nd, nc = lax.axis_size("dp"), lax.axis_size("ctx")
    me = lax.axis_index("ctx")
    rows = layer_input.shape[1]
    seq = rows * nc
    depth, width = wq.shape[0], layer_input.shape[2]
    heads = QUERY_HEADS // nc
    copies = max(1, nc // KEY_VALUE_HEADS)
    kv_heads = max(1, KEY_VALUE_HEADS // nc)
    unit = w_down.shape[0]
    scale = HEAD_SIZE ** (-0.5)

    def columns_to(weight, parts):
        return jnp.moveaxis(weight.reshape(depth, parts, -1), 1, 0)

    def by_head(weight, repeat):
        parts = columns_to(weight, nc // repeat)
        return jnp.repeat(parts, repeat, 0) if repeat > 1 else parts

    def by_unit(weight):
        return jnp.transpose(weight.reshape(depth, nd, nc, unit), (2, 0, 1, 3)).reshape(
            nc, depth, nd * unit
        )

    def everywhere(array):
        return lax.all_gather(array, "dp", axis=0, tiled=True)

    qkv_piece = jnp.concatenate([by_head(wq, 1), by_head(wk, copies), by_head(wv, copies)], 2)
    w_qkv = everywhere(swap_ctx(qkv_piece).reshape(nc * depth, -1))
    plane = nc * wo.shape[0]
    span = QUERY_HEADS * HEAD_SIZE // nc
    need = span // wo.shape[0]
    by_plane = everywhere(wo).reshape(nd, wo.shape[0], width)
    wanted = jnp.stack([by_plane[i * span // plane] for i in range(nc)])
    arrived = swap_ctx(wanted)
    first_source = (me * span % plane) // wo.shape[0]
    w_o = lax.dynamic_slice_in_dim(arrived, first_source, need, 0).reshape(span, width)
    w_gu = everywhere(
        swap_ctx(jnp.concatenate([by_unit(w_gate), by_unit(w_up)], 2)).reshape(nc * depth, -1)
    )
    w_d = everywhere(w_down)
    gain_all = lax.all_gather(gains, ("dp", "ctx"), axis=0, tiled=True).astype(F32)
    gain_one = gain_all[:width]
    gain_two = gain_all[width : 2 * width]
    gain_q = gain_all[2 * width : 2 * width + HEAD_SIZE]
    gain_k = gain_all[2 * width + HEAD_SIZE :]

    def whole(array):
        return lax.all_gather(array, "ctx", axis=0, tiled=True)

    def own_sum(partial):
        return lax.psum_scatter(partial.astype(BF), "ctx", scatter_dimension=0, tiled=True).astype(
            F32
        )

    pos = jnp.arange(seq, dtype=jnp.int32)
    visible = (pos[None, :] <= pos[:, None]) | (pos[None, :] < prefix[0])
    freqs = ROPE_BASE ** (-(jnp.arange(HEAD_SIZE // 2, dtype=F32) * 2.0 / HEAD_SIZE))
    angles = pos.astype(F32)[:, None] * freqs[None, :]
    cosine = jnp.cos(angles)[:, None, :]
    sine = jnp.sin(angles)[:, None, :]

    def prepare_heads(raw, gain):
        return rotate(rms_scale(raw, gain), cosine, sine)

    inputs = layer_input[0].astype(F32)
    n1, back_one = jax.vjp(rms_scale, inputs, gain_one)
    n1_all = whole(n1.astype(BF))
    dy_all = whole(cotangent[0])
    qkv = mm(n1_all, w_qkv)
    q_raw = qkv[:, : heads * HEAD_SIZE].reshape(seq, heads, HEAD_SIZE)
    k_raw = qkv[:, heads * HEAD_SIZE : (heads + kv_heads) * HEAD_SIZE].reshape(
        seq, kv_heads, HEAD_SIZE
    )
    v = qkv[:, (heads + kv_heads) * HEAD_SIZE :].astype(BF).reshape(seq, kv_heads, HEAD_SIZE)
    q_rot, back_q = jax.vjp(prepare_heads, q_raw, gain_q)
    k_rot, back_k = jax.vjp(prepare_heads, k_raw, gain_k)
    q_rot = q_rot.astype(BF).reshape(seq, kv_heads, -1, HEAD_SIZE)
    k_rot = k_rot.astype(BF)
    scores = jnp.einsum("tkgd,skd->kgts", q_rot, k_rot, preferred_element_type=F32) * scale
    scores = jnp.where(visible[None, None], scores, -1e30)
    top = jnp.max(scores, -1, keepdims=True)
    expo = jnp.exp(scores - top)
    total = jnp.sum(expo, -1, keepdims=True)
    probs = expo / total
    probs_bf = probs.astype(BF)
    o = jnp.einsum("kgts,skd->tkgd", probs_bf, v, preferred_element_type=F32).astype(BF)
    o = o.reshape(seq, heads * HEAD_SIZE)
    hidden = inputs + own_sum(mm(o, w_o))
    n2, back_two = jax.vjp(rms_scale, hidden, gain_two)
    n2_all = whole(n2.astype(BF))
    gu = mm(n2_all, w_gu)
    gate, up = gu[:, : nd * unit], gu[:, nd * unit :]
    active, back_gated = jax.vjp(gated_unit, gate, up)
    active = active.astype(BF)
    output = (hidden + own_sum(mm(active, w_d))).astype(BF)
    def row_sum(term):
        return lax.psum_scatter(term.astype(BF), "dp", scatter_dimension=0, tiled=True)

    down_grad = row_sum(mm_tn(active, dy_all)).astype(F32)
    d_gate, d_up = back_gated(mm_nt(dy_all, w_d))
    d_gu = jnp.concatenate([d_gate.astype(BF), d_up.astype(BF)], 1)
    gu_sum = swap_ctx(row_sum(mm_tn(n2_all, d_gu)).reshape(nc, depth, -1)).astype(F32)
    gu_sum = gu_sum.reshape(nc, depth, 2, nd, unit)
    gu_sum = jnp.transpose(gu_sum, (2, 1, 3, 0, 4)).reshape(2, depth, -1)
    gate_grad, up_grad = gu_sum[0], gu_sum[1]
    upstream = cotangent[0].astype(F32)
    d_hidden_part, d_gain_two = back_two(own_sum(mm_nt(d_gu, w_gu)))
    d_hidden = upstream + d_hidden_part
    d_attn = whole(d_hidden.astype(BF))
    wo_term = mm_tn(o, d_attn).astype(BF).reshape(need, wo.shape[0], width)
    slots = jnp.zeros((nc, wo.shape[0], width), BF)
    slots = lax.dynamic_update_slice_in_dim(slots, wo_term, first_source, 0)
    back_home = swap_ctx(slots)
    mine = []
    for plane_index in range(nd):
        total_plane = 0
        for i in range(nc):
            if i * span // plane == plane_index:
                total_plane = total_plane + back_home[i].astype(F32)
        mine.append(total_plane)
    wo_grad = lax.psum_scatter(
        jnp.stack(mine).astype(BF), "dp", scatter_dimension=0, tiled=True
    )[0].astype(F32)
    d_o = mm_nt(d_attn, w_o).astype(BF).reshape(seq, kv_heads, -1, HEAD_SIZE)
    d_probs = jnp.einsum("tkgd,skd->kgts", d_o, v, preferred_element_type=F32)
    d_v = jnp.einsum("kgts,tkgd->skd", probs_bf, d_o, preferred_element_type=F32).astype(BF)
    d_scores = (probs * (d_probs - jnp.sum(d_probs * probs, -1, keepdims=True))).astype(BF)
    d_q = jnp.einsum("kgts,skd->tkgd", d_scores, k_rot, preferred_element_type=F32) * scale
    d_k = jnp.einsum("kgts,tkgd->skd", d_scores, q_rot, preferred_element_type=F32) * scale
    d_q, d_gain_q = back_q(d_q.reshape(seq, heads, HEAD_SIZE))
    d_k, d_gain_k = back_k(d_k)
    d_qkv = jnp.concatenate(
        [a.reshape(seq, -1).astype(BF) for a in (d_q, d_k, d_v)], 1
    )
    qkv_sum = swap_ctx(row_sum(mm_tn(n1_all, d_qkv)).reshape(nc, depth, -1)).astype(F32)
    at_k, at_v = heads * HEAD_SIZE, (heads + kv_heads) * HEAD_SIZE

    def columns_back(part, repeat):
        part = part.reshape(nc // repeat, repeat, depth, -1).sum(1)
        return jnp.moveaxis(part, 0, 1).reshape(depth, -1)

    wq_grad = columns_back(qkv_sum[:, :, :at_k], 1)
    wk_grad = columns_back(qkv_sum[:, :, at_k:at_v], copies)
    wv_grad = columns_back(qkv_sum[:, :, at_v:], copies)
    d_input_part, d_gain_one = back_one(own_sum(mm_nt(d_qkv, w_qkv)))
    x_grad = (d_hidden + d_input_part).astype(BF)
    gain_term = jnp.concatenate([d_gain_one, d_gain_two, d_gain_q, d_gain_k])
    gains_grad = lax.psum_scatter(gain_term, ("dp", "ctx"), scatter_dimension=0, tiled=True)
    return (
        output[None], x_grad[None], wq_grad, wk_grad, wv_grad, wo_grad,
        gate_grad, up_grad, down_grad, gains_grad,
    )


MESH = pl.DeviceIdType.MESH
BLOCK = 128
VMEM_BYTES = 64 << 20


class Copies:
    def __init__(self, sends, receives):
        self.sends, self.receives = sends, receives
        self.used = 0

    def take(self, count=1):
        first = self.used
        self.used += count
        if self.used > SLOTS:
            raise ValueError("more semaphores")
        return first

    def to(self, src, dst, device, slot, receive_slot=None):
        receive_slot = slot if receive_slot is None else receive_slot
        return pltpu.make_async_remote_copy(
            src_ref=src,
            dst_ref=dst,
            send_sem=self.sends.at[slot],
            recv_sem=self.receives.at[receive_slot],
            device_id=device,
            device_id_type=MESH,
        )

    def here(self, src, dst, slot):
        return pltpu.make_async_copy(src, dst, self.sends.at[slot])


class Place:
    def __init__(self):
        self.d = lax.axis_index("dp")
        self.c = lax.axis_index("ctx")
        self.z = self.c // 2
        self.p = lax.rem(self.c, 2)

    def at(self, d, c):
        return (d, c)


def meet():
    barrier = pltpu.get_barrier_semaphore()
    d, c = lax.axis_index("dp"), lax.axis_index("ctx")
    partners = [(d, c ^ rel) for rel in range(1, 8)]
    partners += [(d ^ rel, c ^ twin) for rel in range(1, 4) for twin in range(2)]
    for partner in partners:
        pl.semaphore_signal(barrier, inc=1, device_id=partner, device_id_type=MESH)
    pl.semaphore_wait(barrier, len(partners))


def when(condition, then):
    if isinstance(condition, bool):
        if condition:
            then()
    else:
        pl.when(condition)(then)


def rows_at(start, size):
    return pl.ds(pl.multiple_of(start, 16), size)


class Gather:
    def __init__(self, copies, place, buf, parts=2):
        self.k, self.g, self.buf, self.parts = copies, place, buf, parts
        self.size = BLOCK // parts
        self.right = copies.take(3 * parts)
        self.left = copies.take(3 * parts)
        self.twin = copies.take(7 * parts)

    def piece(self, z, p, part):
        return self.buf.at[rows_at((2 * z + p) * BLOCK + part * self.size, self.size)]

    def line(self, step, part, rightwards):
        g = self.g
        z = g.z - step if rightwards else g.z + step
        slot = (self.right if rightwards else self.left) + step * self.parts + part
        piece = self.piece(z, g.p, part)
        to = g.c + 2 if rightwards else g.c - 2
        return self.k.to(piece, piece, (g.d, to), slot)

    def wait_line(self, step, part, rightwards):
        piece = self.piece(self.g.z, self.g.p, part)
        slot = (self.right if rightwards else self.left) + step * self.parts + part
        self.k.to(piece, piece, (self.g.d, self.g.c ^ 1), slot).wait_recv()

    def twins(self, order, z, part):
        piece = self.piece(z, self.g.p, part)
        return self.k.to(piece, piece, (self.g.d, self.g.c ^ 1), self.twin + order * self.parts + part)

    def can_send(self, step, rightwards):
        z = self.g.z
        return (z >= step) & (z < 3) if rightwards else (z + step <= 3) & (z > 0)

    def gets(self, step, rightwards):
        z = self.g.z
        return z >= step + 1 if rightwards else z + step + 1 <= 3

    def start(self):
        for part in range(self.parts):
            self.start_part(part)

    def start_part(self, part):
        for rightwards in (True, False):

            @pl.when(self.can_send(0, rightwards))
            def _():
                self.line(0, part, rightwards).start()

        self.twins(0, self.g.z, part).start()

    def start_line(self, right, left):
        for part in range(self.parts):
            for now, rightwards in ((right, True), (left, False)):

                @pl.when(now & self.can_send(0, rightwards))
                def _():
                    self.line(0, part, rightwards).start()

    def start_twin(self):
        for part in range(self.parts):
            self.twins(0, self.g.z, part).start()

    def step(self, step):
        for part in range(self.parts):
            self.step_part(step, part)

    def step_part(self, step, part):
        for side, rightwards in enumerate((True, False)):
            z = self.g.z - 1 - step if rightwards else self.g.z + 1 + step

            @pl.when(self.gets(step, rightwards))
            def _():
                self.wait_line(step, part, rightwards)

                def on():
                    @pl.when(self.can_send(step + 1, rightwards))
                    def _():
                        self.line(step + 1, part, rightwards).start()

                when(step < 2, on)
                self.twins(1 + 2 * step + side, z, part).start()

    def twin_own(self):
        for part in range(self.parts):
            self.twins(0, self.g.z, part).wait_recv()

    def twin_step(self, step):
        for part in range(self.parts):
            for side, rightwards in enumerate((True, False)):

                @pl.when(self.gets(step, rightwards))
                def _():
                    self.twins(1 + 2 * step + side, self.g.z, part).wait_recv()

    def drain(self):
        for part in range(self.parts):
            self.twins(0, self.g.z, part).wait_send()
            for step in range(3):
                for side, rightwards in enumerate((True, False)):

                    @pl.when(self.can_send(step, rightwards))
                    def _():
                        self.line(step, part, rightwards).wait_send()

                    @pl.when(self.gets(step, rightwards))
                    def _():
                        self.twins(1 + 2 * step + side, self.g.z, part).wait_send()


def add_rows(dst, dst_row, a, a_row, b, b_row, count):
    def body(i, carry):
        at = i * 32
        total = a[rows_at(a_row + at, 32), :].astype(F32) + b[rows_at(b_row + at, 32), :].astype(F32)
        dst[rows_at(dst_row + at, 32), :] = total.astype(dst.dtype)
        return carry

    lax.fori_loop(0, count // 32, body, 0)


class Scatter:
    def __init__(self, copies, place, partial, from_twin, from_left, from_right, parts=2):
        self.k, self.g = copies, place
        self.partial, self.from_twin = partial, from_twin
        self.from_line = {True: from_left, False: from_right}
        self.parts, self.size = parts, BLOCK // parts
        self.twin = copies.take(4)
        self.slots = {True: copies.take(3 * parts), False: copies.take(3 * parts)}

    def row(self, z, p):
        return (2 * z + p) * BLOCK

    def twins(self, z, slot):
        g = self.g
        src = self.partial.at[rows_at(self.row(z, 1 - g.p), BLOCK)]
        dst = self.from_twin.at[rows_at(z * BLOCK, BLOCK)]
        return self.k.to(src, dst, (g.d, g.c ^ 1), self.twin + slot)

    def send_twin(self, z):
        self.twins(z, z).start()

    def take_twin(self, z):
        self.twins(z, z).wait_recv()
        at = self.row(z, self.g.p)
        add_rows(self.partial, at, self.partial, at, self.from_twin, z * BLOCK, BLOCK)

    def target(self, step, rightwards):
        return self.g.z + 3 - step if rightwards else self.g.z - 3 + step

    def can_send(self, step, rightwards):
        z = self.g.z
        return z <= step if rightwards else 3 - z <= step

    def gets(self, step, rightwards):
        z = self.g.z
        return (z >= 1) & (z - 1 <= step) if rightwards else (z <= 2) & (2 - z <= step)

    def line(self, step, rightwards, part):
        g = self.g
        at = self.row(self.target(step, rightwards), g.p) + part * self.size
        src = self.partial.at[rows_at(at, self.size)]
        dst = self.from_line[rightwards].at[rows_at(step * BLOCK + part * self.size, self.size)]
        slot = self.slots[rightwards] + step * self.parts + part
        return self.k.to(src, dst, (g.d, g.c + 2 if rightwards else g.c - 2), slot)

    def wait_line(self, step, rightwards, part):
        src = self.partial.at[pl.ds(0, self.size)]
        dst = self.from_line[rightwards].at[rows_at(step * BLOCK + part * self.size, self.size)]
        slot = self.slots[rightwards] + step * self.parts + part
        self.k.to(src, dst, (self.g.d, self.g.c ^ 1), slot).wait_recv()

    def send(self, step, part):
        for rightwards in (True, False):

            @pl.when(self.can_send(step, rightwards))
            def _():
                self.line(step, rightwards, part).start()

    def start(self):
        for part in range(self.parts):
            self.send(0, part)

    def advance(self, step):
        for part in range(self.parts):
            for rightwards in (True, False):

                @pl.when(self.gets(step, rightwards))
                def _():
                    self.wait_line(step, rightwards, part)

                    def add():
                        z = self.g.z + 2 - step if rightwards else self.g.z - 2 + step
                        at = self.row(z, self.g.p) + part * self.size
                        add_rows(
                            self.partial, at, self.partial, at, self.from_line[rightwards],
                            step * BLOCK + part * self.size, self.size,
                        )

                    when(step < 2, add)

            when(step < 2, lambda: self.send(step + 1, part))

    def finish(self, done, slot=2, part=None):
        g = self.g
        own = self.row(g.z, g.p)
        first, count = (0, BLOCK) if part is None else (part * self.size, self.size)

        def body(i, carry):
            at = first + i * 16
            total = self.partial[rows_at(own + at, 16), :].astype(F32)
            a = self.from_line[True][rows_at(slot * BLOCK + at, 16), :].astype(F32)
            b = self.from_line[False][rows_at(slot * BLOCK + at, 16), :].astype(F32)
            total = total + jnp.where(g.z >= 1, a, 0.0) + jnp.where(g.z <= 2, b, 0.0)
            done(at, total)
            return carry

        lax.fori_loop(0, count // 16, body, 0)

    def send_ends(self, part, *steps):
        for rightwards in (True, False):

            @pl.when(self.g.z == (0 if rightwards else 3))
            def _():
                for step in steps:
                    self.line(step, rightwards, part).start()

    def relay(self, step, part):
        for rightwards in (True, False):

            @pl.when(self.gets(step, rightwards))
            def _():
                self.wait_line(step, rightwards, part)
                z = self.g.z + 2 - step if rightwards else self.g.z - 2 + step
                at = self.row(z, self.g.p) + part * self.size
                add_rows(
                    self.partial, at, self.partial, at, self.from_line[rightwards],
                    step * BLOCK + part * self.size, self.size,
                )
                self.line(step + 1, rightwards, part).start()

    def last(self, done, part):
        for rightwards in (True, False):

            @pl.when(self.gets(2, rightwards))
            def _():
                self.wait_line(2, rightwards, part)

        self.finish(done, part=part)

    def drain(self):
        for z in range(4):
            self.twins(z, z).wait_send()
        for step in range(3):
            for part in range(self.parts):
                for rightwards in (True, False):

                    @pl.when(self.can_send(step, rightwards))
                    def _():
                        self.line(step, rightwards, part).wait_send()


class Outwards(Scatter):
    def __init__(self, *args):
        super().__init__(*args, parts=1)

    def can_send(self, step, rightwards):
        return self.g.z + 1 + step <= 3 if rightwards else self.g.z - 1 - step >= 0

    def target(self, step, rightwards):
        return self.g.z + 1 + step if rightwards else self.g.z - 1 - step

    def send_ends(self, step):
        for rightwards in (True, False):

            @pl.when(self.g.z == (0 if rightwards else 3))
            def _():
                self.line(step, rightwards, 0).start()

    def relay(self, step, chip):
        for rightwards in (True, False):

            @pl.when(self.g.z == (chip if rightwards else 3 - chip))
            def _():
                self.wait_line(step, rightwards, 0)
                at = self.row(self.target(step - 1, rightwards), self.g.p)
                add_rows(
                    self.partial, at, self.partial, at, self.from_line[rightwards], step * BLOCK, BLOCK
                )
                self.line(step - 1, rightwards, 0).start()

    def take_own(self):
        for rightwards in (True, False):

            @pl.when(self.g.z >= 1 if rightwards else self.g.z <= 2)
            def _():
                self.wait_line(0, rightwards, 0)


class Spread:
    def __init__(self, copies, place, piece):
        self.k, self.g, self.piece = copies, place, piece
        self.slots = copies.take(6)

    def direct(self, half, rel):
        g = self.g
        piece = self.piece(g.d, half)
        return self.k.to(piece, piece, (g.d ^ rel, g.c), self.slots + 2 * (rel - 1) + half)

    def passed(self, rel):
        g = self.g
        piece = self.piece(g.d ^ (3 - rel), rel - 1)
        return self.k.to(piece, piece, (g.d ^ rel, g.c), self.slots + 4 + rel - 1)

    def start(self):
        for half, rel in ((0, 1), (1, 2), (1, 1), (0, 2)):
            self.direct(half, rel).start()

    def forward(self):
        self.direct(1, 1).wait_recv()
        self.passed(2).start()
        self.direct(0, 2).wait_recv()
        self.passed(1).start()

    def finish(self):
        self.direct(0, 1).wait_recv()
        self.direct(1, 2).wait_recv()
        self.passed(1).wait_recv()
        self.passed(2).wait_recv()

    def drain(self):
        for half, rel in ((0, 1), (1, 2), (1, 1), (0, 2)):
            self.direct(half, rel).wait_send()
        self.passed(1).wait_send()
        self.passed(2).wait_send()


class Direct:
    def __init__(self, copies, place, piece):
        self.k, self.g, self.piece = copies, place, piece
        self.slots = copies.take(3)

    def copy(self, rel):
        piece = self.piece(self.g.d)
        return self.k.to(piece, piece, (self.g.d ^ rel, self.g.c), self.slots + rel - 1)

    def start(self):
        for rel in (1, 2, 3):
            self.copy(rel).start()

    def finish(self):
        for rel in (1, 2, 3):
            self.copy(rel).wait_recv()

    def drain(self):
        for rel in (1, 2, 3):
            self.copy(rel).wait_send()


class Fold:
    def __init__(self, copies, place, piece, got, stage):
        self.k, self.g, self.piece, self.got, self.stage = copies, place, piece, got, stage
        self.slots = copies.take(6)
        self.loads = copies.take(6)

    def first(self, half, passed):
        g = self.g
        rel = 1 + half
        src = self.piece(g.d ^ (3 if passed else rel), half)
        i = 2 * half + passed
        return self.k.to(src, self.got(i), (g.d ^ rel, g.c), self.slots + i)

    def second(self, half):
        g = self.g
        rel = 2 - half
        return self.k.to(
            self.piece(g.d ^ rel, half), self.got(4 + half), (g.d ^ rel, g.c), self.slots + 4 + half
        )

    def load(self, i):
        return self.k.here(self.got(i), self.stage(i), self.loads + i)

    def start(self):
        for passed in (1, 0):
            for half in range(2):
                self.first(half, passed).start()

    def middle(self, add):
        for half in range(2):
            self.first(half, 1).wait_recv()
            self.load(2 * half + 1).start()
        for half in range(2):
            self.load(2 * half + 1).wait()
            add(self.piece(self.g.d ^ (2 - half), half), (self.stage(2 * half + 1),))
            self.second(half).start()

    def final(self, add):
        for half in range(2):
            self.first(half, 0).wait_recv()
            self.load(2 * half).start()
        for half in range(2):
            self.second(half).wait_recv()
            self.load(4 + half).start()
        for half in range(2):
            self.load(2 * half).wait()
            self.load(4 + half).wait()
            add(self.piece(self.g.d, half), (self.stage(2 * half), self.stage(4 + half)))

    def drain(self):
        for half in range(2):
            for passed in range(2):
                self.first(half, passed).wait_send()
            self.second(half).wait_send()


def down_to_units(place, copies, src, dst):
    g, p, d = place, place.p, place.d
    send, receive = copies.take(8), copies.take(12)
    odd = lax.rem(d, 2)
    wide = (src.at[rows_at(p * 64, 128)], dst.at[rows_at(wide_row(p, d), 128)])
    thin = (src.at[rows_at((1 - p) * 128, 64)], dst.at[rows_at(thin_row(d, p), 64)])
    stays = odd == p

    def thin_to(rel, core):
        return copies.to(
            *thin, (d ^ rel, 2 * g.z + odd), send + 4 + rel, receive + 4 + 2 * rel + core
        )

    def start_thin():
        for rel in (1, 2, 3):
            thin_to(rel, p).start()

        @pl.when(stays)
        def _():
            copies.here(*thin, send + 4).start()

        @pl.when(jnp.logical_not(stays))
        def _():
            thin_to(0, p).start()

    copies.here(*wide, send).start()
    spread = Spread(
        copies, g, lambda e, half: dst.at[rows_at(wide_row(p, e) + half * 64, 64)]
    )

    def start_wide():
        copies.here(*wide, send).wait()
        spread.start()

    def finish():
        spread.finish()

        @pl.when(stays)
        def _():
            copies.here(*thin, send + 4).wait()

        @pl.when(jnp.logical_not(stays))
        def _():
            thin_to(0, p).wait_send()

        for rel in (1, 2, 3):
            thin_to(rel, p).wait_send()
        for rel in range(4):

            @pl.when(lax.rem(d ^ rel, 2) == p)
            def _():
                if rel:
                    thin_to(rel, p).wait_recv()
                thin_to(rel, 1 - p).wait_recv()

    return start_thin, start_wide, spread, finish


def unit_row(core, plane):
    return (plane // 2) * 384 + (lax.rem(plane, 2) ^ core) * 256


def wide_row(core, plane):
    return unit_row(core, plane) + core * lax.rem(plane, 2) * 128


def thin_row(plane, core):
    odd = lax.rem(plane, 2)
    return unit_row(odd, plane) + (1 - odd) * 128 + core * 64


def down_to_owners(place, copies, src, dst):
    g, p, d = place, place.p, place.d
    send, receive = copies.take(12), copies.take(8)

    def wide(rel):
        plane = d ^ rel
        a = src.at[rows_at(wide_row(p, plane), 128)]
        b = dst.at[rel, rows_at(p * 64, 128)]
        if rel == 0:
            return copies.here(a, b, send)
        return copies.to(a, b, (plane, g.c), send + rel, receive + rel)

    def thin(rel, core):
        plane = d ^ rel
        a = src.at[rows_at(thin_row(plane, core), 64)]
        b = dst.at[rel, rows_at((1 - core) * 128, 64)]
        return copies.to(
            a, b, (plane, 2 * g.z + core), send + 4 + 2 * rel + core, receive + 4 + rel
        )

    def thin_own():
        a = src.at[rows_at(thin_row(d, p), 64)]
        return copies.here(a, dst.at[0, rows_at((1 - p) * 128, 64)], send + 4 + p)

    def holds(rel):
        return lax.rem(d ^ rel, 2) == p

    def start_wide():
        for rel in (1, 2, 3, 0):
            wide(rel).start()

    def start_thin():
        for rel in (1, 2, 3, 0):

            @pl.when(holds(rel))
            def _():
                if rel:
                    thin(rel, p).start()
                else:
                    thin_own().start()
                thin(rel, 1 - p).start()

    def finish():
        wide(0).wait()
        for rel in (1, 2, 3):
            wide(rel).wait()
        for rel in range(4):

            @pl.when(holds(rel))
            def _():
                if rel:
                    thin(rel, p).wait_send()
                else:
                    thin_own().wait()
                thin(rel, 1 - p).wait_send()

        @pl.when(jnp.logical_not(holds(0)))
        def _():
            thin(0, p).wait_recv()

        for rel in (1, 2, 3):
            thin(rel, p).wait_recv()

    return start_wide, start_thin, finish


UNIT_PARTS = ((0, 256), (256, 128), (384, 256), (640, 128))


def unit_column(j, z, core):
    plane = 2 * (j // 2) + (core if j % 2 == 0 else 1 - core)
    return plane * 1536 + z * 384 + core * (128 if j % 2 == 0 else 256)


def lanes(start, size):
    return pl.ds(pl.multiple_of(start, 128), size)


def nt(left, right):
    return lax.dot_general(left, right, (((1,), (1,)), ((), ())), preferred_element_type=F32)


def tn(left, right):
    return lax.dot_general(left, right, (((0,), (0,)), ((), ())), preferred_element_type=F32)


def layer_kernel(
    x, prefix, wq, wk, wv, wo, wg, wu, wd, gains, cosine, sine, dy,
    output, x_grad, gain_out, out_q, out_k, out_v, out_o, out_g, out_u, out_d,
    n1_kept, got_gu, got_d, got_qkv,
    xs, n1, ys, partial, partial2, from_twin, from_left, from_right, from_twin2, from_left2, from_right2,
    w_qkv, w_o, w_gu, w_d, qkv, raw, o, lse, act, d_gu, hidden, d_hidden, x_own, d_kv, d_qkv,
    wo_mid, wo_back, got_o, gain_buf, gain_acc, gain_one, gain_two, gain_qk, gain_vec, gain_ctx, gain_dp,
    sends, receives,
):
    g = Place()
    k = Copies(sends, receives)
    d, c, z, p = g.d, g.c, g.z, g.p
    meet()
    own = rows_at(c * BLOCK, BLOCK)
    shard = rows_at(d * 512, 512)
    mine = rows_at(d * 512 + c * 64, 64)

    gain_buf[d, c] = gains[...]
    gain_slots = k.take(12)

    def gain_over_ctx(rel):
        return k.to(gain_buf.at[d, c], gain_buf.at[d, c], (d, c ^ rel), gain_slots + rel)

    def gain_over_dp(rel):
        return k.to(gain_buf.at[d], gain_buf.at[d], (d ^ rel, c), gain_slots + 8 + rel)

    for rel in range(1, 8):
        gain_over_ctx(rel).start()

    own_slots = k.take(3)
    own_copies = [
        k.here(x, xs.at[own], own_slots),
        k.here(x, x_own, own_slots + 1),
        k.here(dy, ys.at[own], own_slots + 2),
    ]
    for copy in own_copies:
        copy.start()

    qkv_slots = k.take(24)

    def qkv_to(rel, j):
        other = c ^ rel
        width = 256 if j == 0 else 128
        src = (wq, wk, wv)[j].at[:, lanes(other * width, width)]
        dst = w_qkv.at[mine, pl.ds((0, 256, 384)[j], width)]
        slot = qkv_slots + 3 * rel + j
        return k.to(src, dst, (d, other), slot) if rel else k.here(src, dst, slot)

    for rel in range(8):
        for j in range(3):
            qkv_to(rel, j).start()
    own_copies[0].wait()
    tokens = Gather(k, g, xs)
    tokens.start()
    at_end = (z == 0) | (z == 3)
    gu_slots = k.take(64)

    def gu_to(which, rel, j):
        place, count = UNIT_PARTS[j]
        column = unit_column(j, z ^ (rel // 2), p ^ (rel % 2))
        src = (wg, wu)[which].at[:, lanes(column, count)]
        dst = w_gu.at[mine, pl.ds(which * 768 + place, count)]
        slot = gu_slots + which * 32 + rel * 4 + j
        return k.to(src, dst, (d, c ^ rel), slot) if rel else k.here(src, dst, slot)

    def gu_start(*groups):
        for which in range(2):
            for group in groups:
                for rel in (2 * group, 2 * group + 1):
                    for j in range(4):
                        gu_to(which, rel, j).start()

    @pl.when(at_end)
    def _():
        gu_start(1)


    wo_slots = k.take(20)
    far = c // 4

    def wo_over_dp(rel):
        src, dst = wo.at[rows_at((d ^ rel) * 16, 16)], wo_mid.at[d]
        slot = wo_slots + rel
        return k.to(src, dst, (d ^ rel, c), slot) if rel else k.here(src, dst, slot)

    def wo_over_ctx(rel):
        src, dst = wo_mid.at[z ^ rel], w_o.at[lax.rem(c, 4), rows_at(d * 16, 16)]
        return k.to(
            src, dst, (d, 2 * (z ^ rel) + far), wo_slots + 4 + rel, wo_slots + 8 + lax.rem(c, 4)
        )

    def wo_stay():
        return k.here(
            wo_mid.at[z], w_o.at[lax.rem(c, 4), rows_at(d * 16, 16)], wo_slots + 4
        )

    wo_stays = far == p
    for rel in range(4):
        wo_over_dp(rel).start()

    start_thin, start_wide, spread_wide, finish_down = down_to_units(g, k, wd, w_d)

    for rel in range(1, 8):
        gain_over_ctx(rel).wait_recv()
    for rel in range(1, 4):
        gain_over_dp(rel).start()
    start_thin()
    for rel in range(1, 4):
        gain_over_dp(rel).wait_recv()
    gain_acc[...] = jnp.zeros_like(gain_acc)
    for i in range(32):
        row = gain_buf[i // 8, i % 8][0:8, :].astype(F32)
        row = jnp.concatenate([row, jnp.zeros((8, 128), F32)], 1)
        shift = (8 * i) % 128
        if shift:
            row = pltpu.roll(row, shift, 1)
        first = 136 * i - shift
        gain_acc[:, first : first + 384] += row

    def normalize(block):
        def body(i, carry):
            at = rows_at(block * BLOCK + i * 16, 16)
            v = xs[at, :].astype(F32)
            r = lax.rsqrt(jnp.mean(v * v, -1, keepdims=True) + EPSILON)
            n1[at, :] = (v * r * gain_acc[0:1, 0:2048]).astype(BF)
            return carry

        lax.fori_loop(0, BLOCK // 16, body, 0)

    normalize(c)
    for j in range(3):
        qkv_to(0, j).wait()
        for rel in range(1, 8):
            qkv_to(rel, j).wait_recv()
    spread_qkv = Spread(k, g, lambda e, half: w_qkv.at[rows_at(e * 512 + half * 256, 256)])
    spread_qkv.start()
    tokens.twin_own()
    normalize(c ^ 1)

    def each_side(step, use):
        def side(i, carry):
            chip = jnp.where(i == 0, z - 1 - step, z + 1 + step)

            @pl.when((chip >= 0) & (chip <= 3))
            def _():
                use(chip)

            return carry

        lax.fori_loop(0, 2, side, 0)

    def normalize_chip(chip):
        normalize(2 * chip)
        normalize(2 * chip + 1)

    gain_q, gain_k = gain_acc[0:1, 4096:4224], gain_acc[0:1, 4224:4352]

    def rotated(value, gain, at):
        r = lax.rsqrt(jnp.mean(value * value, -1, keepdims=True) + EPSILON)
        value = value * r * gain
        return value * cosine[at, :] + pltpu.roll(value, 64, 1) * sine[at, :]

    def project(chip):
        at = rows_at(chip * 256, 256)
        product = jnp.dot(n1[at, :], w_qkv[...], preferred_element_type=F32)
        raw[at, :] = product[:, :384]
        for j, gain in ((0, gain_q), (1, gain_q), (2, gain_k)):
            qkv[at, j * 128 : j * 128 + 128] = rotated(
                product[:, j * 128 : j * 128 + 128], gain, at
            ).astype(BF)
        qkv[at, 384:512] = product[:, 384:].astype(BF)

    def project_all(first, last):
        def body(i, carry):
            step = first + i // 2
            chip = jnp.where(lax.rem(i, 2) == 0, z - 1 - step, z + 1 + step)

            @pl.when((chip >= 0) & (chip <= 3) & ((step >= 0) | (lax.rem(i, 2) == 0)))
            def _():
                project(chip)

            return carry

        lax.fori_loop(0, 2 * (last - first), body, 0)

    tokens.step(0)

    @pl.when(jnp.logical_not(at_end))
    def _():
        gu_start(3)

    for rel in range(4):
        if rel == 0:
            wo_over_dp(0).wait()
        else:
            wo_over_dp(rel).wait_recv()
    for rel in range(1, 4):
        wo_over_ctx(rel).start()

    @pl.when(wo_stays)
    def _():
        wo_stay().start()

    @pl.when(jnp.logical_not(wo_stays))
    def _():
        wo_over_ctx(0).start()

    tokens.twin_step(0)
    each_side(0, normalize_chip)
    tokens.step(1)
    own_copies[2].wait()
    upstream = Gather(k, g, ys)
    upstream.start_line(z == 2, z == 1)
    spread_qkv.forward()
    tokens.twin_step(1)
    each_side(1, normalize_chip)
    for i in range(4):

        @pl.when(jnp.logical_not(c == 4 * p + i))
        def _():
            src, dst = wo_mid.at[0], w_o.at[0, rows_at(0, 16)]
            k.to(src, dst, (d, c ^ 1), wo_slots + 4, wo_slots + 8 + i).wait_recv()

    @pl.when(wo_stays)
    def _():
        wo_stay().wait()

    spread_o = Direct(k, g, lambda e: w_o.at[:, rows_at(e * 16, 16)])
    spread_o.start()
    start_wide()
    spread_qkv.finish()
    project_all(-1, 1)
    tokens.step(2)
    tokens.twin_step(2)
    each_side(2, normalize_chip)

    def gu_take(which):
        for rel in range(8):
            for j in range(4):
                if rel == 0:
                    gu_to(which, rel, j).wait()
                else:
                    gu_to(which, rel, j).wait_recv()

    @pl.when(at_end)
    def _():
        gu_start(0, 2, 3)

    project_all(1, 3)
    keep_slots = k.take(2)
    keep = k.here(n1, n1_kept, keep_slots)
    keep.start()

    limit = prefix[0]
    scale = HEAD_SIZE**-0.5

    def head_scores(head, at, first_row):
        scores = nt(qkv[at, head * 128 : head * 128 + 128], qkv[:, 256:384]) * scale
        row = first_row + lax.broadcasted_iota(jnp.int32, (256, 1), 0)
        column = lax.broadcasted_iota(jnp.int32, (1, 1024), 1)
        return jnp.where(column < jnp.maximum(row + 1, limit), scores, -1e30)

    def attend(head):
        def body(i, carry):
            at = rows_at(i * 256, 256)
            scores = head_scores(head, at, i * 256)
            top = jnp.max(scores, -1, keepdims=True)
            expo = jnp.exp(scores - top)
            total = jnp.sum(expo, -1, keepdims=True)
            probs = (expo * (1.0 / total)).astype(BF)
            value = jnp.dot(probs, qkv[:, 384:512], preferred_element_type=F32)
            o[at, head * 128 : head * 128 + 128] = value.astype(BF)
            lse[head, at, :] = jnp.broadcast_to(top + jnp.log(total), (256, 128))
            return carry

        lax.fori_loop(0, 4, body, 0)

    attend(0)
    attend(1)

    @pl.when(jnp.logical_not(at_end))
    def _():
        gu_start(0, 1, 2)

    spread_wide.forward()
    tokens.drain()
    spread_o.finish()
    sum_one = Scatter(k, g, partial, from_twin, from_left, from_right)
    for chip in (3, 0, 2, 1):

        def columns(j, carry):
            cols = lanes(j * 512, 512)
            rows = pl.ds(chip * 256, 256)
            value = jnp.dot(
                o[rows, :], w_o[:, :, cols].reshape(256, 512), preferred_element_type=F32
            )
            partial[rows, cols] = value.astype(BF)
            return carry

        lax.fori_loop(0, 4, columns, 0)
        sum_one.send_twin(chip)
    d_hidden[...] = ys[own, :].astype(F32)

    def upstream_goes(step):
        upstream.start_line((step == z) & (z < 2), (step == 3 - z) & (z > 1))


    sum_one.take_twin(3)
    sum_one.take_twin(0)
    sum_one.send_ends(0, 0)
    sum_one.take_twin(2)
    sum_one.take_twin(1)
    sum_one.send_ends(0, 1, 2)
    sum_one.send_ends(1, 0, 1, 2)
    gu_take(0)
    spread_gate = Spread(
        k, g, lambda e, half: w_gu.at[rows_at(e * 512 + half * 256, 256), pl.ds(0, 768)]
    )
    spread_gate.start()
    sum_one.relay(0, 0)
    gu_take(1)
    spread_up = Spread(
        k, g, lambda e, half: w_gu.at[rows_at(e * 512 + half * 256, 256), pl.ds(768, 768)]
    )
    spread_up.start()
    sum_one.relay(1, 0)
    own_copies[1].wait()

    def done_one(at, value):
        rows = rows_at(at, 16)
        h = x_own[rows, :].astype(F32) + value
        r = lax.rsqrt(jnp.mean(h * h, -1, keepdims=True) + EPSILON)
        hidden[rows, :] = h
        xs[rows_at(c * BLOCK + at, 16), :] = (h * r * gain_acc[0:1, 2048:4096]).astype(BF)

    seconds = Gather(k, g, xs)
    sum_one.last(done_one, 0)
    seconds.start_part(0)
    sum_one.relay(0, 1)
    spread_gate.forward()
    sum_one.relay(1, 1)
    seconds.step_part(0, 0)
    sum_one.last(done_one, 1)
    seconds.start_part(1)
    spread_up.forward()
    upstream_goes(0)
    upstream.start_twin()
    seconds.step_part(1, 0)
    seconds.step_part(0, 1)
    upstream_goes(1)
    spread_gate.finish()
    finish_down()
    sum_one.drain()
    keep.wait()
    spread_up.finish()
    sum_two = Scatter(k, g, partial2, from_twin, from_left, from_right)
    sum_out = Scatter(k, g, partial, from_twin2, from_left2, from_right2, parts=1)

    def feed_forward(chip):
        at = rows_at(chip * 256, 256)

        def units(j, carry):
            cols, up_cols = lanes(j * 256, 256), lanes(768 + j * 256, 256)
            gate = jnp.dot(xs[at, :], w_gu[:, cols], preferred_element_type=F32)
            up = jnp.dot(xs[at, :], w_gu[:, up_cols], preferred_element_type=F32)
            act[at, cols] = (gate * up * (1.0 / (1.0 + jnp.exp(-gate)))).astype(BF)
            d_gu[at, cols] = gate.astype(BF)
            d_gu[at, up_cols] = up.astype(BF)
            return carry

        lax.fori_loop(0, 3, units, 0)

        def columns(j, carry):
            cols = lanes(j * 512, 512)
            partial[at, cols] = jnp.dot(
                act[at, :], w_d[:, cols], preferred_element_type=F32
            ).astype(BF)
            return carry

        lax.fori_loop(0, 4, columns, 0)
        sum_out.send_twin(chip)

    def feed_back(chip):
        at = rows_at(chip * 256, 256)

        def units(j, carry):
            cols, up_cols = lanes(j * 256, 256), lanes(768 + j * 256, 256)
            d_act = nt(ys[at, :], w_d[rows_at(j * 256, 256), :])
            gate, up = d_gu[at, cols].astype(F32), d_gu[at, up_cols].astype(F32)
            sig = 1.0 / (1.0 + jnp.exp(-gate))
            d_gu[at, cols] = (d_act * up * sig * (1.0 + gate * (1.0 - sig))).astype(BF)
            d_gu[at, up_cols] = (d_act * gate * sig).astype(BF)
            return carry

        lax.fori_loop(0, 3, units, 0)

        def columns(j, carry):
            rows = rows_at(j * 512, 512)
            partial2[at, lanes(j * 512, 512)] = nt(d_gu[at, :], w_gu[rows, :]).astype(BF)
            return carry

        lax.fori_loop(0, 4, columns, 0)
        sum_two.send_twin(chip)

    def visit(gather, use, between=None, taken=(0, 0), used=None):
        inner = jnp.where(z <= 1, 1, -1)

        def body(step, carry):
            @pl.when(step == 0)
            def _():
                gather.twin_own()

            @pl.when(step > 0)
            @jax.named_scope("twin")
            def _():
                gather.twin_step(step - 1)

            def side(i, carry):
                chip = jnp.where(i == 0, z + inner * step, z - inner * step)

                @pl.when((chip >= 0) & (chip <= 3) & ((i == 0) | (step > 0)))
                @jax.named_scope("use")
                def _():
                    use(chip)

                if used is not None:

                    @pl.when(i == 0)
                    def _():
                        used(step)

                for part in range(gather.parts):

                    @pl.when((i == 0) & (step >= taken[part]) & (step < 3))
                    @jax.named_scope("arrive")
                    def _():
                        gather.step_part(step, part)

                if between is not None:

                    @pl.when(i == 0)
                    @jax.named_scope("between")
                    def _():
                        between(step)

                return carry

            lax.fori_loop(0, 2, side, 0)
            return carry

        lax.fori_loop(0, 4, body, 0)

    def upstream_passes(step):
        @pl.when(step == 1)
        def _():
            upstream_goes(2)

        @pl.when((step == 2) & jnp.logical_not(at_end))
        def _():
            upstream.step(0)

    visit(seconds, feed_forward, taken=(2, 1), between=upstream_passes)

    @pl.when(at_end)
    def _():
        upstream.step(0)

    for i in (3, 0):
        sum_out.take_twin(i)
    sum_out.start()
    for i in (2, 1):
        sum_out.take_twin(i)

    @pl.when(at_end)
    def _():
        sum_out.advance(0)

    def out_goes(step):
        @pl.when((step == 3) & jnp.logical_not(at_end))
        def _():
            sum_out.advance(0)

    visit(upstream, feed_back, taken=(1, 1), between=out_goes)
    sum_two.take_twin(3)
    sum_two.take_twin(0)
    sum_two.send_ends(0, 0)
    sum_two.take_twin(2)
    sum_two.take_twin(1)
    sum_two.send_ends(0, 1, 2)
    sum_two.send_ends(1, 0, 1)
    for spread in (spread_qkv, spread_o, spread_wide, spread_gate, spread_up):
        spread.drain()
    upstream.drain()
    seconds.drain()

    def fold_gu(which):
        cols = pl.ds(which * 768, 768)

        def stage(i):
            block = (0, 4, 1, 5, 2, 3)[i]
            return ys.at[pl.ds((block // 2) * 256, 256), pl.ds((block % 2) * 768, 768)]

        return Fold(
            k, g, lambda e, half: w_gu.at[rows_at(e * 512 + half * 256, 256), cols],
            lambda i: got_gu.at[i, :, cols], stage,
        )

    folds = [fold_gu(0), fold_gu(1)]

    def add_stages(piece, stages):
        def body(i, carry):
            rows = pl.ds(pl.multiple_of(i * 16, 16), 16)
            value = piece[rows, :].astype(F32)
            for stage in stages:
                value = value + stage[rows, :].astype(F32)
            piece[rows, :] = value.astype(BF)
            return carry

        lax.fori_loop(0, 16, body, 0)

    def gu_gradient(which):
        def body(j, carry):
            cols = lanes(j * 512, 512)
            w_gu[rows_at(j * 512, 512), which * 768 : which * 768 + 768] = tn(
                xs[:, cols], d_gu[:, which * 768 : which * 768 + 768]
            ).astype(BF)
            return carry

        lax.fori_loop(0, 4, body, 0)
        folds[which].start()

    def down_gradient(j, carry):
        rows = rows_at(j * 256, 256)
        for i in range(2):
            cols = slice(i * 1024, i * 1024 + 1024)
            w_d[rows, cols] = tn(act[:, lanes(j * 256, 256)], ys[:, cols]).astype(BF)
        return carry

    gu_gradient(0)
    gu_gradient(1)
    load = k.here(n1_kept, xs, keep_slots + 1)
    load.start()
    lax.fori_loop(0, 3, down_gradient, 0)
    start_wide_back, start_thin_back, finish_down_back = down_to_owners(g, k, w_d, got_d)
    sum_two.relay(0, 0)
    folds[0].middle(add_stages)
    sum_two.relay(1, 0)
    gain_two[...] = jnp.zeros_like(gain_two)

    def done_two(at, value):
        rows = rows_at(at, 16)
        there = rows_at(c * BLOCK + at, 16)
        h = hidden[rows, :]
        r = lax.rsqrt(jnp.mean(h * h, -1, keepdims=True) + EPSILON)
        scaled = value * gain_acc[0:1, 2048:4096]
        mean = jnp.mean(h * scaled, -1, keepdims=True)
        d_h = d_hidden[rows, :] + r * scaled - h * (r * r * r * mean)
        part = value * h * r
        gain_two[...] += part[0:8, :] + part[8:16, :]
        d_hidden[rows, :] = d_h
        n1[there, :] = d_h.astype(BF)

    thirds = Gather(k, g, n1)
    sum_two.last(done_two, 0)
    thirds.start_part(0)
    sum_two.send_ends(1, 2)
    sum_two.relay(0, 1)
    sum_two.relay(1, 1)
    thirds.step_part(0, 0)
    sum_two.last(done_two, 1)
    thirds.start_part(1)

    @pl.when(at_end)
    def _():
        sum_out.advance(1)


    folds[1].middle(add_stages)
    start_wide_back()
    thirds.step_part(1, 0)
    thirds.step_part(0, 1)

    sum_two.drain()
    d_kv[...] = jnp.zeros_like(d_kv)
    gain_qk[...] = jnp.zeros_like(gain_qk)

    def unrotated(gradient, value, gain, at):
        gradient = gradient * cosine[at, :] + pltpu.roll(gradient * sine[at, :], 64, 1)
        r = lax.rsqrt(jnp.mean(value * value, -1, keepdims=True) + EPSILON)
        part = gradient * value * r
        gradient = gradient * gain
        mean = jnp.mean(gradient * value, -1, keepdims=True)
        result = gradient * r - value * (r * r * r * mean)
        return result, jnp.sum(part.reshape(-1, 8, 128), 0)

    def attend_back(chip):
        at = rows_at(chip * 256, 256)
        d_o = nt(n1[at, :], w_o[...].reshape(256, 2048)).astype(BF)
        for head in range(2):
            cols = slice(head * 128, head * 128 + 128)
            probs = jnp.exp(head_scores(head, at, chip * 256) - lse[head, at, 0:1])
            d_probs = nt(d_o[:, cols], qkv[:, 384:512])
            delta = jnp.sum(d_probs * probs, -1, keepdims=True)
            d_scores = (probs * (d_probs - delta)).astype(BF)
            d_q = jnp.dot(d_scores, qkv[:, 256:384], preferred_element_type=F32) * scale
            d_kv[:, 0:128] += tn(d_scores, qkv[at, cols]) * scale
            d_kv[:, 128:256] += tn(probs.astype(BF), d_o[:, cols])
            d_q, part = unrotated(d_q, raw[at, cols], gain_q, at)
            d_qkv[at, cols] = d_q.astype(BF)
            gain_qk[:, 0:128] += part

    stage_slots = k.take(16)
    gu_back = k.take(64)

    def gu_home(which, rel, j):
        place, count = UNIT_PARTS[j]
        src = w_gu.at[rows_at(d * 512 + (c ^ rel) * 64, 64), pl.ds(which * 768 + place, count)]
        dst = (out_g, out_u)[which].at[:, lanes(unit_column(j, z, p), count)]
        slot = gu_back + which * 32 + rel * 4 + j
        return k.to(src, dst, (d, c ^ rel), slot) if rel else k.here(src, dst, slot)

    def sum_gu(which):
        folds[which].final(add_stages)
        for rel in range(8):
            for j in range(4):
                gu_home(which, rel, j).start()

    def meanwhile(step):
        @pl.when(step == 1)
        def _():
            @pl.when(jnp.logical_not(at_end))
            def _():
                sum_out.advance(1)

            sum_gu(0)

        @pl.when(step == 2)
        def _():
            sum_gu(1)

    visit(thirds, attend_back, taken=(2, 1), between=meanwhile)

    attn_slots = k.take(8)

    def qkv_rows(e, first, count):
        return d_gu.at[rows_at(lax.rem(e, 2) * 512 + first, count), lanes((e // 2) * 512, 512)]

    def qkv_over_dp(rel):
        return k.to(
            qkv_rows(d ^ rel, 0, 512), got_qkv.at[rel - 1], (d ^ rel, c), attn_slots + rel - 1
        )

    def wo_grad_over_dp(rel):
        src = w_o.at[:, rows_at((d ^ rel) * 16, 16)]
        return k.to(src, got_o.at[rel - 1], (d ^ rel, c), attn_slots + 3 + rel)

    def wo_gradient(j, carry):
        cols = lanes(j * 512, 512)
        w_o[:, :, cols] = tn(o[...], n1[:, cols]).astype(BF).reshape(4, 64, 512)
        return carry

    lax.fori_loop(0, 4, wo_gradient, 0)
    for rel in (1, 2, 3):
        wo_grad_over_dp(rel).start()

    def finish_keys(i, carry):
        at = rows_at(i * 256, 256)
        d_k, part = unrotated(d_kv[at, 0:128], raw[at, 256:384], gain_k, at)
        d_qkv[at, 256:384] = d_k.astype(BF)
        d_qkv[at, 384:512] = d_kv[at, 128:256].astype(BF)
        gain_qk[:, 128:256] += part
        return carry

    lax.fori_loop(0, 4, finish_keys, 0)
    load.wait()

    def qkv_gradient(e, carry):
        cols = lanes(e * 512, 512)
        rows, place = rows_at(lax.rem(e, 2) * 512, 512), lanes((e // 2) * 512, 512)
        d_gu[rows, place] = tn(xs[:, cols], d_qkv[...]).astype(BF)
        return carry

    lax.fori_loop(0, 4, qkv_gradient, 0)
    for rel in (1, 2, 3):
        qkv_over_dp(rel).start()
    start_thin_back()
    sum_three = Scatter(k, g, partial2, from_twin, from_left, from_right)
    for chip in (3, 0, 2, 1):

        def columns(j, carry):
            cols = lanes(j * 512, 512)
            rows = pl.ds(chip * 256, 256)
            value = nt(d_qkv[rows, :], w_qkv[rows_at(j * 512, 512), :])
            partial2[rows, cols] = value.astype(BF)
            return carry

        lax.fori_loop(0, 4, columns, 0)
        sum_three.send_twin(chip)
    sum_three.take_twin(3)
    sum_three.take_twin(0)
    sum_three.start()
    sum_three.take_twin(2)
    sum_three.take_twin(1)

    def gain_columns(e, carry):
        rows, place = rows_at(lax.rem(e, 2) * 512, 512), lanes((e // 2) * 512, 512)
        product = d_gu[rows, place].astype(F32) * w_qkv[rows_at(e * 512, 512), :].astype(F32)
        gain_one[:, lanes(e * 512, 512)] = nt(jnp.ones((8, 512), BF), product.astype(BF))
        return carry

    lax.fori_loop(0, 4, gain_columns, 0)
    gain_vec[:, 0:2048] = gain_one[0:1, :] / gain_acc[0:1, 0:2048]
    gain_vec[:, 2048:4096] = jnp.sum(gain_two[...], 0, keepdims=True)
    gain_vec[:, 4096:4352] = jnp.sum(gain_qk[...], 0, keepdims=True)
    sum_slots = k.take(12)

    def gain_sum_over_ctx(rel):
        return k.to(gain_vec, gain_ctx.at[rel - 1], (d, c ^ rel), sum_slots + rel)

    def gain_sum_over_dp(rel):
        return k.to(gain_out, gain_dp.at[rel - 1], (d ^ rel, c), sum_slots + 8 + rel)

    for rel in range(1, 8):
        gain_sum_over_ctx(rel).start()
    for rel in (1, 2, 3):
        wo_grad_over_dp(rel).wait()
    for i in range(4):
        rows = rows_at(d * 16, 16)
        value = w_o[i, rows, :].astype(F32)
        for j in range(3):
            value = value + got_o[j, i].astype(F32)
        w_o[i, rows, :] = value.astype(BF)
    back_slots = k.take(20)

    def wo_back_ctx(i):
        src, dst = w_o.at[i, rows_at(d * 16, 16)], wo_back.at[z]
        return k.to(src, dst, (d, 4 * p + i), back_slots + i, back_slots + 4 + z)

    def wo_back_here(i):
        return k.here(w_o.at[i, rows_at(d * 16, 16)], wo_back.at[z], back_slots + i)

    def wo_home(rel):
        src, dst = wo_back.at[d ^ rel], out_o.at[rows_at(d * 16, 16)]
        slot = back_slots + 8 + rel
        return k.to(src, dst, (d ^ rel, c), slot) if rel else k.here(src, dst, slot)

    for i in range(4):

        @pl.when(c == 4 * p + i)
        def _():
            wo_back_here(i).start()

        @pl.when(c != 4 * p + i)
        def _():
            wo_back_ctx(i).start()

    sum_three.advance(0)


    sum_three.advance(1)

    qkv_back = k.take(24)

    def qkv_home(rel, j):
        other = c ^ rel
        width = 256 if j == 0 else 128
        src = d_gu.at[
            rows_at(lax.rem(d, 2) * 512 + other * 64, 64),
            lanes((d // 2) * 512 + (0, 256, 384)[j], width),
        ]
        dst = (out_q, out_k, out_v)[j].at[:, lanes(c * width, width)]
        slot = qkv_back + 3 * rel + j
        return k.to(src, dst, (d, other), slot) if rel else k.here(src, dst, slot)

    for rel in (1, 2, 3):
        qkv_over_dp(rel).wait()
    qkv_stage = [
        k.here(
            got_qkv.at[i],
            ys.at[pl.ds(512, 512), pl.ds(i * 512, 512)],
            stage_slots + 11 + i,
        )
        for i in range(3)
    ]
    for copy in qkv_stage:
        copy.start()
    for copy in qkv_stage:
        copy.wait()

    def add_qkv(i, carry):
        at = i * 16
        rows, place = rows_at(lax.rem(d, 2) * 512 + at, 16), lanes((d // 2) * 512, 512)
        value = d_gu[rows, place].astype(F32)
        for j in range(3):
            value = value + ys[rows_at(512 + at, 16), j * 512 : j * 512 + 512].astype(F32)
        d_gu[rows, place] = value.astype(BF)
        return carry

    lax.fori_loop(0, 32, add_qkv, 0)
    for rel in range(8):
        for j in range(3):
            qkv_home(rel, j).start()
    for j in range(4):

        @pl.when(jnp.logical_not((j == z) & wo_stays))
        def _():
            src, dst = w_o.at[0, rows_at(0, 16)], wo_back.at[0]
            k.to(src, dst, (d, c ^ 1), back_slots, back_slots + 4 + j).wait_recv()

    for i in range(4):

        @pl.when(c == 4 * p + i)
        def _():
            wo_back_here(i).wait()

        @pl.when(c != 4 * p + i)
        def _():
            wo_back_ctx(i).wait_send()

    for rel in range(4):
        wo_home(rel).start()

    total = gain_vec[...]
    for rel in range(1, 8):
        gain_sum_over_ctx(rel).wait()
        total = total + gain_ctx[rel - 1]
    gain_out[...] = total
    for rel in range(1, 4):
        gain_sum_over_dp(rel).start()

    sum_out.advance(2)

    def done_out(at, value):
        rows = rows_at(at, 16)
        output[rows, :] = (hidden[rows, :] + value).astype(BF)

    sum_out.finish(done_out)

    finish_down_back()
    stages = [
        k.here(got_d.at[i], ys.at[pl.ds(i * 192, 192)], stage_slots + 6 + i) for i in range(4)
    ]
    for copy in stages:
        copy.start()
    for copy in stages:
        copy.wait()

    def add_down(i, carry):
        at = i * 16
        value = 0.0
        for j in range(4):
            value = value + ys[rows_at(j * 192 + at, 16), :].astype(F32)
        ys[rows_at(at, 16), :] = value.astype(BF)
        return carry

    lax.fori_loop(0, 12, add_down, 0)
    down_home = k.here(ys.at[pl.ds(0, 192)], out_d, stage_slots + 10)
    down_home.start()

    sum_three.advance(2)

    def done_three(at, value):
        rows = rows_at(at, 16)
        v = x_own[rows, :].astype(F32)
        r = lax.rsqrt(jnp.mean(v * v, -1, keepdims=True) + EPSILON)
        scaled = value * gain_acc[0:1, 0:2048]
        mean = jnp.mean(v * scaled, -1, keepdims=True)
        x_grad[rows, :] = (d_hidden[rows, :] + r * scaled - v * (r * r * r * mean)).astype(BF)

    sum_three.finish(done_three)
    total = gain_out[...]
    for rel in range(1, 4):
        gain_sum_over_dp(rel).wait()
        total = total + gain_dp[rel - 1]
    gain_out[...] = total

    for rel in range(8):
        for j in range(3):
            qkv_home(rel, j).wait()
            if rel:
                qkv_to(rel, j).wait_send()
        for which in range(2):
            for j in range(4):
                gu_home(which, rel, j).wait()
                if rel:
                    gu_to(which, rel, j).wait_send()
        if rel:
            gain_over_ctx(rel).wait_send()
    for rel in range(4):
        wo_home(rel).wait()
        if rel:
            gain_over_dp(rel).wait_send()
            wo_over_dp(rel).wait_send()
            wo_over_ctx(rel).wait_send()

    @pl.when(jnp.logical_not(wo_stays))
    def _():
        wo_over_ctx(0).wait_send()

    down_home.wait()
    for fold in folds:
        fold.drain()
    thirds.drain()
    sum_out.drain()
    sum_three.drain()


def run_layer(x, prefix, wq, wk, wv, wo, wg, wu, wd, gains, cosine, sine, dy):
    width = 2048
    any_space, vmem = pl.BlockSpec(memory_space=pl.ANY), pl.BlockSpec(memory_space=pltpu.VMEM)
    shape, hold = jax.ShapeDtypeStruct, pltpu.VMEM
    return pl.pallas_call(
        layer_kernel,
        out_shape=(
            shape((BLOCK, width), BF), shape((BLOCK, width), BF), shape((1, 4352), F32),
            shape((64, 2048), BF), shape((64, 1024), BF), shape((64, 1024), BF), shape((64, 2048), BF),
            shape((64, 6144), BF), shape((64, 6144), BF), shape((192, 2048), BF),
            shape((1024, width), BF), shape((6, 256, 1536), BF), shape((4, 192, 2048), BF),
            shape((3, 512, 512), BF),
        ),
        in_specs=[any_space, pl.BlockSpec(memory_space=pltpu.SMEM)] + [any_space] * 7 + [vmem] * 3 + [any_space],
        out_specs=(vmem,) * 3 + (any_space,) * 11,
        scratch_shapes=[
            hold((1024, width), BF), hold((1024, width), BF), hold((1024, width), BF),
            hold((1024, width), BF), hold((1024, width), BF),
            hold((512, width), BF), hold((384, width), BF), hold((384, width), BF),
            hold((512, width), BF), hold((384, width), BF), hold((384, width), BF),
            hold((width, 512), BF), hold((4, 64, width), BF), hold((width, 1536), BF), hold((768, width), BF),
            hold((1024, 512), BF), hold((1024, 384), F32), hold((1024, 256), BF), hold((2, 1024, 128), F32),
            hold((1024, 768), BF), hold((1024, 1536), BF),
            hold((BLOCK, width), F32), hold((BLOCK, width), F32), hold((BLOCK, width), BF),
            hold((1024, 256), F32), hold((1024, 512), BF),
            hold((4, 16, width), BF), hold((4, 16, width), BF), hold((3, 4, 16, width), BF),
            hold((4, 8, 16, 256), BF), hold((8, 4608), F32), hold((8, width), F32), hold((8, width), F32),
            hold((8, 256), F32), hold((1, 4352), F32), hold((7, 1, 4352), F32), hold((3, 1, 4352), F32),
            pltpu.SemaphoreType.DMA((SLOTS,)), pltpu.SemaphoreType.DMA((SLOTS,)),
        ],
        compiler_params=pltpu.CompilerParams(
            collective_id=0, has_side_effects=True, vmem_limit_bytes=VMEM_BYTES
        ),
        name="layer",
    )(x, prefix, wq, wk, wv, wo, wg, wu, wd, gains, cosine, sine, dy)


SLOTS = 640


def widen_kernel(*refs):
    narrow, wide = refs[:9], refs[9:18]
    held, turned, sems = refs[18:27], refs[27:34], refs[34]
    loads = [pltpu.make_async_copy(a, b, sems.at[i]) for i, (a, b) in enumerate(zip(narrow, held))]
    stores = [
        pltpu.make_async_copy(a, b, sems.at[9 + i])
        for i, (a, b) in enumerate(zip(turned + held[7:], wide))
    ]
    for copy in loads:
        copy.start()
    for load, store, a, b in zip(loads, stores, held, turned):
        load.wait()

        def body(i, carry):
            rows = rows_at(i * 32, 32)
            b[rows, :] = a[rows, :].astype(F32)
            return carry

        lax.fori_loop(0, a.shape[0] // 32, body, 0)
        store.start()
    for i in (7, 8):
        loads[i].wait()
        stores[i].start()
    for copy in stores:
        copy.wait()


def widen(narrow, same):
    place, shape, hold = pl.BlockSpec(memory_space=pltpu.HBM), jax.ShapeDtypeStruct, pltpu.VMEM
    return pl.pallas_call(
        widen_kernel,
        out_shape=tuple(shape(a.shape, F32) for a in narrow) + tuple(shape(a.shape, BF) for a in same),
        in_specs=[place] * 9,
        out_specs=(place,) * 9,
        scratch_shapes=[hold(a.shape, BF) for a in narrow + same]
        + [hold(a.shape, F32) for a in narrow]
        + [pltpu.SemaphoreType.DMA((18,))],
        compiler_params=pltpu.CompilerParams(vmem_limit_bytes=VMEM_BYTES),
        name="widen",
    )(*narrow, *same)


def rope_tables(length):
    freqs = ROPE_BASE ** (-(np.arange(HEAD_SIZE // 2, dtype=np.float32) * 2.0 / HEAD_SIZE))
    angles = np.arange(length, dtype=np.float32)[:, None] * freqs.astype(np.float32)[None, :]
    cosine, sine = np.cos(angles), np.sin(angles)
    return np.concatenate([cosine, cosine], 1), np.concatenate([-sine, sine], 1)


def with_kernel(layer_input, prefix, wq, wk, wv, wo, w_gate, w_up, w_down, gains, cotangent):
    cosine, sine = rope_tables(layer_input.shape[1] * 8)
    results = run_layer(
        layer_input[0], prefix, wq, wk, wv, wo, w_gate, w_up, w_down,
        jnp.pad(gains.reshape(1, 136), ((0, 15), (0, 120))),
        cosine, sine, cotangent[0],
    )
    output, x_grad, gain_sum = results[:3]
    first = (lax.axis_index("dp") * 8 + lax.axis_index("ctx")) * 136
    gains_grad = lax.dynamic_slice_in_dim(gain_sum[0], first, 136, 0)
    big_first = (8, 7, 9, 3, 6, 4, 5)
    final = widen([results[i] for i in big_first], [output, x_grad])
    wide = tuple(final[big_first.index(i)] for i in range(3, 10))
    return (final[7][None], final[8][None]) + wide + (gains_grad,)


def solution(mesh):
    tokens = P("dp", "ctx", None)
    matrix = P(("dp", "ctx"), None)
    vector = P(("dp", "ctx"))
    small = mesh.shape["dp"] == 4 and mesh.shape["ctx"] == 8
    return jax.shard_map(
        with_kernel if small else general,
        mesh=mesh,
        in_specs=(tokens, P("dp")) + (matrix,) * 7 + (vector, tokens),
        out_specs=(tokens, tokens) + (matrix,) * 7 + (vector,),
        check_vma=False,
    )
```

```python
import jax
import jax.numpy as jnp
import numpy as np
from jax import lax
from jax.experimental import pallas as pl
from jax.experimental.pallas import tpu as pltpu
from jax.sharding import PartitionSpec as P

QUERY_HEADS = 16
KEY_VALUE_HEADS = 8
HEAD_SIZE = 128
EPSILON = 1e-06
ROPE_BASE = 1000000.0
BF = jnp.bfloat16
F32 = jnp.float32


def rms_scale(value, gain):
    return value * lax.rsqrt(jnp.mean(value * value, -1, keepdims=True) + EPSILON) * gain


def rotate(value, cosine, sine):
    half = value.shape[-1] // 2
    first = value[..., :half]
    second = value[..., half:]
    return jnp.concatenate([first * cosine - second * sine, second * cosine + first * sine], -1)


def mm(left, right):
    return jnp.dot(left, right, preferred_element_type=F32)


def mm_tn(left, right):
    return lax.dot_general(left, right, (((0,), (0,)), ((), ())), preferred_element_type=F32)


def mm_nt(left, right):
    return lax.dot_general(left, right, (((1,), (1,)), ((), ())), preferred_element_type=F32)


def gated_unit(gate, up):
    return jax.nn.silu(gate) * up


def swap_ctx(pieces):
    return lax.all_to_all(pieces, "ctx", 0, 0)


def general(layer_input, prefix, wq, wk, wv, wo, w_gate, w_up, w_down, gains, cotangent):
    nd, nc = lax.axis_size("dp"), lax.axis_size("ctx")
    me = lax.axis_index("ctx")
    rows = layer_input.shape[1]
    seq = rows * nc
    depth, width = wq.shape[0], layer_input.shape[2]
    heads = QUERY_HEADS // nc
    copies = max(1, nc // KEY_VALUE_HEADS)
    kv_heads = max(1, KEY_VALUE_HEADS // nc)
    unit = w_down.shape[0]
    scale = HEAD_SIZE ** (-0.5)

    def columns_to(weight, parts):
        return jnp.moveaxis(weight.reshape(depth, parts, -1), 1, 0)

    def by_head(weight, repeat):
        parts = columns_to(weight, nc // repeat)
        return jnp.repeat(parts, repeat, 0) if repeat > 1 else parts

    def by_unit(weight):
        return jnp.transpose(weight.reshape(depth, nd, nc, unit), (2, 0, 1, 3)).reshape(
            nc, depth, nd * unit
        )

    def everywhere(array):
        return lax.all_gather(array, "dp", axis=0, tiled=True)

    qkv_piece = jnp.concatenate([by_head(wq, 1), by_head(wk, copies), by_head(wv, copies)], 2)
    w_qkv = everywhere(swap_ctx(qkv_piece).reshape(nc * depth, -1))
    plane = nc * wo.shape[0]
    span = QUERY_HEADS * HEAD_SIZE // nc
    need = span // wo.shape[0]
    by_plane = everywhere(wo).reshape(nd, wo.shape[0], width)
    wanted = jnp.stack([by_plane[i * span // plane] for i in range(nc)])
    arrived = swap_ctx(wanted)
    first_source = (me * span % plane) // wo.shape[0]
    w_o = lax.dynamic_slice_in_dim(arrived, first_source, need, 0).reshape(span, width)
    w_gu = everywhere(
        swap_ctx(jnp.concatenate([by_unit(w_gate), by_unit(w_up)], 2)).reshape(nc * depth, -1)
    )
    w_d = everywhere(w_down)
    gain_all = lax.all_gather(gains, ("dp", "ctx"), axis=0, tiled=True).astype(F32)
    gain_one = gain_all[:width]
    gain_two = gain_all[width : 2 * width]
    gain_q = gain_all[2 * width : 2 * width + HEAD_SIZE]
    gain_k = gain_all[2 * width + HEAD_SIZE :]

    def whole(array):
        return lax.all_gather(array, "ctx", axis=0, tiled=True)

    def own_sum(partial):
        return lax.psum_scatter(partial.astype(BF), "ctx", scatter_dimension=0, tiled=True).astype(
            F32
        )

    pos = jnp.arange(seq, dtype=jnp.int32)
    visible = (pos[None, :] <= pos[:, None]) | (pos[None, :] < prefix[0])
    freqs = ROPE_BASE ** (-(jnp.arange(HEAD_SIZE // 2, dtype=F32) * 2.0 / HEAD_SIZE))
    angles = pos.astype(F32)[:, None] * freqs[None, :]
    cosine = jnp.cos(angles)[:, None, :]
    sine = jnp.sin(angles)[:, None, :]

    def prepare_heads(raw, gain):
        return rotate(rms_scale(raw, gain), cosine, sine)

    inputs = layer_input[0].astype(F32)
    n1, back_one = jax.vjp(rms_scale, inputs, gain_one)
    n1_all = whole(n1.astype(BF))
    dy_all = whole(cotangent[0])
    qkv = mm(n1_all, w_qkv)
    q_raw = qkv[:, : heads * HEAD_SIZE].reshape(seq, heads, HEAD_SIZE)
    k_raw = qkv[:, heads * HEAD_SIZE : (heads + kv_heads) * HEAD_SIZE].reshape(
        seq, kv_heads, HEAD_SIZE
    )
    v = qkv[:, (heads + kv_heads) * HEAD_SIZE :].astype(BF).reshape(seq, kv_heads, HEAD_SIZE)
    q_rot, back_q = jax.vjp(prepare_heads, q_raw, gain_q)
    k_rot, back_k = jax.vjp(prepare_heads, k_raw, gain_k)
    q_rot = q_rot.astype(BF).reshape(seq, kv_heads, -1, HEAD_SIZE)
    k_rot = k_rot.astype(BF)
    scores = jnp.einsum("tkgd,skd->kgts", q_rot, k_rot, preferred_element_type=F32) * scale
    scores = jnp.where(visible[None, None], scores, -1e30)
    top = jnp.max(scores, -1, keepdims=True)
    expo = jnp.exp(scores - top)
    total = jnp.sum(expo, -1, keepdims=True)
    probs = expo / total
    probs_bf = probs.astype(BF)
    o = jnp.einsum("kgts,skd->tkgd", probs_bf, v, preferred_element_type=F32).astype(BF)
    o = o.reshape(seq, heads * HEAD_SIZE)
    hidden = inputs + own_sum(mm(o, w_o))
    n2, back_two = jax.vjp(rms_scale, hidden, gain_two)
    n2_all = whole(n2.astype(BF))
    gu = mm(n2_all, w_gu)
    gate, up = gu[:, : nd * unit], gu[:, nd * unit :]
    active, back_gated = jax.vjp(gated_unit, gate, up)
    active = active.astype(BF)
    output = (hidden + own_sum(mm(active, w_d))).astype(BF)
    def row_sum(term):
        return lax.psum_scatter(term.astype(BF), "dp", scatter_dimension=0, tiled=True)

    down_grad = row_sum(mm_tn(active, dy_all)).astype(F32)
    d_gate, d_up = back_gated(mm_nt(dy_all, w_d))
    d_gu = jnp.concatenate([d_gate.astype(BF), d_up.astype(BF)], 1)
    gu_sum = swap_ctx(row_sum(mm_tn(n2_all, d_gu)).reshape(nc, depth, -1)).astype(F32)
    gu_sum = gu_sum.reshape(nc, depth, 2, nd, unit)
    gu_sum = jnp.transpose(gu_sum, (2, 1, 3, 0, 4)).reshape(2, depth, -1)
    gate_grad, up_grad = gu_sum[0], gu_sum[1]
    upstream = cotangent[0].astype(F32)
    d_hidden_part, d_gain_two = back_two(own_sum(mm_nt(d_gu, w_gu)))
    d_hidden = upstream + d_hidden_part
    d_attn = whole(d_hidden.astype(BF))
    wo_term = mm_tn(o, d_attn).astype(BF).reshape(need, wo.shape[0], width)
    slots = jnp.zeros((nc, wo.shape[0], width), BF)
    slots = lax.dynamic_update_slice_in_dim(slots, wo_term, first_source, 0)
    back_home = swap_ctx(slots)
    mine = []
    for plane_index in range(nd):
        total_plane = 0
        for i in range(nc):
            if i * span // plane == plane_index:
                total_plane = total_plane + back_home[i].astype(F32)
        mine.append(total_plane)
    wo_grad = lax.psum_scatter(
        jnp.stack(mine).astype(BF), "dp", scatter_dimension=0, tiled=True
    )[0].astype(F32)
    d_o = mm_nt(d_attn, w_o).astype(BF).reshape(seq, kv_heads, -1, HEAD_SIZE)
    d_probs = jnp.einsum("tkgd,skd->kgts", d_o, v, preferred_element_type=F32)
    d_v = jnp.einsum("kgts,tkgd->skd", probs_bf, d_o, preferred_element_type=F32).astype(BF)
    d_scores = (probs * (d_probs - jnp.sum(d_probs * probs, -1, keepdims=True))).astype(BF)
    d_q = jnp.einsum("kgts,skd->tkgd", d_scores, k_rot, preferred_element_type=F32) * scale
    d_k = jnp.einsum("kgts,tkgd->skd", d_scores, q_rot, preferred_element_type=F32) * scale
    d_q, d_gain_q = back_q(d_q.reshape(seq, heads, HEAD_SIZE))
    d_k, d_gain_k = back_k(d_k)
    d_qkv = jnp.concatenate(
        [a.reshape(seq, -1).astype(BF) for a in (d_q, d_k, d_v)], 1
    )
    qkv_sum = swap_ctx(row_sum(mm_tn(n1_all, d_qkv)).reshape(nc, depth, -1)).astype(F32)
    at_k, at_v = heads * HEAD_SIZE, (heads + kv_heads) * HEAD_SIZE

    def columns_back(part, repeat):
        part = part.reshape(nc // repeat, repeat, depth, -1).sum(1)
        return jnp.moveaxis(part, 0, 1).reshape(depth, -1)

    wq_grad = columns_back(qkv_sum[:, :, :at_k], 1)
    wk_grad = columns_back(qkv_sum[:, :, at_k:at_v], copies)
    wv_grad = columns_back(qkv_sum[:, :, at_v:], copies)
    d_input_part, d_gain_one = back_one(own_sum(mm_nt(d_qkv, w_qkv)))
    x_grad = (d_hidden + d_input_part).astype(BF)
    gain_term = jnp.concatenate([d_gain_one, d_gain_two, d_gain_q, d_gain_k])
    gains_grad = lax.psum_scatter(gain_term, ("dp", "ctx"), scatter_dimension=0, tiled=True)
    return (
        output[None], x_grad[None], wq_grad, wk_grad, wv_grad, wo_grad,
        gate_grad, up_grad, down_grad, gains_grad,
    )


MESH = pl.DeviceIdType.MESH
BLOCK = 128
VMEM_BYTES = 64 << 20


class Copies:
    def __init__(self, sends, receives):
        self.sends, self.receives = sends, receives
        self.used = 0

    def take(self, count=1):
        first = self.used
        self.used += count
        if self.used > SLOTS:
            raise ValueError("more semaphores")
        return first

    def to(self, src, dst, device, slot, receive_slot=None):
        receive_slot = slot if receive_slot is None else receive_slot
        return pltpu.make_async_remote_copy(
            src_ref=src,
            dst_ref=dst,
            send_sem=self.sends.at[slot],
            recv_sem=self.receives.at[receive_slot],
            device_id=device,
            device_id_type=MESH,
        )

    def here(self, src, dst, slot):
        return pltpu.make_async_copy(src, dst, self.sends.at[slot])


class Place:
    def __init__(self):
        self.d = lax.axis_index("dp")
        self.c = lax.axis_index("ctx")
        self.z = self.c // 2
        self.p = lax.rem(self.c, 2)

    def at(self, d, c):
        return (d, c)


def meet():
    barrier = pltpu.get_barrier_semaphore()
    d, c = lax.axis_index("dp"), lax.axis_index("ctx")
    partners = [(d, c ^ rel) for rel in range(1, 8)]
    partners += [(d ^ rel, c ^ twin) for rel in range(1, 4) for twin in range(2)]
    for partner in partners:
        pl.semaphore_signal(barrier, inc=1, device_id=partner, device_id_type=MESH)
    pl.semaphore_wait(barrier, len(partners))


def when(condition, then):
    if isinstance(condition, bool):
        if condition:
            then()
    else:
        pl.when(condition)(then)


def rows_at(start, size):
    return pl.ds(pl.multiple_of(start, 16), size)


class Gather:
    def __init__(self, copies, place, buf, parts=2, after=None):
        self.k, self.g, self.buf, self.parts = copies, place, buf, parts
        self.size = BLOCK // parts
        if after is None:
            self.right = copies.take(3 * parts)
            self.left = copies.take(3 * parts)
            self.twin = copies.take(7 * parts)
        else:
            self.right, self.left, self.twin = after.right, after.left, after.twin

    def piece(self, z, p, part):
        return self.buf.at[rows_at((2 * z + p) * BLOCK + part * self.size, self.size)]

    def line(self, step, part, rightwards):
        g = self.g
        z = g.z - step if rightwards else g.z + step
        slot = (self.right if rightwards else self.left) + step * self.parts + part
        piece = self.piece(z, g.p, part)
        to = g.c + 2 if rightwards else g.c - 2
        return self.k.to(piece, piece, (g.d, to), slot)

    def wait_line(self, step, part, rightwards):
        piece = self.piece(self.g.z, self.g.p, part)
        slot = (self.right if rightwards else self.left) + step * self.parts + part
        self.k.to(piece, piece, (self.g.d, self.g.c ^ 1), slot).wait_recv()

    def twins(self, order, z, part):
        piece = self.piece(z, self.g.p, part)
        return self.k.to(piece, piece, (self.g.d, self.g.c ^ 1), self.twin + order * self.parts + part)

    def can_send(self, step, rightwards):
        z = self.g.z
        return (z >= step) & (z < 3) if rightwards else (z + step <= 3) & (z > 0)

    def gets(self, step, rightwards):
        z = self.g.z
        return z >= step + 1 if rightwards else z + step + 1 <= 3

    def start(self):
        for part in range(self.parts):
            self.start_part(part)

    def start_part(self, part):
        for rightwards in (True, False):

            @pl.when(self.can_send(0, rightwards))
            def _():
                self.line(0, part, rightwards).start()

        self.twins(0, self.g.z, part).start()

    def start_line(self, right, left):
        for part in range(self.parts):
            for now, rightwards in ((right, True), (left, False)):

                @pl.when(now & self.can_send(0, rightwards))
                def _():
                    self.line(0, part, rightwards).start()

    def start_twin(self):
        for part in range(self.parts):
            self.twins(0, self.g.z, part).start()

    def step(self, step):
        for part in range(self.parts):
            self.step_part(step, part)

    def step_part(self, step, part):
        for side, rightwards in enumerate((True, False)):
            z = self.g.z - 1 - step if rightwards else self.g.z + 1 + step

            @pl.when(self.gets(step, rightwards))
            def _():
                self.wait_line(step, part, rightwards)

                def on():
                    @pl.when(self.can_send(step + 1, rightwards))
                    def _():
                        self.line(step + 1, part, rightwards).start()

                when(step < 2, on)
                self.twins(1 + 2 * step + side, z, part).start()

    def twin_own(self):
        for part in range(self.parts):
            self.twins(0, self.g.z, part).wait_recv()

    def twin_step(self, step):
        for part in range(self.parts):
            for side, rightwards in enumerate((True, False)):

                @pl.when(self.gets(step, rightwards))
                def _():
                    self.twins(1 + 2 * step + side, self.g.z, part).wait_recv()

    def drain(self):
        for part in range(self.parts):
            self.twins(0, self.g.z, part).wait_send()
            for step in range(3):
                for side, rightwards in enumerate((True, False)):

                    @pl.when(self.can_send(step, rightwards))
                    def _():
                        self.line(step, part, rightwards).wait_send()

                    @pl.when(self.gets(step, rightwards))
                    def _():
                        self.twins(1 + 2 * step + side, self.g.z, part).wait_send()


def add_rows(dst, dst_row, a, a_row, b, b_row, count):
    def body(i, carry):
        at = i * 32
        total = a[rows_at(a_row + at, 32), :].astype(F32) + b[rows_at(b_row + at, 32), :].astype(F32)
        dst[rows_at(dst_row + at, 32), :] = total.astype(dst.dtype)
        return carry

    lax.fori_loop(0, count // 32, body, 0)


class Scatter:
    def __init__(self, copies, place, partial, from_twin, from_left, from_right, parts=2, after=None):
        self.k, self.g = copies, place
        self.partial, self.from_twin = partial, from_twin
        self.from_line = {True: from_left, False: from_right}
        self.parts, self.size = parts, BLOCK // parts
        if after is None:
            self.twin = copies.take(4)
            self.slots = {True: copies.take(3 * parts), False: copies.take(3 * parts)}
        else:
            self.twin, self.slots = after.twin, after.slots

    def row(self, z, p):
        return (2 * z + p) * BLOCK

    def twins(self, z, slot):
        g = self.g
        src = self.partial.at[rows_at(self.row(z, 1 - g.p), BLOCK)]
        dst = self.from_twin.at[rows_at(z * BLOCK, BLOCK)]
        return self.k.to(src, dst, (g.d, g.c ^ 1), self.twin + slot)

    def send_twin(self, z):
        self.twins(z, z).start()

    def take_twin(self, z):
        self.twins(z, z).wait_recv()
        at = self.row(z, self.g.p)
        add_rows(self.partial, at, self.partial, at, self.from_twin, z * BLOCK, BLOCK)

    def target(self, step, rightwards):
        return self.g.z + 3 - step if rightwards else self.g.z - 3 + step

    def can_send(self, step, rightwards):
        z = self.g.z
        return z <= step if rightwards else 3 - z <= step

    def gets(self, step, rightwards):
        z = self.g.z
        return (z >= 1) & (z - 1 <= step) if rightwards else (z <= 2) & (2 - z <= step)

    def line(self, step, rightwards, part):
        g = self.g
        at = self.row(self.target(step, rightwards), g.p) + part * self.size
        src = self.partial.at[rows_at(at, self.size)]
        dst = self.from_line[rightwards].at[rows_at(step * BLOCK + part * self.size, self.size)]
        slot = self.slots[rightwards] + step * self.parts + part
        return self.k.to(src, dst, (g.d, g.c + 2 if rightwards else g.c - 2), slot)

    def wait_line(self, step, rightwards, part):
        src = self.partial.at[pl.ds(0, self.size)]
        dst = self.from_line[rightwards].at[rows_at(step * BLOCK + part * self.size, self.size)]
        slot = self.slots[rightwards] + step * self.parts + part
        self.k.to(src, dst, (self.g.d, self.g.c ^ 1), slot).wait_recv()

    def send(self, step, part):
        for rightwards in (True, False):

            @pl.when(self.can_send(step, rightwards))
            def _():
                self.line(step, rightwards, part).start()

    def start(self):
        for part in range(self.parts):
            self.send(0, part)

    def advance(self, step):
        for part in range(self.parts):
            for rightwards in (True, False):

                @pl.when(self.gets(step, rightwards))
                def _():
                    self.wait_line(step, rightwards, part)

                    def add():
                        z = self.g.z + 2 - step if rightwards else self.g.z - 2 + step
                        at = self.row(z, self.g.p) + part * self.size
                        add_rows(
                            self.partial, at, self.partial, at, self.from_line[rightwards],
                            step * BLOCK + part * self.size, self.size,
                        )

                    when(step < 2, add)

            when(step < 2, lambda: self.send(step + 1, part))

    def finish(self, done, slot=2, part=None):
        g = self.g
        own = self.row(g.z, g.p)
        first, count = (0, BLOCK) if part is None else (part * self.size, self.size)

        def body(i, carry):
            at = first + i * 16
            total = self.partial[rows_at(own + at, 16), :].astype(F32)
            a = self.from_line[True][rows_at(slot * BLOCK + at, 16), :].astype(F32)
            b = self.from_line[False][rows_at(slot * BLOCK + at, 16), :].astype(F32)
            total = total + jnp.where(g.z >= 1, a, 0.0) + jnp.where(g.z <= 2, b, 0.0)
            done(at, total)
            return carry

        lax.fori_loop(0, count // 16, body, 0)

    def send_ends(self, part, *steps):
        for rightwards in (True, False):

            @pl.when(self.g.z == (0 if rightwards else 3))
            def _():
                for step in steps:
                    self.line(step, rightwards, part).start()

    def relay(self, step, part):
        for rightwards in (True, False):

            @pl.when(self.gets(step, rightwards))
            def _():
                self.wait_line(step, rightwards, part)
                z = self.g.z + 2 - step if rightwards else self.g.z - 2 + step
                at = self.row(z, self.g.p) + part * self.size
                add_rows(
                    self.partial, at, self.partial, at, self.from_line[rightwards],
                    step * BLOCK + part * self.size, self.size,
                )
                self.line(step + 1, rightwards, part).start()

    def last(self, done, part):
        for rightwards in (True, False):

            @pl.when(self.gets(2, rightwards))
            def _():
                self.wait_line(2, rightwards, part)

        self.finish(done, part=part)

    def drain(self):
        for z in range(4):
            self.twins(z, z).wait_send()
        for step in range(3):
            for part in range(self.parts):
                for rightwards in (True, False):

                    @pl.when(self.can_send(step, rightwards))
                    def _():
                        self.line(step, rightwards, part).wait_send()


class Spread:
    def __init__(self, copies, place, piece):
        self.k, self.g, self.piece = copies, place, piece
        self.slots = copies.take(6)

    def direct(self, half, rel):
        g = self.g
        piece = self.piece(g.d, half)
        return self.k.to(piece, piece, (g.d ^ rel, g.c), self.slots + 2 * (rel - 1) + half)

    def passed(self, rel):
        g = self.g
        piece = self.piece(g.d ^ (3 - rel), rel - 1)
        return self.k.to(piece, piece, (g.d ^ rel, g.c), self.slots + 4 + rel - 1)

    def start(self):
        for half, rel in ((0, 1), (1, 2), (1, 1), (0, 2)):
            self.direct(half, rel).start()

    def forward(self):
        self.direct(1, 1).wait_recv()
        self.passed(2).start()
        self.direct(0, 2).wait_recv()
        self.passed(1).start()

    def finish(self):
        self.direct(0, 1).wait_recv()
        self.direct(1, 2).wait_recv()
        self.passed(1).wait_recv()
        self.passed(2).wait_recv()

    def drain(self):
        for half, rel in ((0, 1), (1, 2), (1, 1), (0, 2)):
            self.direct(half, rel).wait_send()
        self.passed(1).wait_send()
        self.passed(2).wait_send()


class Direct:
    def __init__(self, copies, place, piece):
        self.k, self.g, self.piece = copies, place, piece
        self.slots = copies.take(3)

    def copy(self, rel):
        piece = self.piece(self.g.d)
        return self.k.to(piece, piece, (self.g.d ^ rel, self.g.c), self.slots + rel - 1)

    def start(self):
        for rel in (1, 2, 3):
            self.copy(rel).start()

    def finish(self):
        for rel in (1, 2, 3):
            self.copy(rel).wait_recv()

    def drain(self):
        for rel in (1, 2, 3):
            self.copy(rel).wait_send()


class Fold:
    def __init__(self, copies, place, piece, got, stage):
        self.k, self.g, self.piece, self.got, self.stage = copies, place, piece, got, stage
        self.slots = copies.take(6)
        self.loads = copies.take(6)

    def first(self, half, passed):
        g = self.g
        rel = 1 + half
        src = self.piece(g.d ^ (3 if passed else rel), half)
        i = 2 * half + passed
        return self.k.to(src, self.got(i), (g.d ^ rel, g.c), self.slots + i)

    def second(self, half):
        g = self.g
        rel = 2 - half
        return self.k.to(
            self.piece(g.d ^ rel, half), self.got(4 + half), (g.d ^ rel, g.c), self.slots + 4 + half
        )

    def load(self, i):
        return self.k.here(self.got(i), self.stage(i), self.loads + i)

    def start(self):
        for passed in (1, 0):
            for half in range(2):
                self.first(half, passed).start()

    def middle(self, add):
        for half in range(2):
            self.first(half, 1).wait_recv()
            self.load(2 * half + 1).start()
        for half in range(2):
            self.load(2 * half + 1).wait()
            add(self.piece(self.g.d ^ (2 - half), half), (self.stage(2 * half + 1),))
            self.second(half).start()

    def final(self, add):
        for half in range(2):
            self.first(half, 0).wait_recv()
            self.load(2 * half).start()
        for half in range(2):
            self.second(half).wait_recv()
            self.load(4 + half).start()
        for half in range(2):
            self.load(2 * half).wait()
            self.load(4 + half).wait()
            add(self.piece(self.g.d, half), (self.stage(2 * half), self.stage(4 + half)))

    def drain(self):
        for half in range(2):
            for passed in range(2):
                self.first(half, passed).wait_send()
            self.second(half).wait_send()


def down_to_units(place, copies, src, dst):
    g, p, d = place, place.p, place.d
    send, receive = copies.take(8), copies.take(12)
    odd = lax.rem(d, 2)
    wide = (src.at[rows_at(p * 64, 128)], dst.at[rows_at(wide_row(p, d), 128)])
    thin = (src.at[rows_at((1 - p) * 128, 64)], dst.at[rows_at(thin_row(d, p), 64)])
    stays = odd == p

    def thin_to(rel, core):
        return copies.to(
            *thin, (d ^ rel, 2 * g.z + odd), send + 4 + rel, receive + 4 + 2 * rel + core
        )

    def start_thin():
        for rel in (1, 2, 3):
            thin_to(rel, p).start()

        @pl.when(stays)
        def _():
            copies.here(*thin, send + 4).start()

        @pl.when(jnp.logical_not(stays))
        def _():
            thin_to(0, p).start()

    copies.here(*wide, send).start()
    spread = Spread(
        copies, g, lambda e, half: dst.at[rows_at(wide_row(p, e) + half * 64, 64)]
    )

    def start_wide():
        copies.here(*wide, send).wait()
        spread.start()

    def finish():
        spread.finish()

        @pl.when(stays)
        def _():
            copies.here(*thin, send + 4).wait()

        @pl.when(jnp.logical_not(stays))
        def _():
            thin_to(0, p).wait_send()

        for rel in (1, 2, 3):
            thin_to(rel, p).wait_send()
        for rel in range(4):

            @pl.when(lax.rem(d ^ rel, 2) == p)
            def _():
                if rel:
                    thin_to(rel, p).wait_recv()
                thin_to(rel, 1 - p).wait_recv()

    return start_thin, start_wide, spread, finish


def unit_row(core, plane):
    return (plane // 2) * 384 + (lax.rem(plane, 2) ^ core) * 256


def wide_row(core, plane):
    return unit_row(core, plane) + core * lax.rem(plane, 2) * 128


def thin_row(plane, core):
    odd = lax.rem(plane, 2)
    return unit_row(odd, plane) + (1 - odd) * 128 + core * 64


def down_to_owners(place, copies, src, dst):
    g, p, d = place, place.p, place.d
    send, receive = copies.take(12), copies.take(8)

    def wide(rel):
        plane = d ^ rel
        a = src.at[rows_at(wide_row(p, plane), 128)]
        b = dst.at[rel, rows_at(p * 64, 128)]
        if rel == 0:
            return copies.here(a, b, send)
        return copies.to(a, b, (plane, g.c), send + rel, receive + rel)

    def thin(rel, core):
        plane = d ^ rel
        a = src.at[rows_at(thin_row(plane, core), 64)]
        b = dst.at[rel, rows_at((1 - core) * 128, 64)]
        return copies.to(
            a, b, (plane, 2 * g.z + core), send + 4 + 2 * rel + core, receive + 4 + rel
        )

    def thin_own():
        a = src.at[rows_at(thin_row(d, p), 64)]
        return copies.here(a, dst.at[0, rows_at((1 - p) * 128, 64)], send + 4 + p)

    def holds(rel):
        return lax.rem(d ^ rel, 2) == p

    def start_wide():
        for rel in (1, 2, 3, 0):
            wide(rel).start()

    def start_thin():
        for rel in (1, 2, 3, 0):

            @pl.when(holds(rel))
            def _():
                if rel:
                    thin(rel, p).start()
                else:
                    thin_own().start()
                thin(rel, 1 - p).start()

    def finish():
        wide(0).wait()
        for rel in (1, 2, 3):
            wide(rel).wait()
        for rel in range(4):

            @pl.when(holds(rel))
            def _():
                if rel:
                    thin(rel, p).wait_send()
                else:
                    thin_own().wait()
                thin(rel, 1 - p).wait_send()

        @pl.when(jnp.logical_not(holds(0)))
        def _():
            thin(0, p).wait_recv()

        for rel in (1, 2, 3):
            thin(rel, p).wait_recv()

    return start_wide, start_thin, finish


UNIT_PARTS = ((0, 256), (256, 128), (384, 256), (640, 128))


def unit_column(j, z, core):
    plane = 2 * (j // 2) + (core if j % 2 == 0 else 1 - core)
    return plane * 1536 + z * 384 + core * (128 if j % 2 == 0 else 256)


def lanes(start, size):
    return pl.ds(pl.multiple_of(start, 128), size)


def nt(left, right):
    return lax.dot_general(left, right, (((1,), (1,)), ((), ())), preferred_element_type=F32)


def tn(left, right):
    return lax.dot_general(left, right, (((0,), (0,)), ((), ())), preferred_element_type=F32)


def layer_kernel(
    x, prefix, wq, wk, wv, wo, wg, wu, wd, gains, cosine, sine, dy,
    output, x_grad, gain_out, out_q, out_k, out_v, out_o, out_g, out_u, out_d,
    n1_kept, got_gu, got_d, got_qkv,
    xs, n1, ys, partial, partial2, from_twin, from_left, from_right, from_twin2, from_left2, from_right2,
    w_qkv, w_o, w_gu, w_d, qkv, raw, o, lse, act, d_gu, hidden, d_hidden, x_own, d_kv, d_qkv,
    wo_mid, wo_back, got_o, gain_buf, gain_acc, gain_one, gain_two, gain_qk, gain_vec, gain_ctx, gain_dp,
    sends, receives,
):
    g = Place()
    k = Copies(sends, receives)
    d, c, z, p = g.d, g.c, g.z, g.p
    meet()
    own = rows_at(c * BLOCK, BLOCK)
    shard = rows_at(d * 512, 512)
    mine = rows_at(d * 512 + c * 64, 64)

    gain_buf[d, c] = gains[...]
    gain_slots = k.take(12)

    def gain_over_ctx(rel):
        return k.to(gain_buf.at[d, c], gain_buf.at[d, c], (d, c ^ rel), gain_slots + rel)

    def gain_over_dp(rel):
        return k.to(gain_buf.at[d], gain_buf.at[d], (d ^ rel, c), gain_slots + 8 + rel)

    for rel in range(1, 8):
        gain_over_ctx(rel).start()

    own_slots = k.take(3)
    own_copies = [
        k.here(x, xs.at[own], own_slots),
        k.here(x, x_own, own_slots + 1),
        k.here(dy, ys.at[own], own_slots + 2),
    ]
    for copy in own_copies:
        copy.start()

    qkv_slots = k.take(24)

    def qkv_to(rel, j):
        other = c ^ rel
        width = 256 if j == 0 else 128
        src = (wq, wk, wv)[j].at[:, lanes(other * width, width)]
        dst = w_qkv.at[mine, pl.ds((0, 256, 384)[j], width)]
        slot = qkv_slots + 3 * rel + j
        return k.to(src, dst, (d, other), slot) if rel else k.here(src, dst, slot)

    for rel in range(8):
        for j in range(3):
            qkv_to(rel, j).start()
    own_copies[0].wait()
    tokens = Gather(k, g, xs)
    tokens.start()
    at_end = (z == 0) | (z == 3)
    gu_slots = k.take(64)

    def gu_to(which, rel, j):
        place, count = UNIT_PARTS[j]
        column = unit_column(j, z ^ (rel // 2), p ^ (rel % 2))
        src = (wg, wu)[which].at[:, lanes(column, count)]
        dst = w_gu.at[mine, pl.ds(which * 768 + place, count)]
        slot = gu_slots + which * 32 + rel * 4 + j
        return k.to(src, dst, (d, c ^ rel), slot) if rel else k.here(src, dst, slot)

    def gu_start(*groups):
        for which in range(2):
            for group in groups:
                for rel in (2 * group, 2 * group + 1):
                    for j in range(4):
                        gu_to(which, rel, j).start()

    @pl.when(at_end)
    def _():
        gu_start(1)


    wo_slots = k.take(20)
    far = c // 4

    def wo_over_dp(rel):
        src, dst = wo.at[rows_at((d ^ rel) * 16, 16)], wo_mid.at[d]
        slot = wo_slots + rel
        return k.to(src, dst, (d ^ rel, c), slot) if rel else k.here(src, dst, slot)

    def wo_over_ctx(rel):
        src, dst = wo_mid.at[z ^ rel], w_o.at[lax.rem(c, 4), rows_at(d * 16, 16)]
        return k.to(
            src, dst, (d, 2 * (z ^ rel) + far), wo_slots + 4 + rel, wo_slots + 8 + lax.rem(c, 4)
        )

    def wo_stay():
        return k.here(
            wo_mid.at[z], w_o.at[lax.rem(c, 4), rows_at(d * 16, 16)], wo_slots + 4
        )

    wo_stays = far == p
    for rel in range(4):
        wo_over_dp(rel).start()

    start_thin, start_wide, spread_wide, finish_down = down_to_units(g, k, wd, w_d)

    for rel in range(1, 8):
        gain_over_ctx(rel).wait_recv()
    for rel in range(1, 4):
        gain_over_dp(rel).start()
    start_thin()
    for rel in range(1, 4):
        gain_over_dp(rel).wait_recv()
    gain_acc[...] = jnp.zeros_like(gain_acc)
    for i in range(32):
        row = gain_buf[i // 8, i % 8][0:8, :].astype(F32)
        row = jnp.concatenate([row, jnp.zeros((8, 128), F32)], 1)
        shift = (8 * i) % 128
        if shift:
            row = pltpu.roll(row, shift, 1)
        first = 136 * i - shift
        gain_acc[:, first : first + 384] += row

    def normalize(block):
        def body(i, carry):
            at = rows_at(block * BLOCK + i * 16, 16)
            v = xs[at, :].astype(F32)
            r = lax.rsqrt(jnp.mean(v * v, -1, keepdims=True) + EPSILON)
            n1[at, :] = (v * r * gain_acc[0:1, 0:2048]).astype(BF)
            return carry

        lax.fori_loop(0, BLOCK // 16, body, 0)

    normalize(c)
    for j in range(3):
        qkv_to(0, j).wait()
        for rel in range(1, 8):
            qkv_to(rel, j).wait_recv()
    spread_qkv = Spread(k, g, lambda e, half: w_qkv.at[rows_at(e * 512 + half * 256, 256)])
    spread_qkv.start()
    tokens.twin_own()
    normalize(c ^ 1)

    def each_side(step, use):
        def side(i, carry):
            chip = jnp.where(i == 0, z - 1 - step, z + 1 + step)

            @pl.when((chip >= 0) & (chip <= 3))
            def _():
                use(chip)

            return carry

        lax.fori_loop(0, 2, side, 0)

    def normalize_chip(chip):
        normalize(2 * chip)
        normalize(2 * chip + 1)

    gain_q, gain_k = gain_acc[0:1, 4096:4224], gain_acc[0:1, 4224:4352]

    def rotated(value, gain, at):
        r = lax.rsqrt(jnp.mean(value * value, -1, keepdims=True) + EPSILON)
        value = value * r * gain
        return value * cosine[at, :] + pltpu.roll(value, 64, 1) * sine[at, :]

    def project(chip):
        at = rows_at(chip * 256, 256)
        product = jnp.dot(n1[at, :], w_qkv[...], preferred_element_type=F32)
        raw[at, :] = product[:, :384]
        for j, gain in ((0, gain_q), (1, gain_q), (2, gain_k)):
            qkv[at, j * 128 : j * 128 + 128] = rotated(
                product[:, j * 128 : j * 128 + 128], gain, at
            ).astype(BF)
        qkv[at, 384:512] = product[:, 384:].astype(BF)

    def project_all(first, last):
        def body(i, carry):
            step = first + i // 2
            chip = jnp.where(lax.rem(i, 2) == 0, z - 1 - step, z + 1 + step)

            @pl.when((chip >= 0) & (chip <= 3) & ((step >= 0) | (lax.rem(i, 2) == 0)))
            def _():
                project(chip)

            return carry

        lax.fori_loop(0, 2 * (last - first), body, 0)

    tokens.step(0)

    @pl.when(jnp.logical_not(at_end))
    def _():
        gu_start(3)

    for rel in range(4):
        if rel == 0:
            wo_over_dp(0).wait()
        else:
            wo_over_dp(rel).wait_recv()
    for rel in range(1, 4):
        wo_over_ctx(rel).start()

    @pl.when(wo_stays)
    def _():
        wo_stay().start()

    @pl.when(jnp.logical_not(wo_stays))
    def _():
        wo_over_ctx(0).start()

    tokens.twin_step(0)
    each_side(0, normalize_chip)
    tokens.step(1)
    own_copies[2].wait()
    upstream = Gather(k, g, ys)
    upstream.start_line(z == 2, z == 1)
    spread_qkv.forward()
    tokens.twin_step(1)
    each_side(1, normalize_chip)
    for i in range(4):

        @pl.when(jnp.logical_not(c == 4 * p + i))
        def _():
            src, dst = wo_mid.at[0], w_o.at[0, rows_at(0, 16)]
            k.to(src, dst, (d, c ^ 1), wo_slots + 4, wo_slots + 8 + i).wait_recv()

    @pl.when(wo_stays)
    def _():
        wo_stay().wait()

    spread_o = Direct(k, g, lambda e: w_o.at[:, rows_at(e * 16, 16)])
    spread_o.start()
    start_wide()
    spread_qkv.finish()
    project_all(-1, 1)
    tokens.step(2)
    tokens.twin_step(2)
    each_side(2, normalize_chip)

    def gu_take(which):
        for rel in range(8):
            for j in range(4):
                if rel == 0:
                    gu_to(which, rel, j).wait()
                else:
                    gu_to(which, rel, j).wait_recv()

    @pl.when(at_end)
    def _():
        gu_start(0, 2, 3)

    project_all(1, 3)
    keep_slots = k.take(2)
    keep = k.here(n1, n1_kept, keep_slots)
    keep.start()

    limit = prefix[0]
    scale = HEAD_SIZE**-0.5

    def head_scores(head, at, first_row):
        scores = nt(qkv[at, head * 128 : head * 128 + 128], qkv[:, 256:384]) * scale
        row = first_row + lax.broadcasted_iota(jnp.int32, (256, 1), 0)
        column = lax.broadcasted_iota(jnp.int32, (1, 1024), 1)
        return jnp.where(column < jnp.maximum(row + 1, limit), scores, -1e30)

    def attend(head):
        def body(i, carry):
            at = rows_at(i * 256, 256)
            scores = head_scores(head, at, i * 256)
            top = jnp.max(scores, -1, keepdims=True)
            expo = jnp.exp(scores - top)
            total = jnp.sum(expo, -1, keepdims=True)
            probs = (expo * (1.0 / total)).astype(BF)
            value = jnp.dot(probs, qkv[:, 384:512], preferred_element_type=F32)
            o[at, head * 128 : head * 128 + 128] = value.astype(BF)
            lse[head, at, :] = jnp.broadcast_to(top + jnp.log(total), (256, 128))
            return carry

        lax.fori_loop(0, 4, body, 0)

    attend(0)
    attend(1)

    @pl.when(jnp.logical_not(at_end))
    def _():
        gu_start(0, 1, 2)

    spread_wide.forward()
    tokens.drain()
    spread_o.finish()
    sum_one = Scatter(k, g, partial, from_twin, from_left, from_right)
    for chip in (3, 0, 2, 1):

        def columns(j, carry):
            cols = lanes(j * 512, 512)
            rows = pl.ds(chip * 256, 256)
            value = jnp.dot(
                o[rows, :], w_o[:, :, cols].reshape(256, 512), preferred_element_type=F32
            )
            partial[rows, cols] = value.astype(BF)
            return carry

        lax.fori_loop(0, 4, columns, 0)
        sum_one.send_twin(chip)
    d_hidden[...] = ys[own, :].astype(F32)

    def upstream_goes(step):
        upstream.start_line((step == z) & (z < 2), (step == 3 - z) & (z > 1))


    sum_one.take_twin(3)
    sum_one.take_twin(0)
    sum_one.send_ends(0, 0)
    sum_one.take_twin(2)
    sum_one.take_twin(1)
    sum_one.send_ends(0, 1, 2)
    sum_one.send_ends(1, 0, 1, 2)
    gu_take(0)
    spread_gate = Spread(
        k, g, lambda e, half: w_gu.at[rows_at(e * 512 + half * 256, 256), pl.ds(0, 768)]
    )
    spread_gate.start()
    sum_one.relay(0, 0)
    gu_take(1)
    spread_up = Spread(
        k, g, lambda e, half: w_gu.at[rows_at(e * 512 + half * 256, 256), pl.ds(768, 768)]
    )
    spread_up.start()
    sum_one.relay(1, 0)
    own_copies[1].wait()

    def done_one(at, value):
        rows = rows_at(at, 16)
        h = x_own[rows, :].astype(F32) + value
        r = lax.rsqrt(jnp.mean(h * h, -1, keepdims=True) + EPSILON)
        hidden[rows, :] = h
        xs[rows_at(c * BLOCK + at, 16), :] = (h * r * gain_acc[0:1, 2048:4096]).astype(BF)

    seconds = Gather(k, g, xs, after=tokens)
    sum_one.last(done_one, 0)
    seconds.start_part(0)
    sum_one.relay(0, 1)
    spread_gate.forward()
    sum_one.relay(1, 1)
    seconds.step_part(0, 0)
    sum_one.last(done_one, 1)
    seconds.start_part(1)
    spread_up.forward()
    upstream_goes(0)
    upstream.start_twin()
    seconds.step_part(1, 0)
    seconds.step_part(0, 1)
    upstream_goes(1)
    spread_gate.finish()
    finish_down()
    sum_one.drain()
    keep.wait()
    spread_up.finish()
    sum_two = Scatter(k, g, partial2, from_twin, from_left, from_right, after=sum_one)
    sum_out = Scatter(k, g, partial, from_twin2, from_left2, from_right2, parts=1)

    def feed_forward(chip):
        at = rows_at(chip * 256, 256)

        def units(j, carry):
            cols, up_cols = lanes(j * 256, 256), lanes(768 + j * 256, 256)
            gate = jnp.dot(xs[at, :], w_gu[:, cols], preferred_element_type=F32)
            up = jnp.dot(xs[at, :], w_gu[:, up_cols], preferred_element_type=F32)
            act[at, cols] = (gate * up * (1.0 / (1.0 + jnp.exp(-gate)))).astype(BF)
            d_gu[at, cols] = gate.astype(BF)
            d_gu[at, up_cols] = up.astype(BF)
            return carry

        lax.fori_loop(0, 3, units, 0)

        def columns(j, carry):
            cols = lanes(j * 512, 512)
            partial[at, cols] = jnp.dot(
                act[at, :], w_d[:, cols], preferred_element_type=F32
            ).astype(BF)
            return carry

        lax.fori_loop(0, 4, columns, 0)
        sum_out.send_twin(chip)

    def feed_back(chip):
        at = rows_at(chip * 256, 256)

        def units(j, carry):
            cols, up_cols = lanes(j * 256, 256), lanes(768 + j * 256, 256)
            d_act = nt(ys[at, :], w_d[rows_at(j * 256, 256), :])
            gate, up = d_gu[at, cols].astype(F32), d_gu[at, up_cols].astype(F32)
            sig = 1.0 / (1.0 + jnp.exp(-gate))
            d_gu[at, cols] = (d_act * up * sig * (1.0 + gate * (1.0 - sig))).astype(BF)
            d_gu[at, up_cols] = (d_act * gate * sig).astype(BF)
            return carry

        lax.fori_loop(0, 3, units, 0)

        def columns(j, carry):
            rows = rows_at(j * 512, 512)
            partial2[at, lanes(j * 512, 512)] = nt(d_gu[at, :], w_gu[rows, :]).astype(BF)
            return carry

        lax.fori_loop(0, 4, columns, 0)
        sum_two.send_twin(chip)

    def visit(gather, use, between=None, taken=(0, 0), used=None):
        inner = jnp.where(z <= 1, 1, -1)

        def body(step, carry):
            @pl.when(step == 0)
            def _():
                gather.twin_own()

            @pl.when(step > 0)
            @jax.named_scope("twin")
            def _():
                gather.twin_step(step - 1)

            def side(i, carry):
                chip = jnp.where(i == 0, z + inner * step, z - inner * step)

                @pl.when((chip >= 0) & (chip <= 3) & ((i == 0) | (step > 0)))
                @jax.named_scope("use")
                def _():
                    use(chip)

                if used is not None:

                    @pl.when(i == 0)
                    def _():
                        used(step)

                for part in range(gather.parts):

                    @pl.when((i == 0) & (step >= taken[part]) & (step < 3))
                    @jax.named_scope("arrive")
                    def _():
                        gather.step_part(step, part)

                if between is not None:

                    @pl.when(i == 0)
                    @jax.named_scope("between")
                    def _():
                        between(step)

                return carry

            lax.fori_loop(0, 2, side, 0)
            return carry

        lax.fori_loop(0, 4, body, 0)

    def upstream_passes(step):
        @pl.when(step == 1)
        def _():
            upstream_goes(2)

        @pl.when((step == 2) & jnp.logical_not(at_end))
        def _():
            upstream.step(0)

    visit(seconds, feed_forward, taken=(2, 1), between=upstream_passes)

    @pl.when(at_end)
    def _():
        upstream.step(0)

    for i in (3, 0):
        sum_out.take_twin(i)
    sum_out.start()
    for i in (2, 1):
        sum_out.take_twin(i)

    @pl.when(at_end)
    def _():
        sum_out.advance(0)

    def out_goes(step):
        @pl.when((step == 3) & jnp.logical_not(at_end))
        def _():
            sum_out.advance(0)

    visit(upstream, feed_back, taken=(1, 1), between=out_goes)
    sum_two.take_twin(3)
    sum_two.take_twin(0)
    sum_two.send_ends(0, 0)
    sum_two.take_twin(2)
    sum_two.take_twin(1)
    sum_two.send_ends(0, 1, 2)
    sum_two.send_ends(1, 0, 1)
    for spread in (spread_qkv, spread_o, spread_wide, spread_gate, spread_up):
        spread.drain()
    upstream.drain()
    seconds.drain()
    for rel in range(1, 8):
        for j in range(3):
            qkv_to(rel, j).wait_send()
        for which in range(2):
            for j in range(4):
                gu_to(which, rel, j).wait_send()

    def fold_gu(which):
        cols = pl.ds(which * 768, 768)

        def stage(i):
            block = (0, 4, 1, 5, 2, 3)[i]
            return ys.at[pl.ds((block // 2) * 256, 256), pl.ds((block % 2) * 768, 768)]

        return Fold(
            k, g, lambda e, half: w_gu.at[rows_at(e * 512 + half * 256, 256), cols],
            lambda i: got_gu.at[i, :, cols], stage,
        )

    folds = [fold_gu(0), fold_gu(1)]

    def add_stages(piece, stages):
        def body(i, carry):
            rows = pl.ds(pl.multiple_of(i * 16, 16), 16)
            value = piece[rows, :].astype(F32)
            for stage in stages:
                value = value + stage[rows, :].astype(F32)
            piece[rows, :] = value.astype(BF)
            return carry

        lax.fori_loop(0, 16, body, 0)

    def gu_gradient(which):
        def body(j, carry):
            cols = lanes(j * 512, 512)
            w_gu[rows_at(j * 512, 512), which * 768 : which * 768 + 768] = tn(
                xs[:, cols], d_gu[:, which * 768 : which * 768 + 768]
            ).astype(BF)
            return carry

        lax.fori_loop(0, 4, body, 0)
        folds[which].start()

    def down_gradient(j, carry):
        rows = rows_at(j * 256, 256)
        for i in range(2):
            cols = slice(i * 1024, i * 1024 + 1024)
            w_d[rows, cols] = tn(act[:, lanes(j * 256, 256)], ys[:, cols]).astype(BF)
        return carry

    gu_gradient(0)
    gu_gradient(1)
    load = k.here(n1_kept, xs, keep_slots + 1)
    load.start()
    lax.fori_loop(0, 3, down_gradient, 0)
    start_wide_back, start_thin_back, finish_down_back = down_to_owners(g, k, w_d, got_d)
    sum_two.relay(0, 0)
    folds[0].middle(add_stages)
    sum_two.relay(1, 0)
    gain_two[...] = jnp.zeros_like(gain_two)

    def done_two(at, value):
        rows = rows_at(at, 16)
        there = rows_at(c * BLOCK + at, 16)
        h = hidden[rows, :]
        r = lax.rsqrt(jnp.mean(h * h, -1, keepdims=True) + EPSILON)
        scaled = value * gain_acc[0:1, 2048:4096]
        mean = jnp.mean(h * scaled, -1, keepdims=True)
        d_h = d_hidden[rows, :] + r * scaled - h * (r * r * r * mean)
        part = value * h * r
        gain_two[...] += part[0:8, :] + part[8:16, :]
        d_hidden[rows, :] = d_h
        n1[there, :] = d_h.astype(BF)

    thirds = Gather(k, g, n1, after=tokens)
    sum_two.last(done_two, 0)
    thirds.start_part(0)
    sum_two.send_ends(1, 2)
    sum_two.relay(0, 1)
    sum_two.relay(1, 1)
    thirds.step_part(0, 0)
    sum_two.last(done_two, 1)
    thirds.start_part(1)

    @pl.when(at_end)
    def _():
        sum_out.advance(1)


    folds[1].middle(add_stages)
    start_wide_back()
    thirds.step_part(1, 0)
    thirds.step_part(0, 1)

    sum_two.drain()
    d_kv[...] = jnp.zeros_like(d_kv)
    gain_qk[...] = jnp.zeros_like(gain_qk)

    def unrotated(gradient, value, gain, at):
        gradient = gradient * cosine[at, :] + pltpu.roll(gradient * sine[at, :], 64, 1)
        r = lax.rsqrt(jnp.mean(value * value, -1, keepdims=True) + EPSILON)
        part = gradient * value * r
        gradient = gradient * gain
        mean = jnp.mean(gradient * value, -1, keepdims=True)
        result = gradient * r - value * (r * r * r * mean)
        return result, jnp.sum(part.reshape(-1, 8, 128), 0)

    def attend_back(chip):
        at = rows_at(chip * 256, 256)
        d_o = nt(n1[at, :], w_o[...].reshape(256, 2048)).astype(BF)
        for head in range(2):
            cols = slice(head * 128, head * 128 + 128)
            probs = jnp.exp(head_scores(head, at, chip * 256) - lse[head, at, 0:1])
            d_probs = nt(d_o[:, cols], qkv[:, 384:512])
            delta = jnp.sum(d_probs * probs, -1, keepdims=True)
            d_scores = (probs * (d_probs - delta)).astype(BF)
            d_q = jnp.dot(d_scores, qkv[:, 256:384], preferred_element_type=F32) * scale
            d_kv[:, 0:128] += tn(d_scores, qkv[at, cols]) * scale
            d_kv[:, 128:256] += tn(probs.astype(BF), d_o[:, cols])
            d_q, part = unrotated(d_q, raw[at, cols], gain_q, at)
            d_qkv[at, cols] = d_q.astype(BF)
            gain_qk[:, 0:128] += part

    stage_slots = k.take(14)

    def gu_home(which, rel, j):
        place, count = UNIT_PARTS[j]
        src = w_gu.at[rows_at(d * 512 + (c ^ rel) * 64, 64), pl.ds(which * 768 + place, count)]
        dst = (out_g, out_u)[which].at[:, lanes(unit_column(j, z, p), count)]
        slot = gu_slots + which * 32 + rel * 4 + j
        return k.to(src, dst, (d, c ^ rel), slot) if rel else k.here(src, dst, slot)

    def sum_gu(which):
        folds[which].final(add_stages)
        for rel in range(8):
            for j in range(4):
                gu_home(which, rel, j).start()

    def meanwhile(step):
        @pl.when(step == 1)
        def _():
            @pl.when(jnp.logical_not(at_end))
            def _():
                sum_out.advance(1)

            sum_gu(0)

        @pl.when(step == 2)
        def _():
            sum_gu(1)

    visit(thirds, attend_back, taken=(2, 1), between=meanwhile)

    attn_slots = k.take(8)

    def qkv_rows(e, first, count):
        return d_gu.at[rows_at(lax.rem(e, 2) * 512 + first, count), lanes((e // 2) * 512, 512)]

    def qkv_over_dp(rel):
        return k.to(
            qkv_rows(d ^ rel, 0, 512), got_qkv.at[rel - 1], (d ^ rel, c), attn_slots + rel - 1
        )

    def wo_grad_over_dp(rel):
        src = w_o.at[:, rows_at((d ^ rel) * 16, 16)]
        return k.to(src, got_o.at[rel - 1], (d ^ rel, c), attn_slots + 3 + rel)

    def wo_gradient(j, carry):
        cols = lanes(j * 512, 512)
        w_o[:, :, cols] = tn(o[...], n1[:, cols]).astype(BF).reshape(4, 64, 512)
        return carry

    lax.fori_loop(0, 4, wo_gradient, 0)
    for rel in (1, 2, 3):
        wo_grad_over_dp(rel).start()

    def finish_keys(i, carry):
        at = rows_at(i * 256, 256)
        d_k, part = unrotated(d_kv[at, 0:128], raw[at, 256:384], gain_k, at)
        d_qkv[at, 256:384] = d_k.astype(BF)
        d_qkv[at, 384:512] = d_kv[at, 128:256].astype(BF)
        gain_qk[:, 128:256] += part
        return carry

    lax.fori_loop(0, 4, finish_keys, 0)
    load.wait()

    def qkv_gradient(e, carry):
        cols = lanes(e * 512, 512)
        rows, place = rows_at(lax.rem(e, 2) * 512, 512), lanes((e // 2) * 512, 512)
        d_gu[rows, place] = tn(xs[:, cols], d_qkv[...]).astype(BF)
        return carry

    lax.fori_loop(0, 4, qkv_gradient, 0)
    for rel in (1, 2, 3):
        qkv_over_dp(rel).start()
    start_thin_back()
    sum_three = Scatter(k, g, partial2, from_twin, from_left, from_right, after=sum_one)
    for chip in (3, 0, 2, 1):

        def columns(j, carry):
            cols = lanes(j * 512, 512)
            rows = pl.ds(chip * 256, 256)
            value = nt(d_qkv[rows, :], w_qkv[rows_at(j * 512, 512), :])
            partial2[rows, cols] = value.astype(BF)
            return carry

        lax.fori_loop(0, 4, columns, 0)
        sum_three.send_twin(chip)
    sum_three.take_twin(3)
    sum_three.take_twin(0)
    sum_three.start()
    sum_three.take_twin(2)
    sum_three.take_twin(1)

    def gain_columns(e, carry):
        rows, place = rows_at(lax.rem(e, 2) * 512, 512), lanes((e // 2) * 512, 512)
        product = d_gu[rows, place].astype(F32) * w_qkv[rows_at(e * 512, 512), :].astype(F32)
        gain_one[:, lanes(e * 512, 512)] = nt(jnp.ones((8, 512), BF), product.astype(BF))
        return carry

    lax.fori_loop(0, 4, gain_columns, 0)
    gain_vec[:, 0:2048] = gain_one[0:1, :] / gain_acc[0:1, 0:2048]
    gain_vec[:, 2048:4096] = jnp.sum(gain_two[...], 0, keepdims=True)
    gain_vec[:, 4096:4352] = jnp.sum(gain_qk[...], 0, keepdims=True)
    sum_slots = k.take(12)

    def gain_sum_over_ctx(rel):
        return k.to(gain_vec, gain_ctx.at[rel - 1], (d, c ^ rel), sum_slots + rel)

    def gain_sum_over_dp(rel):
        return k.to(gain_out, gain_dp.at[rel - 1], (d ^ rel, c), sum_slots + 8 + rel)

    for rel in range(1, 8):
        gain_sum_over_ctx(rel).start()
    for rel in (1, 2, 3):
        wo_grad_over_dp(rel).wait()
    for i in range(4):
        rows = rows_at(d * 16, 16)
        value = w_o[i, rows, :].astype(F32)
        for j in range(3):
            value = value + got_o[j, i].astype(F32)
        w_o[i, rows, :] = value.astype(BF)
    back_slots = k.take(20)

    def wo_back_ctx(i):
        src, dst = w_o.at[i, rows_at(d * 16, 16)], wo_back.at[z]
        return k.to(src, dst, (d, 4 * p + i), back_slots + i, back_slots + 4 + z)

    def wo_back_here(i):
        return k.here(w_o.at[i, rows_at(d * 16, 16)], wo_back.at[z], back_slots + i)

    def wo_home(rel):
        src, dst = wo_back.at[d ^ rel], out_o.at[rows_at(d * 16, 16)]
        slot = back_slots + 8 + rel
        return k.to(src, dst, (d ^ rel, c), slot) if rel else k.here(src, dst, slot)

    for i in range(4):

        @pl.when(c == 4 * p + i)
        def _():
            wo_back_here(i).start()

        @pl.when(c != 4 * p + i)
        def _():
            wo_back_ctx(i).start()

    sum_three.advance(0)


    sum_three.advance(1)


    def qkv_home(rel, j):
        other = c ^ rel
        width = 256 if j == 0 else 128
        src = d_gu.at[
            rows_at(lax.rem(d, 2) * 512 + other * 64, 64),
            lanes((d // 2) * 512 + (0, 256, 384)[j], width),
        ]
        dst = (out_q, out_k, out_v)[j].at[:, lanes(c * width, width)]
        slot = qkv_slots + 3 * rel + j
        return k.to(src, dst, (d, other), slot) if rel else k.here(src, dst, slot)

    for rel in (1, 2, 3):
        qkv_over_dp(rel).wait()
    qkv_stage = [
        k.here(
            got_qkv.at[i],
            ys.at[pl.ds(512, 512), pl.ds(i * 512, 512)],
            stage_slots + 11 + i,
        )
        for i in range(3)
    ]
    for copy in qkv_stage:
        copy.start()
    for copy in qkv_stage:
        copy.wait()

    def add_qkv(i, carry):
        at = i * 16
        rows, place = rows_at(lax.rem(d, 2) * 512 + at, 16), lanes((d // 2) * 512, 512)
        value = d_gu[rows, place].astype(F32)
        for j in range(3):
            value = value + ys[rows_at(512 + at, 16), j * 512 : j * 512 + 512].astype(F32)
        d_gu[rows, place] = value.astype(BF)
        return carry

    lax.fori_loop(0, 32, add_qkv, 0)
    for rel in range(8):
        for j in range(3):
            qkv_home(rel, j).start()
    for j in range(4):

        @pl.when(jnp.logical_not((j == z) & wo_stays))
        def _():
            src, dst = w_o.at[0, rows_at(0, 16)], wo_back.at[0]
            k.to(src, dst, (d, c ^ 1), back_slots, back_slots + 4 + j).wait_recv()

    for i in range(4):

        @pl.when(c == 4 * p + i)
        def _():
            wo_back_here(i).wait()

        @pl.when(c != 4 * p + i)
        def _():
            wo_back_ctx(i).wait_send()

    for rel in range(4):
        wo_home(rel).start()

    total = gain_vec[...]
    for rel in range(1, 8):
        gain_sum_over_ctx(rel).wait()
        total = total + gain_ctx[rel - 1]
    gain_out[...] = total
    for rel in range(1, 4):
        gain_sum_over_dp(rel).start()

    sum_out.advance(2)

    def done_out(at, value):
        rows = rows_at(at, 16)
        output[rows, :] = (hidden[rows, :] + value).astype(BF)

    sum_out.finish(done_out)

    finish_down_back()
    stages = [
        k.here(got_d.at[i], ys.at[pl.ds(i * 192, 192)], stage_slots + 6 + i) for i in range(4)
    ]
    for copy in stages:
        copy.start()
    for copy in stages:
        copy.wait()

    def add_down(i, carry):
        at = i * 16
        value = 0.0
        for j in range(4):
            value = value + ys[rows_at(j * 192 + at, 16), :].astype(F32)
        ys[rows_at(at, 16), :] = value.astype(BF)
        return carry

    lax.fori_loop(0, 12, add_down, 0)
    down_home = k.here(ys.at[pl.ds(0, 192)], out_d, stage_slots + 10)
    down_home.start()

    sum_three.advance(2)

    def done_three(at, value):
        rows = rows_at(at, 16)
        v = x_own[rows, :].astype(F32)
        r = lax.rsqrt(jnp.mean(v * v, -1, keepdims=True) + EPSILON)
        scaled = value * gain_acc[0:1, 0:2048]
        mean = jnp.mean(v * scaled, -1, keepdims=True)
        x_grad[rows, :] = (d_hidden[rows, :] + r * scaled - v * (r * r * r * mean)).astype(BF)

    sum_three.finish(done_three)
    total = gain_out[...]
    for rel in range(1, 4):
        gain_sum_over_dp(rel).wait()
        total = total + gain_dp[rel - 1]
    gain_out[...] = total

    for rel in range(8):
        for j in range(3):
            qkv_home(rel, j).wait()
        for which in range(2):
            for j in range(4):
                gu_home(which, rel, j).wait()
        if rel:
            gain_over_ctx(rel).wait_send()
    for rel in range(4):
        wo_home(rel).wait()
        if rel:
            gain_over_dp(rel).wait_send()
            wo_over_dp(rel).wait_send()
            wo_over_ctx(rel).wait_send()

    @pl.when(jnp.logical_not(wo_stays))
    def _():
        wo_over_ctx(0).wait_send()

    down_home.wait()
    for fold in folds:
        fold.drain()
    thirds.drain()
    sum_out.drain()
    sum_three.drain()


def run_layer(x, prefix, wq, wk, wv, wo, wg, wu, wd, gains, cosine, sine, dy):
    width = 2048
    any_space, vmem = pl.BlockSpec(memory_space=pl.ANY), pl.BlockSpec(memory_space=pltpu.VMEM)
    shape, hold = jax.ShapeDtypeStruct, pltpu.VMEM
    return pl.pallas_call(
        layer_kernel,
        out_shape=(
            shape((BLOCK, width), BF), shape((BLOCK, width), BF), shape((1, 4352), F32),
            shape((64, 2048), BF), shape((64, 1024), BF), shape((64, 1024), BF), shape((64, 2048), BF),
            shape((64, 6144), BF), shape((64, 6144), BF), shape((192, 2048), BF),
            shape((1024, width), BF), shape((6, 256, 1536), BF), shape((4, 192, 2048), BF),
            shape((3, 512, 512), BF),
        ),
        in_specs=[any_space, pl.BlockSpec(memory_space=pltpu.SMEM)] + [any_space] * 7 + [vmem] * 3 + [any_space],
        out_specs=(vmem,) * 3 + (any_space,) * 11,
        scratch_shapes=[
            hold((1024, width), BF), hold((1024, width), BF), hold((1024, width), BF),
            hold((1024, width), BF), hold((1024, width), BF),
            hold((512, width), BF), hold((384, width), BF), hold((384, width), BF),
            hold((512, width), BF), hold((384, width), BF), hold((384, width), BF),
            hold((width, 512), BF), hold((4, 64, width), BF), hold((width, 1536), BF), hold((768, width), BF),
            hold((1024, 512), BF), hold((1024, 384), F32), hold((1024, 256), BF), hold((2, 1024, 128), F32),
            hold((1024, 768), BF), hold((1024, 1536), BF),
            hold((BLOCK, width), F32), hold((BLOCK, width), F32), hold((BLOCK, width), BF),
            hold((1024, 256), F32), hold((1024, 512), BF),
            hold((4, 16, width), BF), hold((4, 16, width), BF), hold((3, 4, 16, width), BF),
            hold((4, 8, 16, 256), BF), hold((8, 4608), F32), hold((8, width), F32), hold((8, width), F32),
            hold((8, 256), F32), hold((1, 4352), F32), hold((7, 1, 4352), F32), hold((3, 1, 4352), F32),
            pltpu.SemaphoreType.DMA((SLOTS,)), pltpu.SemaphoreType.DMA((SLOTS,)),
        ],
        compiler_params=pltpu.CompilerParams(
            collective_id=0, has_side_effects=True, vmem_limit_bytes=VMEM_BYTES
        ),
        name="layer",
    )(x, prefix, wq, wk, wv, wo, wg, wu, wd, gains, cosine, sine, dy)


SLOTS = 348


def widen_kernel(*refs):
    narrow, wide = refs[:9], refs[9:18]
    held, turned, sems = refs[18:27], refs[27:34], refs[34]
    loads = [pltpu.make_async_copy(a, b, sems.at[i]) for i, (a, b) in enumerate(zip(narrow, held))]
    stores = [
        pltpu.make_async_copy(a, b, sems.at[9 + i])
        for i, (a, b) in enumerate(zip(turned + held[7:], wide))
    ]
    for copy in loads:
        copy.start()
    for load, store, a, b in zip(loads, stores, held, turned):
        load.wait()

        def body(i, carry):
            rows = rows_at(i * 32, 32)
            b[rows, :] = a[rows, :].astype(F32)
            return carry

        lax.fori_loop(0, a.shape[0] // 32, body, 0)
        store.start()
    for i in (7, 8):
        loads[i].wait()
        stores[i].start()
    for copy in stores:
        copy.wait()


def widen(narrow, same):
    place, shape, hold = pl.BlockSpec(memory_space=pltpu.HBM), jax.ShapeDtypeStruct, pltpu.VMEM
    return pl.pallas_call(
        widen_kernel,
        out_shape=tuple(shape(a.shape, F32) for a in narrow) + tuple(shape(a.shape, BF) for a in same),
        in_specs=[place] * 9,
        out_specs=(place,) * 9,
        scratch_shapes=[hold(a.shape, BF) for a in narrow + same]
        + [hold(a.shape, F32) for a in narrow]
        + [pltpu.SemaphoreType.DMA((18,))],
        compiler_params=pltpu.CompilerParams(vmem_limit_bytes=VMEM_BYTES),
        name="widen",
    )(*narrow, *same)


def rope_tables(length):
    freqs = ROPE_BASE ** (-(np.arange(HEAD_SIZE // 2, dtype=np.float32) * 2.0 / HEAD_SIZE))
    angles = np.arange(length, dtype=np.float32)[:, None] * freqs.astype(np.float32)[None, :]
    cosine, sine = np.cos(angles), np.sin(angles)
    return np.concatenate([cosine, cosine], 1), np.concatenate([-sine, sine], 1)


def with_kernel(layer_input, prefix, wq, wk, wv, wo, w_gate, w_up, w_down, gains, cotangent):
    cosine, sine = rope_tables(layer_input.shape[1] * 8)
    results = run_layer(
        layer_input[0], prefix, wq, wk, wv, wo, w_gate, w_up, w_down,
        jnp.pad(gains.reshape(1, 136), ((0, 15), (0, 120))),
        cosine, sine, cotangent[0],
    )
    output, x_grad, gain_sum = results[:3]
    first = (lax.axis_index("dp") * 8 + lax.axis_index("ctx")) * 136
    gains_grad = lax.dynamic_slice_in_dim(gain_sum[0], first, 136, 0)
    big_first = (8, 7, 9, 3, 6, 4, 5)
    final = widen([results[i] for i in big_first], [output, x_grad])
    wide = tuple(final[big_first.index(i)] for i in range(3, 10))
    return (final[7][None], final[8][None]) + wide + (gains_grad,)


def solution(mesh):
    tokens = P("dp", "ctx", None)
    matrix = P(("dp", "ctx"), None)
    vector = P(("dp", "ctx"))
    small = mesh.shape["dp"] == 4 and mesh.shape["ctx"] == 8
    return jax.shard_map(
        with_kernel if small else general,
        mesh=mesh,
        in_specs=(tokens, P("dp")) + (matrix,) * 7 + (vector, tokens),
        out_specs=(tokens, tokens) + (matrix,) * 7 + (vector,),
        check_vma=False,
    )
```

```python
import jax
import jax.numpy as jnp
import numpy as np
from jax import lax
from jax.experimental import pallas as pl
from jax.experimental.pallas import tpu as pltpu
from jax.sharding import PartitionSpec as P

QUERY_HEADS = 16
KEY_VALUE_HEADS = 8
HEAD_SIZE = 128
EPSILON = 1e-06
ROPE_BASE = 1000000.0
BF = jnp.bfloat16
F32 = jnp.float32


def rms_scale(value, gain):
    return value * lax.rsqrt(jnp.mean(value * value, -1, keepdims=True) + EPSILON) * gain


def rotate(value, cosine, sine):
    half = value.shape[-1] // 2
    first = value[..., :half]
    second = value[..., half:]
    return jnp.concatenate([first * cosine - second * sine, second * cosine + first * sine], -1)


def mm(left, right):
    return jnp.dot(left, right, preferred_element_type=F32)


def mm_tn(left, right):
    return lax.dot_general(left, right, (((0,), (0,)), ((), ())), preferred_element_type=F32)


def mm_nt(left, right):
    return lax.dot_general(left, right, (((1,), (1,)), ((), ())), preferred_element_type=F32)


def gated_unit(gate, up):
    return jax.nn.silu(gate) * up


def swap_ctx(pieces):
    return lax.all_to_all(pieces, "ctx", 0, 0)


def general(layer_input, prefix, wq, wk, wv, wo, w_gate, w_up, w_down, gains, cotangent):
    nd, nc = lax.axis_size("dp"), lax.axis_size("ctx")
    me = lax.axis_index("ctx")
    rows = layer_input.shape[1]
    seq = rows * nc
    depth, width = wq.shape[0], layer_input.shape[2]
    heads = QUERY_HEADS // nc
    copies = max(1, nc // KEY_VALUE_HEADS)
    kv_heads = max(1, KEY_VALUE_HEADS // nc)
    unit = w_down.shape[0]
    scale = HEAD_SIZE ** (-0.5)

    def columns_to(weight, parts):
        return jnp.moveaxis(weight.reshape(depth, parts, -1), 1, 0)

    def by_head(weight, repeat):
        parts = columns_to(weight, nc // repeat)
        return jnp.repeat(parts, repeat, 0) if repeat > 1 else parts

    def by_unit(weight):
        return jnp.transpose(weight.reshape(depth, nd, nc, unit), (2, 0, 1, 3)).reshape(
            nc, depth, nd * unit
        )

    def everywhere(array):
        return lax.all_gather(array, "dp", axis=0, tiled=True)

    qkv_piece = jnp.concatenate([by_head(wq, 1), by_head(wk, copies), by_head(wv, copies)], 2)
    w_qkv = everywhere(swap_ctx(qkv_piece).reshape(nc * depth, -1))
    plane = nc * wo.shape[0]
    span = QUERY_HEADS * HEAD_SIZE // nc
    need = span // wo.shape[0]
    by_plane = everywhere(wo).reshape(nd, wo.shape[0], width)
    wanted = jnp.stack([by_plane[i * span // plane] for i in range(nc)])
    arrived = swap_ctx(wanted)
    first_source = (me * span % plane) // wo.shape[0]
    w_o = lax.dynamic_slice_in_dim(arrived, first_source, need, 0).reshape(span, width)
    w_gu = everywhere(
        swap_ctx(jnp.concatenate([by_unit(w_gate), by_unit(w_up)], 2)).reshape(nc * depth, -1)
    )
    w_d = everywhere(w_down)
    gain_all = lax.all_gather(gains, ("dp", "ctx"), axis=0, tiled=True).astype(F32)
    gain_one = gain_all[:width]
    gain_two = gain_all[width : 2 * width]
    gain_q = gain_all[2 * width : 2 * width + HEAD_SIZE]
    gain_k = gain_all[2 * width + HEAD_SIZE :]

    def whole(array):
        return lax.all_gather(array, "ctx", axis=0, tiled=True)

    def own_sum(partial):
        return lax.psum_scatter(partial.astype(BF), "ctx", scatter_dimension=0, tiled=True).astype(
            F32
        )

    pos = jnp.arange(seq, dtype=jnp.int32)
    visible = (pos[None, :] <= pos[:, None]) | (pos[None, :] < prefix[0])
    freqs = ROPE_BASE ** (-(jnp.arange(HEAD_SIZE // 2, dtype=F32) * 2.0 / HEAD_SIZE))
    angles = pos.astype(F32)[:, None] * freqs[None, :]
    cosine = jnp.cos(angles)[:, None, :]
    sine = jnp.sin(angles)[:, None, :]

    def prepare_heads(raw, gain):
        return rotate(rms_scale(raw, gain), cosine, sine)

    inputs = layer_input[0].astype(F32)
    n1, back_one = jax.vjp(rms_scale, inputs, gain_one)
    n1_all = whole(n1.astype(BF))
    dy_all = whole(cotangent[0])
    qkv = mm(n1_all, w_qkv)
    q_raw = qkv[:, : heads * HEAD_SIZE].reshape(seq, heads, HEAD_SIZE)
    k_raw = qkv[:, heads * HEAD_SIZE : (heads + kv_heads) * HEAD_SIZE].reshape(
        seq, kv_heads, HEAD_SIZE
    )
    v = qkv[:, (heads + kv_heads) * HEAD_SIZE :].astype(BF).reshape(seq, kv_heads, HEAD_SIZE)
    q_rot, back_q = jax.vjp(prepare_heads, q_raw, gain_q)
    k_rot, back_k = jax.vjp(prepare_heads, k_raw, gain_k)
    q_rot = q_rot.astype(BF).reshape(seq, kv_heads, -1, HEAD_SIZE)
    k_rot = k_rot.astype(BF)
    scores = jnp.einsum("tkgd,skd->kgts", q_rot, k_rot, preferred_element_type=F32) * scale
    scores = jnp.where(visible[None, None], scores, -1e30)
    top = jnp.max(scores, -1, keepdims=True)
    expo = jnp.exp(scores - top)
    total = jnp.sum(expo, -1, keepdims=True)
    probs = expo / total
    probs_bf = probs.astype(BF)
    o = jnp.einsum("kgts,skd->tkgd", probs_bf, v, preferred_element_type=F32).astype(BF)
    o = o.reshape(seq, heads * HEAD_SIZE)
    hidden = inputs + own_sum(mm(o, w_o))
    n2, back_two = jax.vjp(rms_scale, hidden, gain_two)
    n2_all = whole(n2.astype(BF))
    gu = mm(n2_all, w_gu)
    gate, up = gu[:, : nd * unit], gu[:, nd * unit :]
    active, back_gated = jax.vjp(gated_unit, gate, up)
    active = active.astype(BF)
    output = (hidden + own_sum(mm(active, w_d))).astype(BF)
    def row_sum(term):
        return lax.psum_scatter(term.astype(BF), "dp", scatter_dimension=0, tiled=True)

    down_grad = row_sum(mm_tn(active, dy_all)).astype(F32)
    d_gate, d_up = back_gated(mm_nt(dy_all, w_d))
    d_gu = jnp.concatenate([d_gate.astype(BF), d_up.astype(BF)], 1)
    gu_sum = swap_ctx(row_sum(mm_tn(n2_all, d_gu)).reshape(nc, depth, -1)).astype(F32)
    gu_sum = gu_sum.reshape(nc, depth, 2, nd, unit)
    gu_sum = jnp.transpose(gu_sum, (2, 1, 3, 0, 4)).reshape(2, depth, -1)
    gate_grad, up_grad = gu_sum[0], gu_sum[1]
    upstream = cotangent[0].astype(F32)
    d_hidden_part, d_gain_two = back_two(own_sum(mm_nt(d_gu, w_gu)))
    d_hidden = upstream + d_hidden_part
    d_attn = whole(d_hidden.astype(BF))
    wo_term = mm_tn(o, d_attn).astype(BF).reshape(need, wo.shape[0], width)
    slots = jnp.zeros((nc, wo.shape[0], width), BF)
    slots = lax.dynamic_update_slice_in_dim(slots, wo_term, first_source, 0)
    back_home = swap_ctx(slots)
    mine = []
    for plane_index in range(nd):
        total_plane = 0
        for i in range(nc):
            if i * span // plane == plane_index:
                total_plane = total_plane + back_home[i].astype(F32)
        mine.append(total_plane)
    wo_grad = lax.psum_scatter(
        jnp.stack(mine).astype(BF), "dp", scatter_dimension=0, tiled=True
    )[0].astype(F32)
    d_o = mm_nt(d_attn, w_o).astype(BF).reshape(seq, kv_heads, -1, HEAD_SIZE)
    d_probs = jnp.einsum("tkgd,skd->kgts", d_o, v, preferred_element_type=F32)
    d_v = jnp.einsum("kgts,tkgd->skd", probs_bf, d_o, preferred_element_type=F32).astype(BF)
    d_scores = (probs * (d_probs - jnp.sum(d_probs * probs, -1, keepdims=True))).astype(BF)
    d_q = jnp.einsum("kgts,skd->tkgd", d_scores, k_rot, preferred_element_type=F32) * scale
    d_k = jnp.einsum("kgts,tkgd->skd", d_scores, q_rot, preferred_element_type=F32) * scale
    d_q, d_gain_q = back_q(d_q.reshape(seq, heads, HEAD_SIZE))
    d_k, d_gain_k = back_k(d_k)
    d_qkv = jnp.concatenate(
        [a.reshape(seq, -1).astype(BF) for a in (d_q, d_k, d_v)], 1
    )
    qkv_sum = swap_ctx(row_sum(mm_tn(n1_all, d_qkv)).reshape(nc, depth, -1)).astype(F32)
    at_k, at_v = heads * HEAD_SIZE, (heads + kv_heads) * HEAD_SIZE

    def columns_back(part, repeat):
        part = part.reshape(nc // repeat, repeat, depth, -1).sum(1)
        return jnp.moveaxis(part, 0, 1).reshape(depth, -1)

    wq_grad = columns_back(qkv_sum[:, :, :at_k], 1)
    wk_grad = columns_back(qkv_sum[:, :, at_k:at_v], copies)
    wv_grad = columns_back(qkv_sum[:, :, at_v:], copies)
    d_input_part, d_gain_one = back_one(own_sum(mm_nt(d_qkv, w_qkv)))
    x_grad = (d_hidden + d_input_part).astype(BF)
    gain_term = jnp.concatenate([d_gain_one, d_gain_two, d_gain_q, d_gain_k])
    gains_grad = lax.psum_scatter(gain_term, ("dp", "ctx"), scatter_dimension=0, tiled=True)
    return (
        output[None], x_grad[None], wq_grad, wk_grad, wv_grad, wo_grad,
        gate_grad, up_grad, down_grad, gains_grad,
    )


MESH = pl.DeviceIdType.MESH
BLOCK = 128
VMEM_BYTES = 64 << 20


class Copies:
    def __init__(self, sends, receives):
        self.sends, self.receives = sends, receives
        self.used = 0

    def take(self, count=1):
        first = self.used
        self.used += count
        if self.used > SLOTS:
            raise ValueError("more semaphores")
        return first

    def to(self, src, dst, device, slot, receive_slot=None):
        receive_slot = slot if receive_slot is None else receive_slot
        return pltpu.make_async_remote_copy(
            src_ref=src,
            dst_ref=dst,
            send_sem=self.sends.at[slot],
            recv_sem=self.receives.at[receive_slot],
            device_id=device,
            device_id_type=MESH,
        )

    def here(self, src, dst, slot):
        return pltpu.make_async_copy(src, dst, self.sends.at[slot])


class Place:
    def __init__(self):
        self.d = lax.axis_index("dp")
        self.c = lax.axis_index("ctx")
        self.z = self.c // 2
        self.p = lax.rem(self.c, 2)

    def at(self, d, c):
        return (d, c)


def meet():
    barrier = pltpu.get_barrier_semaphore()
    d, c = lax.axis_index("dp"), lax.axis_index("ctx")
    partners = [(d, c ^ rel) for rel in range(1, 8)]
    partners += [(d ^ rel, c ^ twin) for rel in range(1, 4) for twin in range(2)]
    for partner in partners:
        pl.semaphore_signal(barrier, inc=1, device_id=partner, device_id_type=MESH)
    pl.semaphore_wait(barrier, len(partners))


def when(condition, then):
    if isinstance(condition, bool):
        if condition:
            then()
    else:
        pl.when(condition)(then)


def rows_at(start, size):
    return pl.ds(pl.multiple_of(start, 16), size)


class Gather:
    def __init__(self, copies, place, buf, parts=2, after=None):
        self.k, self.g, self.buf, self.parts = copies, place, buf, parts
        self.size = BLOCK // parts
        if after is None:
            self.right = copies.take(3 * parts)
            self.left = copies.take(3 * parts)
            self.twin = copies.take(7 * parts)
        else:
            self.right, self.left, self.twin = after.right, after.left, after.twin

    def piece(self, z, p, part):
        return self.buf.at[rows_at((2 * z + p) * BLOCK + part * self.size, self.size)]

    def line(self, step, part, rightwards):
        g = self.g
        z = g.z - step if rightwards else g.z + step
        slot = (self.right if rightwards else self.left) + step * self.parts + part
        piece = self.piece(z, g.p, part)
        to = g.c + 2 if rightwards else g.c - 2
        return self.k.to(piece, piece, (g.d, to), slot)

    def wait_line(self, step, part, rightwards):
        piece = self.piece(self.g.z, self.g.p, part)
        slot = (self.right if rightwards else self.left) + step * self.parts + part
        self.k.to(piece, piece, (self.g.d, self.g.c ^ 1), slot).wait_recv()

    def twins(self, order, z, part):
        piece = self.piece(z, self.g.p, part)
        return self.k.to(piece, piece, (self.g.d, self.g.c ^ 1), self.twin + order * self.parts + part)

    def can_send(self, step, rightwards):
        z = self.g.z
        return (z >= step) & (z < 3) if rightwards else (z + step <= 3) & (z > 0)

    def gets(self, step, rightwards):
        z = self.g.z
        return z >= step + 1 if rightwards else z + step + 1 <= 3

    def start(self):
        for part in range(self.parts):
            self.start_part(part)

    def start_part(self, part):
        for rightwards in (True, False):

            @pl.when(self.can_send(0, rightwards))
            def _():
                self.line(0, part, rightwards).start()

        self.twins(0, self.g.z, part).start()

    def start_line(self, right, left):
        for part in range(self.parts):
            for now, rightwards in ((right, True), (left, False)):

                @pl.when(now & self.can_send(0, rightwards))
                def _():
                    self.line(0, part, rightwards).start()

    def start_twin(self):
        for part in range(self.parts):
            self.twins(0, self.g.z, part).start()

    def step(self, step):
        for part in range(self.parts):
            self.step_part(step, part)

    def step_part(self, step, part):
        for side, rightwards in enumerate((True, False)):
            z = self.g.z - 1 - step if rightwards else self.g.z + 1 + step

            @pl.when(self.gets(step, rightwards))
            def _():
                self.wait_line(step, part, rightwards)

                def on():
                    @pl.when(self.can_send(step + 1, rightwards))
                    def _():
                        self.line(step + 1, part, rightwards).start()

                when(step < 2, on)
                self.twins(1 + 2 * step + side, z, part).start()

    def twin_own(self):
        for part in range(self.parts):
            self.twins(0, self.g.z, part).wait_recv()

    def twin_step(self, step):
        for part in range(self.parts):
            for side, rightwards in enumerate((True, False)):

                @pl.when(self.gets(step, rightwards))
                def _():
                    self.twins(1 + 2 * step + side, self.g.z, part).wait_recv()

    def drain(self):
        for part in range(self.parts):
            self.twins(0, self.g.z, part).wait_send()
            for step in range(3):
                for side, rightwards in enumerate((True, False)):

                    @pl.when(self.can_send(step, rightwards))
                    def _():
                        self.line(step, part, rightwards).wait_send()

                    @pl.when(self.gets(step, rightwards))
                    def _():
                        self.twins(1 + 2 * step + side, self.g.z, part).wait_send()


def add_rows(dst, dst_row, a, a_row, b, b_row, count):
    def body(i, carry):
        at = i * 32
        total = a[rows_at(a_row + at, 32), :].astype(F32) + b[rows_at(b_row + at, 32), :].astype(F32)
        dst[rows_at(dst_row + at, 32), :] = total.astype(dst.dtype)
        return carry

    lax.fori_loop(0, count // 32, body, 0)


class Scatter:
    def __init__(self, copies, place, partial, from_twin, from_left, from_right, parts=2, after=None):
        self.k, self.g = copies, place
        self.partial, self.from_twin = partial, from_twin
        self.from_line = {True: from_left, False: from_right}
        self.parts, self.size = parts, BLOCK // parts
        if after is None:
            self.twin = copies.take(4)
            self.slots = {True: copies.take(3 * parts), False: copies.take(3 * parts)}
        else:
            self.twin, self.slots = after.twin, after.slots

    def row(self, z, p):
        return (2 * z + p) * BLOCK

    def twins(self, z, slot):
        g = self.g
        src = self.partial.at[rows_at(self.row(z, 1 - g.p), BLOCK)]
        dst = self.from_twin.at[rows_at(z * BLOCK, BLOCK)]
        return self.k.to(src, dst, (g.d, g.c ^ 1), self.twin + slot)

    def send_twin(self, z):
        self.twins(z, z).start()

    def take_twin(self, z):
        self.twins(z, z).wait_recv()
        at = self.row(z, self.g.p)
        add_rows(self.partial, at, self.partial, at, self.from_twin, z * BLOCK, BLOCK)

    def target(self, step, rightwards):
        return self.g.z + 3 - step if rightwards else self.g.z - 3 + step

    def can_send(self, step, rightwards):
        z = self.g.z
        return z <= step if rightwards else 3 - z <= step

    def gets(self, step, rightwards):
        z = self.g.z
        return (z >= 1) & (z - 1 <= step) if rightwards else (z <= 2) & (2 - z <= step)

    def line(self, step, rightwards, part):
        g = self.g
        at = self.row(self.target(step, rightwards), g.p) + part * self.size
        src = self.partial.at[rows_at(at, self.size)]
        dst = self.from_line[rightwards].at[rows_at(step * BLOCK + part * self.size, self.size)]
        slot = self.slots[rightwards] + step * self.parts + part
        return self.k.to(src, dst, (g.d, g.c + 2 if rightwards else g.c - 2), slot)

    def wait_line(self, step, rightwards, part):
        src = self.partial.at[pl.ds(0, self.size)]
        dst = self.from_line[rightwards].at[rows_at(step * BLOCK + part * self.size, self.size)]
        slot = self.slots[rightwards] + step * self.parts + part
        self.k.to(src, dst, (self.g.d, self.g.c ^ 1), slot).wait_recv()

    def send(self, step, part):
        for rightwards in (True, False):

            @pl.when(self.can_send(step, rightwards))
            def _():
                self.line(step, rightwards, part).start()

    def start(self):
        for part in range(self.parts):
            self.send(0, part)

    def advance(self, step):
        for part in range(self.parts):
            for rightwards in (True, False):

                @pl.when(self.gets(step, rightwards))
                def _():
                    self.wait_line(step, rightwards, part)

                    def add():
                        z = self.g.z + 2 - step if rightwards else self.g.z - 2 + step
                        at = self.row(z, self.g.p) + part * self.size
                        add_rows(
                            self.partial, at, self.partial, at, self.from_line[rightwards],
                            step * BLOCK + part * self.size, self.size,
                        )

                    when(step < 2, add)

            when(step < 2, lambda: self.send(step + 1, part))

    def finish(self, done, slot=2, part=None):
        g = self.g
        own = self.row(g.z, g.p)
        first, count = (0, BLOCK) if part is None else (part * self.size, self.size)

        def body(i, carry):
            at = first + i * 16
            total = self.partial[rows_at(own + at, 16), :].astype(F32)
            a = self.from_line[True][rows_at(slot * BLOCK + at, 16), :].astype(F32)
            b = self.from_line[False][rows_at(slot * BLOCK + at, 16), :].astype(F32)
            total = total + jnp.where(g.z >= 1, a, 0.0) + jnp.where(g.z <= 2, b, 0.0)
            done(at, total)
            return carry

        lax.fori_loop(0, count // 16, body, 0)

    def send_ends(self, part, *steps):
        for rightwards in (True, False):

            @pl.when(self.g.z == (0 if rightwards else 3))
            def _():
                for step in steps:
                    self.line(step, rightwards, part).start()

    def relay(self, step, part):
        for rightwards in (True, False):

            @pl.when(self.gets(step, rightwards))
            def _():
                self.wait_line(step, rightwards, part)
                z = self.g.z + 2 - step if rightwards else self.g.z - 2 + step
                at = self.row(z, self.g.p) + part * self.size
                add_rows(
                    self.partial, at, self.partial, at, self.from_line[rightwards],
                    step * BLOCK + part * self.size, self.size,
                )
                self.line(step + 1, rightwards, part).start()

    def last(self, done, part):
        for rightwards in (True, False):

            @pl.when(self.gets(2, rightwards))
            def _():
                self.wait_line(2, rightwards, part)

        self.finish(done, part=part)

    def drain(self):
        for z in range(4):
            self.twins(z, z).wait_send()
        for step in range(3):
            for part in range(self.parts):
                for rightwards in (True, False):

                    @pl.when(self.can_send(step, rightwards))
                    def _():
                        self.line(step, rightwards, part).wait_send()


class Spread:
    def __init__(self, copies, place, piece):
        self.k, self.g, self.piece = copies, place, piece
        self.slots = copies.take(6)

    def direct(self, half, rel):
        g = self.g
        piece = self.piece(g.d, half)
        return self.k.to(piece, piece, (g.d ^ rel, g.c), self.slots + 2 * (rel - 1) + half)

    def passed(self, rel):
        g = self.g
        piece = self.piece(g.d ^ (3 - rel), rel - 1)
        return self.k.to(piece, piece, (g.d ^ rel, g.c), self.slots + 4 + rel - 1)

    def start(self):
        for half, rel in ((0, 1), (1, 2), (1, 1), (0, 2)):
            self.direct(half, rel).start()

    def forward(self):
        self.direct(1, 1).wait_recv()
        self.passed(2).start()
        self.direct(0, 2).wait_recv()
        self.passed(1).start()

    def finish(self):
        self.direct(0, 1).wait_recv()
        self.direct(1, 2).wait_recv()
        self.passed(1).wait_recv()
        self.passed(2).wait_recv()

    def drain(self):
        for half, rel in ((0, 1), (1, 2), (1, 1), (0, 2)):
            self.direct(half, rel).wait_send()
        self.passed(1).wait_send()
        self.passed(2).wait_send()


class Direct:
    def __init__(self, copies, place, piece):
        self.k, self.g, self.piece = copies, place, piece
        self.slots = copies.take(3)

    def copy(self, rel):
        piece = self.piece(self.g.d)
        return self.k.to(piece, piece, (self.g.d ^ rel, self.g.c), self.slots + rel - 1)

    def start(self):
        for rel in (1, 2, 3):
            self.copy(rel).start()

    def finish(self):
        for rel in (1, 2, 3):
            self.copy(rel).wait_recv()

    def drain(self):
        for rel in (1, 2, 3):
            self.copy(rel).wait_send()


class Fold:
    def __init__(self, copies, place, piece, got, stage):
        self.k, self.g, self.piece, self.got, self.stage = copies, place, piece, got, stage
        self.slots = copies.take(6)
        self.loads = copies.take(6)

    def first(self, half, passed):
        g = self.g
        rel = 1 + half
        src = self.piece(g.d ^ (3 if passed else rel), half)
        i = 2 * half + passed
        return self.k.to(src, self.got(i), (g.d ^ rel, g.c), self.slots + i)

    def second(self, half):
        g = self.g
        rel = 2 - half
        return self.k.to(
            self.piece(g.d ^ rel, half), self.got(4 + half), (g.d ^ rel, g.c), self.slots + 4 + half
        )

    def load(self, i):
        return self.k.here(self.got(i), self.stage(i), self.loads + i)

    def start(self):
        for passed in (1, 0):
            for half in range(2):
                self.first(half, passed).start()

    def middle(self, add):
        for half in range(2):
            self.first(half, 1).wait_recv()
            self.load(2 * half + 1).start()
        for half in range(2):
            self.load(2 * half + 1).wait()
            add(self.piece(self.g.d ^ (2 - half), half), (self.stage(2 * half + 1),))
            self.second(half).start()

    def final(self, add):
        for half in range(2):
            self.first(half, 0).wait_recv()
            self.load(2 * half).start()
        for half in range(2):
            self.second(half).wait_recv()
            self.load(4 + half).start()
        for half in range(2):
            self.load(2 * half).wait()
            self.load(4 + half).wait()
            add(self.piece(self.g.d, half), (self.stage(2 * half), self.stage(4 + half)))

    def drain(self):
        for half in range(2):
            for passed in range(2):
                self.first(half, passed).wait_send()
            self.second(half).wait_send()


def down_to_units(place, copies, src, dst):
    g, p, d = place, place.p, place.d
    send, receive = copies.take(8), copies.take(12)
    odd = lax.rem(d, 2)
    wide = (src.at[rows_at(p * 64, 128)], dst.at[rows_at(wide_row(p, d), 128)])
    thin = (src.at[rows_at((1 - p) * 128, 64)], dst.at[rows_at(thin_row(d, p), 64)])
    stays = odd == p

    def thin_to(rel, core):
        return copies.to(
            *thin, (d ^ rel, 2 * g.z + odd), send + 4 + rel, receive + 4 + 2 * rel + core
        )

    def start_thin():
        for rel in (1, 2, 3):
            thin_to(rel, p).start()

        @pl.when(stays)
        def _():
            copies.here(*thin, send + 4).start()

        @pl.when(jnp.logical_not(stays))
        def _():
            thin_to(0, p).start()

    copies.here(*wide, send).start()
    spread = Spread(
        copies, g, lambda e, half: dst.at[rows_at(wide_row(p, e) + half * 64, 64)]
    )

    def start_wide():
        copies.here(*wide, send).wait()
        spread.start()

    def finish():
        spread.finish()

        @pl.when(stays)
        def _():
            copies.here(*thin, send + 4).wait()

        @pl.when(jnp.logical_not(stays))
        def _():
            thin_to(0, p).wait_send()

        for rel in (1, 2, 3):
            thin_to(rel, p).wait_send()
        for rel in range(4):

            @pl.when(lax.rem(d ^ rel, 2) == p)
            def _():
                if rel:
                    thin_to(rel, p).wait_recv()
                thin_to(rel, 1 - p).wait_recv()

    return start_thin, start_wide, spread, finish


def unit_row(core, plane):
    return (plane // 2) * 384 + (lax.rem(plane, 2) ^ core) * 256


def wide_row(core, plane):
    return unit_row(core, plane) + core * lax.rem(plane, 2) * 128


def thin_row(plane, core):
    odd = lax.rem(plane, 2)
    return unit_row(odd, plane) + (1 - odd) * 128 + core * 64


def down_to_owners(place, copies, src, dst):
    g, p, d = place, place.p, place.d
    send, receive = copies.take(12), copies.take(8)

    def wide(rel):
        plane = d ^ rel
        a = src.at[rows_at(wide_row(p, plane), 128)]
        b = dst.at[rel, rows_at(p * 64, 128)]
        if rel == 0:
            return copies.here(a, b, send)
        return copies.to(a, b, (plane, g.c), send + rel, receive + rel)

    def thin(rel, core):
        plane = d ^ rel
        a = src.at[rows_at(thin_row(plane, core), 64)]
        b = dst.at[rel, rows_at((1 - core) * 128, 64)]
        return copies.to(
            a, b, (plane, 2 * g.z + core), send + 4 + 2 * rel + core, receive + 4 + rel
        )

    def thin_own():
        a = src.at[rows_at(thin_row(d, p), 64)]
        return copies.here(a, dst.at[0, rows_at((1 - p) * 128, 64)], send + 4 + p)

    def holds(rel):
        return lax.rem(d ^ rel, 2) == p

    def start_wide():
        for rel in (1, 2, 3, 0):
            wide(rel).start()

    def start_thin():
        for rel in (1, 2, 3, 0):

            @pl.when(holds(rel))
            def _():
                if rel:
                    thin(rel, p).start()
                else:
                    thin_own().start()
                thin(rel, 1 - p).start()

    def finish():
        wide(0).wait()
        for rel in (1, 2, 3):
            wide(rel).wait()
        for rel in range(4):

            @pl.when(holds(rel))
            def _():
                if rel:
                    thin(rel, p).wait_send()
                else:
                    thin_own().wait()
                thin(rel, 1 - p).wait_send()

        @pl.when(jnp.logical_not(holds(0)))
        def _():
            thin(0, p).wait_recv()

        for rel in (1, 2, 3):
            thin(rel, p).wait_recv()

    return start_wide, start_thin, finish


UNIT_PARTS = ((0, 256), (256, 128), (384, 256), (640, 128))


def unit_column(j, z, core):
    plane = 2 * (j // 2) + (core if j % 2 == 0 else 1 - core)
    return plane * 1536 + z * 384 + core * (128 if j % 2 == 0 else 256)


def lanes(start, size):
    return pl.ds(pl.multiple_of(start, 128), size)


def nt(left, right):
    return lax.dot_general(left, right, (((1,), (1,)), ((), ())), preferred_element_type=F32)


def tn(left, right):
    return lax.dot_general(left, right, (((0,), (0,)), ((), ())), preferred_element_type=F32)


def layer_kernel(
    x, prefix, wq, wk, wv, wo, wg, wu, wd, gains, cosine, sine, dy,
    output, x_grad, gain_out, out_q, out_k, out_v, out_o, out_g, out_u, out_d,
    n1_kept, got_gu, got_d, got_qkv,
    xs, n1, ys, partial, partial2, from_twin, from_left, from_right, from_twin2, from_left2, from_right2,
    w_qkv, w_o, w_gu, w_d, qkv, raw, o, lse, act, d_gu, hidden, d_hidden, x_own, d_kv, d_qkv,
    wo_mid, wo_back, got_o, gain_buf, gain_acc, gain_one, gain_two, gain_qk, gain_vec, gain_ctx, gain_dp,
    sends, receives,
):
    g = Place()
    k = Copies(sends, receives)
    d, c, z, p = g.d, g.c, g.z, g.p
    meet()
    own = rows_at(c * BLOCK, BLOCK)
    shard = rows_at(d * 512, 512)
    mine = rows_at(d * 512 + c * 64, 64)

    gain_buf[d, c] = gains[...]
    gain_slots = k.take(12)

    def gain_over_ctx(rel):
        return k.to(gain_buf.at[d, c], gain_buf.at[d, c], (d, c ^ rel), gain_slots + rel)

    def gain_over_dp(rel):
        return k.to(gain_buf.at[d], gain_buf.at[d], (d ^ rel, c), gain_slots + 8 + rel)

    for rel in range(1, 8):
        gain_over_ctx(rel).start()

    own_slots = k.take(3)
    own_copies = [
        k.here(x, xs.at[own], own_slots),
        k.here(x, x_own, own_slots + 1),
        k.here(dy, ys.at[own], own_slots + 2),
    ]
    for copy in own_copies:
        copy.start()

    qkv_slots = k.take(8)

    def qkv_to(rel, j):
        other = c ^ rel
        width = 256 if j == 0 else 128
        src = (wq, wk, wv)[j].at[:, lanes(other * width, width)]
        dst = w_qkv.at[mine, pl.ds((0, 256, 384)[j], width)]
        slot = qkv_slots + rel
        return k.to(src, dst, (d, other), slot) if rel else k.here(src, dst, slot)

    def qkv_pieces(rel):
        whole = w_qkv.at[mine]
        slot = qkv_slots + rel
        return k.to(whole, whole, (d, c ^ rel), slot) if rel else k.here(whole, whole, slot)

    for rel in range(8):
        for j in range(3):
            qkv_to(rel, j).start()
    own_copies[0].wait()
    tokens = Gather(k, g, xs)
    tokens.start()
    at_end = (z == 0) | (z == 3)
    gu_slots = k.take(16)

    def gu_to(which, rel, j):
        place, count = UNIT_PARTS[j]
        column = unit_column(j, z ^ (rel // 2), p ^ (rel % 2))
        src = (wg, wu)[which].at[:, lanes(column, count)]
        dst = w_gu.at[mine, pl.ds(which * 768 + place, count)]
        slot = gu_slots + which * 8 + rel
        return k.to(src, dst, (d, c ^ rel), slot) if rel else k.here(src, dst, slot)

    def gu_start(*groups):
        for which in range(2):
            for group in groups:
                for rel in (2 * group, 2 * group + 1):
                    for j in range(4):
                        gu_to(which, rel, j).start()

    @pl.when(at_end)
    def _():
        gu_start(1)


    wo_slots = k.take(20)
    far = c // 4

    def wo_over_dp(rel):
        src, dst = wo.at[rows_at((d ^ rel) * 16, 16)], wo_mid.at[d]
        slot = wo_slots + rel
        return k.to(src, dst, (d ^ rel, c), slot) if rel else k.here(src, dst, slot)

    def wo_over_ctx(rel):
        src, dst = wo_mid.at[z ^ rel], w_o.at[lax.rem(c, 4), rows_at(d * 16, 16)]
        return k.to(
            src, dst, (d, 2 * (z ^ rel) + far), wo_slots + 4 + rel, wo_slots + 8 + lax.rem(c, 4)
        )

    def wo_stay():
        return k.here(
            wo_mid.at[z], w_o.at[lax.rem(c, 4), rows_at(d * 16, 16)], wo_slots + 4
        )

    wo_stays = far == p
    for rel in range(4):
        wo_over_dp(rel).start()

    start_thin, start_wide, spread_wide, finish_down = down_to_units(g, k, wd, w_d)

    for rel in range(1, 8):
        gain_over_ctx(rel).wait_recv()
    for rel in range(1, 4):
        gain_over_dp(rel).start()
    start_thin()
    for rel in range(1, 4):
        gain_over_dp(rel).wait_recv()
    gain_acc[...] = jnp.zeros_like(gain_acc)
    for i in range(32):
        row = gain_buf[i // 8, i % 8][0:8, :].astype(F32)
        row = jnp.concatenate([row, jnp.zeros((8, 128), F32)], 1)
        shift = (8 * i) % 128
        if shift:
            row = pltpu.roll(row, shift, 1)
        first = 136 * i - shift
        gain_acc[:, first : first + 384] += row

    def normalize(block):
        def body(i, carry):
            at = rows_at(block * BLOCK + i * 16, 16)
            v = xs[at, :].astype(F32)
            r = lax.rsqrt(jnp.mean(v * v, -1, keepdims=True) + EPSILON)
            n1[at, :] = (v * r * gain_acc[0:1, 0:2048]).astype(BF)
            return carry

        lax.fori_loop(0, BLOCK // 16, body, 0)

    normalize(c)
    qkv_pieces(0).wait()
    for rel in range(1, 8):
        qkv_pieces(rel).wait_recv()
    spread_qkv = Spread(k, g, lambda e, half: w_qkv.at[rows_at(e * 512 + half * 256, 256)])
    spread_qkv.start()
    tokens.twin_own()
    normalize(c ^ 1)

    def each_side(step, use):
        def side(i, carry):
            chip = jnp.where(i == 0, z - 1 - step, z + 1 + step)

            @pl.when((chip >= 0) & (chip <= 3))
            def _():
                use(chip)

            return carry

        lax.fori_loop(0, 2, side, 0)

    def normalize_chip(chip):
        normalize(2 * chip)
        normalize(2 * chip + 1)

    gain_q, gain_k = gain_acc[0:1, 4096:4224], gain_acc[0:1, 4224:4352]

    def rotated(value, gain, at):
        r = lax.rsqrt(jnp.mean(value * value, -1, keepdims=True) + EPSILON)
        value = value * r * gain
        return value * cosine[at, :] + pltpu.roll(value, 64, 1) * sine[at, :]

    def project(chip):
        at = rows_at(chip * 256, 256)
        product = jnp.dot(n1[at, :], w_qkv[...], preferred_element_type=F32)
        raw[at, :] = product[:, :384]
        for j, gain in ((0, gain_q), (1, gain_q), (2, gain_k)):
            qkv[at, j * 128 : j * 128 + 128] = rotated(
                product[:, j * 128 : j * 128 + 128], gain, at
            ).astype(BF)
        qkv[at, 384:512] = product[:, 384:].astype(BF)

    def project_all(first, last):
        def body(i, carry):
            step = first + i // 2
            chip = jnp.where(lax.rem(i, 2) == 0, z - 1 - step, z + 1 + step)

            @pl.when((chip >= 0) & (chip <= 3) & ((step >= 0) | (lax.rem(i, 2) == 0)))
            def _():
                project(chip)

            return carry

        lax.fori_loop(0, 2 * (last - first), body, 0)

    tokens.step(0)

    @pl.when(jnp.logical_not(at_end))
    def _():
        gu_start(3)

    for rel in range(4):
        if rel == 0:
            wo_over_dp(0).wait()
        else:
            wo_over_dp(rel).wait_recv()
    for rel in range(1, 4):
        wo_over_ctx(rel).start()

    @pl.when(wo_stays)
    def _():
        wo_stay().start()

    @pl.when(jnp.logical_not(wo_stays))
    def _():
        wo_over_ctx(0).start()

    tokens.twin_step(0)
    each_side(0, normalize_chip)
    tokens.step(1)
    own_copies[2].wait()
    upstream = Gather(k, g, ys)
    upstream.start_line(z == 2, z == 1)
    spread_qkv.forward()
    tokens.twin_step(1)
    each_side(1, normalize_chip)
    for i in range(4):

        @pl.when(jnp.logical_not(c == 4 * p + i))
        def _():
            src, dst = wo_mid.at[0], w_o.at[0, rows_at(0, 16)]
            k.to(src, dst, (d, c ^ 1), wo_slots + 4, wo_slots + 8 + i).wait_recv()

    @pl.when(wo_stays)
    def _():
        wo_stay().wait()

    spread_o = Direct(k, g, lambda e: w_o.at[:, rows_at(e * 16, 16)])
    spread_o.start()
    start_wide()
    spread_qkv.finish()
    project_all(-1, 1)
    tokens.step(2)
    tokens.twin_step(2)
    each_side(2, normalize_chip)

    def gu_pieces(which, rel):
        whole = w_gu.at[mine, pl.ds(which * 768, 768)]
        slot = gu_slots + which * 8 + rel
        return k.to(whole, whole, (d, c ^ rel), slot) if rel else k.here(whole, whole, slot)

    def gu_take(which):
        gu_pieces(which, 0).wait()
        for rel in range(1, 8):
            gu_pieces(which, rel).wait_recv()

    @pl.when(at_end)
    def _():
        gu_start(0, 2, 3)

    project_all(1, 3)
    keep_slots = k.take(2)
    keep = k.here(n1, n1_kept, keep_slots)
    keep.start()

    limit = prefix[0]
    scale = HEAD_SIZE**-0.5

    def head_scores(head, at, first_row):
        scores = nt(qkv[at, head * 128 : head * 128 + 128], qkv[:, 256:384]) * scale
        row = first_row + lax.broadcasted_iota(jnp.int32, (256, 1), 0)
        column = lax.broadcasted_iota(jnp.int32, (1, 1024), 1)
        return jnp.where(column < jnp.maximum(row + 1, limit), scores, -1e30)

    def attend(head):
        def body(i, carry):
            at = rows_at(i * 256, 256)
            scores = head_scores(head, at, i * 256)
            top = jnp.max(scores, -1, keepdims=True)
            expo = jnp.exp(scores - top)
            total = jnp.sum(expo, -1, keepdims=True)
            probs = (expo * (1.0 / total)).astype(BF)
            value = jnp.dot(probs, qkv[:, 384:512], preferred_element_type=F32)
            o[at, head * 128 : head * 128 + 128] = value.astype(BF)
            lse[head, at, :] = jnp.broadcast_to(top + jnp.log(total), (256, 128))
            return carry

        lax.fori_loop(0, 4, body, 0)

    attend(0)
    attend(1)

    @pl.when(jnp.logical_not(at_end))
    def _():
        gu_start(0, 1, 2)

    spread_wide.forward()
    tokens.drain()
    spread_o.finish()
    sum_one = Scatter(k, g, partial, from_twin, from_left, from_right)
    for chip in (3, 0, 2, 1):

        def columns(j, carry):
            cols = lanes(j * 512, 512)
            rows = pl.ds(chip * 256, 256)
            value = jnp.dot(
                o[rows, :], w_o[:, :, cols].reshape(256, 512), preferred_element_type=F32
            )
            partial[rows, cols] = value.astype(BF)
            return carry

        lax.fori_loop(0, 4, columns, 0)
        sum_one.send_twin(chip)
    d_hidden[...] = ys[own, :].astype(F32)

    def upstream_goes(step):
        upstream.start_line((step == z) & (z < 2), (step == 3 - z) & (z > 1))


    sum_one.take_twin(3)
    sum_one.take_twin(0)
    sum_one.send_ends(0, 0)
    sum_one.take_twin(2)
    sum_one.take_twin(1)
    sum_one.send_ends(0, 1, 2)
    sum_one.send_ends(1, 0, 1, 2)
    gu_take(0)
    spread_gate = Spread(
        k, g, lambda e, half: w_gu.at[rows_at(e * 512 + half * 256, 256), pl.ds(0, 768)]
    )
    spread_gate.start()
    sum_one.relay(0, 0)
    gu_take(1)
    spread_up = Spread(
        k, g, lambda e, half: w_gu.at[rows_at(e * 512 + half * 256, 256), pl.ds(768, 768)]
    )
    spread_up.start()
    sum_one.relay(1, 0)
    own_copies[1].wait()

    def done_one(at, value):
        rows = rows_at(at, 16)
        h = x_own[rows, :].astype(F32) + value
        r = lax.rsqrt(jnp.mean(h * h, -1, keepdims=True) + EPSILON)
        hidden[rows, :] = h
        xs[rows_at(c * BLOCK + at, 16), :] = (h * r * gain_acc[0:1, 2048:4096]).astype(BF)

    seconds = Gather(k, g, xs, after=tokens)
    sum_one.last(done_one, 0)
    seconds.start_part(0)
    sum_one.relay(0, 1)
    spread_gate.forward()
    sum_one.relay(1, 1)
    seconds.step_part(0, 0)
    sum_one.last(done_one, 1)
    seconds.start_part(1)
    spread_up.forward()
    upstream_goes(0)
    upstream.start_twin()
    seconds.step_part(1, 0)
    seconds.step_part(0, 1)
    upstream_goes(1)
    spread_gate.finish()
    finish_down()
    sum_one.drain()
    keep.wait()
    spread_up.finish()
    sum_two = Scatter(k, g, partial2, from_twin, from_left, from_right, after=sum_one)
    sum_out = Scatter(k, g, partial, from_twin2, from_left2, from_right2, parts=1)

    def feed_forward(chip):
        at = rows_at(chip * 256, 256)

        def units(j, carry):
            cols, up_cols = lanes(j * 256, 256), lanes(768 + j * 256, 256)
            gate = jnp.dot(xs[at, :], w_gu[:, cols], preferred_element_type=F32)
            up = jnp.dot(xs[at, :], w_gu[:, up_cols], preferred_element_type=F32)
            act[at, cols] = (gate * up * (1.0 / (1.0 + jnp.exp(-gate)))).astype(BF)
            d_gu[at, cols] = gate.astype(BF)
            d_gu[at, up_cols] = up.astype(BF)
            return carry

        lax.fori_loop(0, 3, units, 0)

        def columns(j, carry):
            cols = lanes(j * 512, 512)
            partial[at, cols] = jnp.dot(
                act[at, :], w_d[:, cols], preferred_element_type=F32
            ).astype(BF)
            return carry

        lax.fori_loop(0, 4, columns, 0)
        sum_out.send_twin(chip)

    def feed_back(chip):
        at = rows_at(chip * 256, 256)

        def units(j, carry):
            cols, up_cols = lanes(j * 256, 256), lanes(768 + j * 256, 256)
            d_act = nt(ys[at, :], w_d[rows_at(j * 256, 256), :])
            gate, up = d_gu[at, cols].astype(F32), d_gu[at, up_cols].astype(F32)
            sig = 1.0 / (1.0 + jnp.exp(-gate))
            d_gu[at, cols] = (d_act * up * sig * (1.0 + gate * (1.0 - sig))).astype(BF)
            d_gu[at, up_cols] = (d_act * gate * sig).astype(BF)
            return carry

        lax.fori_loop(0, 3, units, 0)

        def columns(j, carry):
            rows = rows_at(j * 512, 512)
            partial2[at, lanes(j * 512, 512)] = nt(d_gu[at, :], w_gu[rows, :]).astype(BF)
            return carry

        lax.fori_loop(0, 4, columns, 0)
        sum_two.send_twin(chip)

    def visit(gather, use, between=None, taken=(0, 0), used=None):
        inner = jnp.where(z <= 1, 1, -1)

        def body(step, carry):
            @pl.when(step == 0)
            def _():
                gather.twin_own()

            @pl.when(step > 0)
            @jax.named_scope("twin")
            def _():
                gather.twin_step(step - 1)

            def side(i, carry):
                chip = jnp.where(i == 0, z + inner * step, z - inner * step)

                @pl.when((chip >= 0) & (chip <= 3) & ((i == 0) | (step > 0)))
                @jax.named_scope("use")
                def _():
                    use(chip)

                if used is not None:

                    @pl.when(i == 0)
                    def _():
                        used(step)

                for part in range(gather.parts):

                    @pl.when((i == 0) & (step >= taken[part]) & (step < 3))
                    @jax.named_scope("arrive")
                    def _():
                        gather.step_part(step, part)

                if between is not None:

                    @pl.when(i == 0)
                    @jax.named_scope("between")
                    def _():
                        between(step)

                return carry

            lax.fori_loop(0, 2, side, 0)
            return carry

        lax.fori_loop(0, 4, body, 0)

    def upstream_passes(step):
        @pl.when(step == 1)
        def _():
            upstream_goes(2)

        @pl.when((step == 2) & jnp.logical_not(at_end))
        def _():
            upstream.step(0)

    visit(seconds, feed_forward, taken=(2, 1), between=upstream_passes)

    @pl.when(at_end)
    def _():
        upstream.step(0)

    for i in (3, 0):
        sum_out.take_twin(i)
    sum_out.start()
    for i in (2, 1):
        sum_out.take_twin(i)

    @pl.when(at_end)
    def _():
        sum_out.advance(0)

    def out_goes(step):
        @pl.when((step == 3) & jnp.logical_not(at_end))
        def _():
            sum_out.advance(0)

    visit(upstream, feed_back, taken=(1, 1), between=out_goes)
    sum_two.take_twin(3)
    sum_two.take_twin(0)
    sum_two.send_ends(0, 0)
    sum_two.take_twin(2)
    sum_two.take_twin(1)
    sum_two.send_ends(0, 1, 2)
    sum_two.send_ends(1, 0, 1)
    for spread in (spread_qkv, spread_o, spread_wide, spread_gate, spread_up):
        spread.drain()
    upstream.drain()
    seconds.drain()
    for rel in range(1, 8):
        qkv_pieces(rel).wait_send()
        for which in range(2):
            gu_pieces(which, rel).wait_send()

    def fold_gu(which):
        cols = pl.ds(which * 768, 768)

        def stage(i):
            block = (0, 4, 1, 5, 2, 3)[i]
            return ys.at[pl.ds((block // 2) * 256, 256), pl.ds((block % 2) * 768, 768)]

        return Fold(
            k, g, lambda e, half: w_gu.at[rows_at(e * 512 + half * 256, 256), cols],
            lambda i: got_gu.at[i, :, cols], stage,
        )

    folds = [fold_gu(0), fold_gu(1)]

    def add_stages(piece, stages):
        def body(i, carry):
            rows = pl.ds(pl.multiple_of(i * 16, 16), 16)
            value = piece[rows, :].astype(F32)
            for stage in stages:
                value = value + stage[rows, :].astype(F32)
            piece[rows, :] = value.astype(BF)
            return carry

        lax.fori_loop(0, 16, body, 0)

    def gu_gradient(which):
        def body(j, carry):
            cols = lanes(j * 512, 512)
            w_gu[rows_at(j * 512, 512), which * 768 : which * 768 + 768] = tn(
                xs[:, cols], d_gu[:, which * 768 : which * 768 + 768]
            ).astype(BF)
            return carry

        lax.fori_loop(0, 4, body, 0)
        folds[which].start()

    def down_gradient(j, carry):
        rows = rows_at(j * 256, 256)
        for i in range(2):
            cols = slice(i * 1024, i * 1024 + 1024)
            w_d[rows, cols] = tn(act[:, lanes(j * 256, 256)], ys[:, cols]).astype(BF)
        return carry

    gu_gradient(0)
    gu_gradient(1)
    load = k.here(n1_kept, xs, keep_slots + 1)
    load.start()
    lax.fori_loop(0, 3, down_gradient, 0)
    start_wide_back, start_thin_back, finish_down_back = down_to_owners(g, k, w_d, got_d)
    sum_two.relay(0, 0)
    folds[0].middle(add_stages)
    sum_two.relay(1, 0)
    gain_two[...] = jnp.zeros_like(gain_two)

    def done_two(at, value):
        rows = rows_at(at, 16)
        there = rows_at(c * BLOCK + at, 16)
        h = hidden[rows, :]
        r = lax.rsqrt(jnp.mean(h * h, -1, keepdims=True) + EPSILON)
        scaled = value * gain_acc[0:1, 2048:4096]
        mean = jnp.mean(h * scaled, -1, keepdims=True)
        d_h = d_hidden[rows, :] + r * scaled - h * (r * r * r * mean)
        part = value * h * r
        gain_two[...] += part[0:8, :] + part[8:16, :]
        d_hidden[rows, :] = d_h
        n1[there, :] = d_h.astype(BF)

    thirds = Gather(k, g, n1, after=tokens)
    sum_two.last(done_two, 0)
    thirds.start_part(0)
    sum_two.send_ends(1, 2)
    sum_two.relay(0, 1)
    sum_two.relay(1, 1)
    thirds.step_part(0, 0)
    sum_two.last(done_two, 1)
    thirds.start_part(1)

    @pl.when(at_end)
    def _():
        sum_out.advance(1)


    folds[1].middle(add_stages)
    start_wide_back()
    thirds.step_part(1, 0)
    thirds.step_part(0, 1)

    sum_two.drain()
    d_kv[...] = jnp.zeros_like(d_kv)
    gain_qk[...] = jnp.zeros_like(gain_qk)

    def unrotated(gradient, value, gain, at):
        gradient = gradient * cosine[at, :] + pltpu.roll(gradient * sine[at, :], 64, 1)
        r = lax.rsqrt(jnp.mean(value * value, -1, keepdims=True) + EPSILON)
        part = gradient * value * r
        gradient = gradient * gain
        mean = jnp.mean(gradient * value, -1, keepdims=True)
        result = gradient * r - value * (r * r * r * mean)
        return result, jnp.sum(part.reshape(-1, 8, 128), 0)

    def attend_back(chip):
        at = rows_at(chip * 256, 256)
        d_o = nt(n1[at, :], w_o[...].reshape(256, 2048)).astype(BF)
        for head in range(2):
            cols = slice(head * 128, head * 128 + 128)
            probs = jnp.exp(head_scores(head, at, chip * 256) - lse[head, at, 0:1])
            d_probs = nt(d_o[:, cols], qkv[:, 384:512])
            delta = jnp.sum(d_probs * probs, -1, keepdims=True)
            d_scores = (probs * (d_probs - delta)).astype(BF)
            d_q = jnp.dot(d_scores, qkv[:, 256:384], preferred_element_type=F32) * scale
            d_kv[:, 0:128] += tn(d_scores, qkv[at, cols]) * scale
            d_kv[:, 128:256] += tn(probs.astype(BF), d_o[:, cols])
            d_q, part = unrotated(d_q, raw[at, cols], gain_q, at)
            d_qkv[at, cols] = d_q.astype(BF)
            gain_qk[:, 0:128] += part

    stage_slots = k.take(14)

    def gu_home(which, rel, j):
        place, count = UNIT_PARTS[j]
        src = w_gu.at[rows_at(d * 512 + (c ^ rel) * 64, 64), pl.ds(which * 768 + place, count)]
        dst = (out_g, out_u)[which].at[:, lanes(unit_column(j, z, p), count)]
        slot = gu_slots + which * 8 + rel
        return k.to(src, dst, (d, c ^ rel), slot) if rel else k.here(src, dst, slot)

    def sum_gu(which):
        folds[which].final(add_stages)
        for rel in range(8):
            for j in range(4):
                gu_home(which, rel, j).start()

    def meanwhile(step):
        @pl.when(step == 1)
        def _():
            @pl.when(jnp.logical_not(at_end))
            def _():
                sum_out.advance(1)

            sum_gu(0)

        @pl.when(step == 2)
        def _():
            sum_gu(1)

    visit(thirds, attend_back, taken=(2, 1), between=meanwhile)

    attn_slots = k.take(8)

    def qkv_rows(e, first, count):
        return d_gu.at[rows_at(lax.rem(e, 2) * 512 + first, count), lanes((e // 2) * 512, 512)]

    def qkv_over_dp(rel):
        return k.to(
            qkv_rows(d ^ rel, 0, 512), got_qkv.at[rel - 1], (d ^ rel, c), attn_slots + rel - 1
        )

    def wo_grad_over_dp(rel):
        src = w_o.at[:, rows_at((d ^ rel) * 16, 16)]
        return k.to(src, got_o.at[rel - 1], (d ^ rel, c), attn_slots + 3 + rel)

    def wo_gradient(j, carry):
        cols = lanes(j * 512, 512)
        w_o[:, :, cols] = tn(o[...], n1[:, cols]).astype(BF).reshape(4, 64, 512)
        return carry

    lax.fori_loop(0, 4, wo_gradient, 0)
    for rel in (1, 2, 3):
        wo_grad_over_dp(rel).start()

    def finish_keys(i, carry):
        at = rows_at(i * 256, 256)
        d_k, part = unrotated(d_kv[at, 0:128], raw[at, 256:384], gain_k, at)
        d_qkv[at, 256:384] = d_k.astype(BF)
        d_qkv[at, 384:512] = d_kv[at, 128:256].astype(BF)
        gain_qk[:, 128:256] += part
        return carry

    lax.fori_loop(0, 4, finish_keys, 0)
    load.wait()

    def qkv_gradient(e, carry):
        cols = lanes(e * 512, 512)
        rows, place = rows_at(lax.rem(e, 2) * 512, 512), lanes((e // 2) * 512, 512)
        d_gu[rows, place] = tn(xs[:, cols], d_qkv[...]).astype(BF)
        return carry

    lax.fori_loop(0, 4, qkv_gradient, 0)
    for rel in (1, 2, 3):
        qkv_over_dp(rel).start()
    start_thin_back()
    sum_three = Scatter(k, g, partial2, from_twin, from_left, from_right, after=sum_one)
    for chip in (3, 0, 2, 1):

        def columns(j, carry):
            cols = lanes(j * 512, 512)
            rows = pl.ds(chip * 256, 256)
            value = nt(d_qkv[rows, :], w_qkv[rows_at(j * 512, 512), :])
            partial2[rows, cols] = value.astype(BF)
            return carry

        lax.fori_loop(0, 4, columns, 0)
        sum_three.send_twin(chip)
    sum_three.take_twin(3)
    sum_three.take_twin(0)
    sum_three.start()
    sum_three.take_twin(2)
    sum_three.take_twin(1)

    def gain_columns(e, carry):
        rows, place = rows_at(lax.rem(e, 2) * 512, 512), lanes((e // 2) * 512, 512)
        product = d_gu[rows, place].astype(F32) * w_qkv[rows_at(e * 512, 512), :].astype(F32)
        gain_one[:, lanes(e * 512, 512)] = nt(jnp.ones((8, 512), BF), product.astype(BF))
        return carry

    lax.fori_loop(0, 4, gain_columns, 0)
    gain_vec[:, 0:2048] = gain_one[0:1, :] / gain_acc[0:1, 0:2048]
    gain_vec[:, 2048:4096] = jnp.sum(gain_two[...], 0, keepdims=True)
    gain_vec[:, 4096:4352] = jnp.sum(gain_qk[...], 0, keepdims=True)
    sum_slots = k.take(12)

    def gain_sum_over_ctx(rel):
        return k.to(gain_vec, gain_ctx.at[rel - 1], (d, c ^ rel), sum_slots + rel)

    def gain_sum_over_dp(rel):
        return k.to(gain_out, gain_dp.at[rel - 1], (d ^ rel, c), sum_slots + 8 + rel)

    for rel in range(1, 8):
        gain_sum_over_ctx(rel).start()
    for rel in (1, 2, 3):
        wo_grad_over_dp(rel).wait()
    for i in range(4):
        rows = rows_at(d * 16, 16)
        value = w_o[i, rows, :].astype(F32)
        for j in range(3):
            value = value + got_o[j, i].astype(F32)
        w_o[i, rows, :] = value.astype(BF)
    back_slots = k.take(20)

    def wo_back_ctx(i):
        src, dst = w_o.at[i, rows_at(d * 16, 16)], wo_back.at[z]
        return k.to(src, dst, (d, 4 * p + i), back_slots + i, back_slots + 4 + z)

    def wo_back_here(i):
        return k.here(w_o.at[i, rows_at(d * 16, 16)], wo_back.at[z], back_slots + i)

    def wo_home(rel):
        src, dst = wo_back.at[d ^ rel], out_o.at[rows_at(d * 16, 16)]
        slot = back_slots + 8 + rel
        return k.to(src, dst, (d ^ rel, c), slot) if rel else k.here(src, dst, slot)

    for i in range(4):

        @pl.when(c == 4 * p + i)
        def _():
            wo_back_here(i).start()

        @pl.when(c != 4 * p + i)
        def _():
            wo_back_ctx(i).start()

    sum_three.advance(0)


    sum_three.advance(1)


    def qkv_home(rel, j):
        other = c ^ rel
        width = 256 if j == 0 else 128
        src = d_gu.at[
            rows_at(lax.rem(d, 2) * 512 + other * 64, 64),
            lanes((d // 2) * 512 + (0, 256, 384)[j], width),
        ]
        dst = (out_q, out_k, out_v)[j].at[:, lanes(c * width, width)]
        slot = qkv_slots + rel
        return k.to(src, dst, (d, other), slot) if rel else k.here(src, dst, slot)

    for rel in (1, 2, 3):
        qkv_over_dp(rel).wait()
    qkv_stage = [
        k.here(
            got_qkv.at[i],
            ys.at[pl.ds(512, 512), pl.ds(i * 512, 512)],
            stage_slots + 11 + i,
        )
        for i in range(3)
    ]
    for copy in qkv_stage:
        copy.start()
    for copy in qkv_stage:
        copy.wait()

    def add_qkv(i, carry):
        at = i * 16
        rows, place = rows_at(lax.rem(d, 2) * 512 + at, 16), lanes((d // 2) * 512, 512)
        value = d_gu[rows, place].astype(F32)
        for j in range(3):
            value = value + ys[rows_at(512 + at, 16), j * 512 : j * 512 + 512].astype(F32)
        d_gu[rows, place] = value.astype(BF)
        return carry

    lax.fori_loop(0, 32, add_qkv, 0)
    for rel in range(8):
        for j in range(3):
            qkv_home(rel, j).start()
    for j in range(4):

        @pl.when(jnp.logical_not((j == z) & wo_stays))
        def _():
            src, dst = w_o.at[0, rows_at(0, 16)], wo_back.at[0]
            k.to(src, dst, (d, c ^ 1), back_slots, back_slots + 4 + j).wait_recv()

    for i in range(4):

        @pl.when(c == 4 * p + i)
        def _():
            wo_back_here(i).wait()

        @pl.when(c != 4 * p + i)
        def _():
            wo_back_ctx(i).wait_send()

    for rel in range(4):
        wo_home(rel).start()

    total = gain_vec[...]
    for rel in range(1, 8):
        gain_sum_over_ctx(rel).wait()
        total = total + gain_ctx[rel - 1]
    gain_out[...] = total
    for rel in range(1, 4):
        gain_sum_over_dp(rel).start()

    sum_out.advance(2)

    def done_out(at, value):
        rows = rows_at(at, 16)
        output[rows, :] = (hidden[rows, :] + value).astype(BF)

    sum_out.finish(done_out)

    finish_down_back()
    stages = [
        k.here(got_d.at[i], ys.at[pl.ds(i * 192, 192)], stage_slots + 6 + i) for i in range(4)
    ]
    for copy in stages:
        copy.start()
    for copy in stages:
        copy.wait()

    def add_down(i, carry):
        at = i * 16
        value = 0.0
        for j in range(4):
            value = value + ys[rows_at(j * 192 + at, 16), :].astype(F32)
        ys[rows_at(at, 16), :] = value.astype(BF)
        return carry

    lax.fori_loop(0, 12, add_down, 0)
    down_home = k.here(ys.at[pl.ds(0, 192)], out_d, stage_slots + 10)
    down_home.start()

    sum_three.advance(2)

    def done_three(at, value):
        rows = rows_at(at, 16)
        v = x_own[rows, :].astype(F32)
        r = lax.rsqrt(jnp.mean(v * v, -1, keepdims=True) + EPSILON)
        scaled = value * gain_acc[0:1, 0:2048]
        mean = jnp.mean(v * scaled, -1, keepdims=True)
        x_grad[rows, :] = (d_hidden[rows, :] + r * scaled - v * (r * r * r * mean)).astype(BF)

    sum_three.finish(done_three)
    total = gain_out[...]
    for rel in range(1, 4):
        gain_sum_over_dp(rel).wait()
        total = total + gain_dp[rel - 1]
    gain_out[...] = total

    for rel in range(8):
        qkv_pieces(rel).wait()
        for which in range(2):
            gu_pieces(which, rel).wait()
        if rel:
            gain_over_ctx(rel).wait_send()
    for rel in range(4):
        wo_home(rel).wait()
        if rel:
            gain_over_dp(rel).wait_send()
            wo_over_dp(rel).wait_send()
            wo_over_ctx(rel).wait_send()

    @pl.when(jnp.logical_not(wo_stays))
    def _():
        wo_over_ctx(0).wait_send()

    down_home.wait()
    for fold in folds:
        fold.drain()
    thirds.drain()
    sum_out.drain()
    sum_three.drain()


def run_layer(x, prefix, wq, wk, wv, wo, wg, wu, wd, gains, cosine, sine, dy):
    width = 2048
    any_space, vmem = pl.BlockSpec(memory_space=pl.ANY), pl.BlockSpec(memory_space=pltpu.VMEM)
    shape, hold = jax.ShapeDtypeStruct, pltpu.VMEM
    return pl.pallas_call(
        layer_kernel,
        out_shape=(
            shape((BLOCK, width), BF), shape((BLOCK, width), BF), shape((1, 4352), F32),
            shape((64, 2048), BF), shape((64, 1024), BF), shape((64, 1024), BF), shape((64, 2048), BF),
            shape((64, 6144), BF), shape((64, 6144), BF), shape((192, 2048), BF),
            shape((1024, width), BF), shape((6, 256, 1536), BF), shape((4, 192, 2048), BF),
            shape((3, 512, 512), BF),
        ),
        in_specs=[any_space, pl.BlockSpec(memory_space=pltpu.SMEM)] + [any_space] * 7 + [vmem] * 3 + [any_space],
        out_specs=(vmem,) * 3 + (any_space,) * 11,
        scratch_shapes=[
            hold((1024, width), BF), hold((1024, width), BF), hold((1024, width), BF),
            hold((1024, width), BF), hold((1024, width), BF),
            hold((512, width), BF), hold((384, width), BF), hold((384, width), BF),
            hold((512, width), BF), hold((384, width), BF), hold((384, width), BF),
            hold((width, 512), BF), hold((4, 64, width), BF), hold((width, 1536), BF), hold((768, width), BF),
            hold((1024, 512), BF), hold((1024, 384), F32), hold((1024, 256), BF), hold((2, 1024, 128), F32),
            hold((1024, 768), BF), hold((1024, 1536), BF),
            hold((BLOCK, width), F32), hold((BLOCK, width), F32), hold((BLOCK, width), BF),
            hold((1024, 256), F32), hold((1024, 512), BF),
            hold((4, 16, width), BF), hold((4, 16, width), BF), hold((3, 4, 16, width), BF),
            hold((4, 8, 16, 256), BF), hold((8, 4608), F32), hold((8, width), F32), hold((8, width), F32),
            hold((8, 256), F32), hold((1, 4352), F32), hold((7, 1, 4352), F32), hold((3, 1, 4352), F32),
            pltpu.SemaphoreType.DMA((SLOTS,)), pltpu.SemaphoreType.DMA((SLOTS,)),
        ],
        compiler_params=pltpu.CompilerParams(
            collective_id=0, has_side_effects=True, vmem_limit_bytes=VMEM_BYTES
        ),
        name="layer",
    )(x, prefix, wq, wk, wv, wo, wg, wu, wd, gains, cosine, sine, dy)


SLOTS = 284


def widen_kernel(*refs):
    narrow, wide = refs[:9], refs[9:18]
    held, turned, sems = refs[18:27], refs[27:34], refs[34]
    loads = [pltpu.make_async_copy(a, b, sems.at[i]) for i, (a, b) in enumerate(zip(narrow, held))]
    stores = [
        pltpu.make_async_copy(a, b, sems.at[9 + i])
        for i, (a, b) in enumerate(zip(turned + held[7:], wide))
    ]
    for copy in loads:
        copy.start()
    for load, store, a, b in zip(loads, stores, held, turned):
        load.wait()

        def body(i, carry):
            rows = rows_at(i * 32, 32)
            b[rows, :] = a[rows, :].astype(F32)
            return carry

        lax.fori_loop(0, a.shape[0] // 32, body, 0)
        store.start()
    for i in (7, 8):
        loads[i].wait()
        stores[i].start()
    for copy in stores:
        copy.wait()


def widen(narrow, same):
    place, shape, hold = pl.BlockSpec(memory_space=pltpu.HBM), jax.ShapeDtypeStruct, pltpu.VMEM
    return pl.pallas_call(
        widen_kernel,
        out_shape=tuple(shape(a.shape, F32) for a in narrow) + tuple(shape(a.shape, BF) for a in same),
        in_specs=[place] * 9,
        out_specs=(place,) * 9,
        scratch_shapes=[hold(a.shape, BF) for a in narrow + same]
        + [hold(a.shape, F32) for a in narrow]
        + [pltpu.SemaphoreType.DMA((18,))],
        compiler_params=pltpu.CompilerParams(vmem_limit_bytes=VMEM_BYTES),
        name="widen",
    )(*narrow, *same)


def rope_tables(length):
    freqs = ROPE_BASE ** (-(np.arange(HEAD_SIZE // 2, dtype=np.float32) * 2.0 / HEAD_SIZE))
    angles = np.arange(length, dtype=np.float32)[:, None] * freqs.astype(np.float32)[None, :]
    cosine, sine = np.cos(angles), np.sin(angles)
    return np.concatenate([cosine, cosine], 1), np.concatenate([-sine, sine], 1)


def with_kernel(layer_input, prefix, wq, wk, wv, wo, w_gate, w_up, w_down, gains, cotangent):
    cosine, sine = rope_tables(layer_input.shape[1] * 8)
    results = run_layer(
        layer_input[0], prefix, wq, wk, wv, wo, w_gate, w_up, w_down,
        jnp.pad(gains.reshape(1, 136), ((0, 15), (0, 120))),
        cosine, sine, cotangent[0],
    )
    output, x_grad, gain_sum = results[:3]
    first = (lax.axis_index("dp") * 8 + lax.axis_index("ctx")) * 136
    gains_grad = lax.dynamic_slice_in_dim(gain_sum[0], first, 136, 0)
    big_first = (8, 7, 9, 3, 6, 4, 5)
    final = widen([results[i] for i in big_first], [output, x_grad])
    wide = tuple(final[big_first.index(i)] for i in range(3, 10))
    return (final[7][None], final[8][None]) + wide + (gains_grad,)


def solution(mesh):
    tokens = P("dp", "ctx", None)
    matrix = P(("dp", "ctx"), None)
    vector = P(("dp", "ctx"))
    small = mesh.shape["dp"] == 4 and mesh.shape["ctx"] == 8
    return jax.shard_map(
        with_kernel if small else general,
        mesh=mesh,
        in_specs=(tokens, P("dp")) + (matrix,) * 7 + (vector, tokens),
        out_specs=(tokens, tokens) + (matrix,) * 7 + (vector,),
        check_vma=False,
    )
```

```python
import jax
import jax.numpy as jnp
import numpy as np
from jax import lax
from jax.experimental import pallas as pl
from jax.experimental.pallas import tpu as pltpu
from jax.sharding import PartitionSpec as P

QUERY_HEADS = 16
KEY_VALUE_HEADS = 8
HEAD_SIZE = 128
EPSILON = 1e-06
ROPE_BASE = 1000000.0
BF = jnp.bfloat16
F32 = jnp.float32


def rms_scale(value, gain):
    return value * lax.rsqrt(jnp.mean(value * value, -1, keepdims=True) + EPSILON) * gain


def rotate(value, cosine, sine):
    half = value.shape[-1] // 2
    first = value[..., :half]
    second = value[..., half:]
    return jnp.concatenate([first * cosine - second * sine, second * cosine + first * sine], -1)


def mm(left, right):
    return jnp.dot(left, right, preferred_element_type=F32)


def mm_tn(left, right):
    return lax.dot_general(left, right, (((0,), (0,)), ((), ())), preferred_element_type=F32)


def mm_nt(left, right):
    return lax.dot_general(left, right, (((1,), (1,)), ((), ())), preferred_element_type=F32)


def gated_unit(gate, up):
    return jax.nn.silu(gate) * up


def swap_ctx(pieces):
    return lax.all_to_all(pieces, "ctx", 0, 0)


def general(layer_input, prefix, wq, wk, wv, wo, w_gate, w_up, w_down, gains, cotangent):
    nd, nc = lax.axis_size("dp"), lax.axis_size("ctx")
    me = lax.axis_index("ctx")
    rows = layer_input.shape[1]
    seq = rows * nc
    depth, width = wq.shape[0], layer_input.shape[2]
    heads = QUERY_HEADS // nc
    copies = max(1, nc // KEY_VALUE_HEADS)
    kv_heads = max(1, KEY_VALUE_HEADS // nc)
    unit = w_down.shape[0]
    scale = HEAD_SIZE ** (-0.5)

    def columns_to(weight, parts):
        return jnp.moveaxis(weight.reshape(depth, parts, -1), 1, 0)

    def by_head(weight, repeat):
        parts = columns_to(weight, nc // repeat)
        return jnp.repeat(parts, repeat, 0) if repeat > 1 else parts

    def by_unit(weight):
        return jnp.transpose(weight.reshape(depth, nd, nc, unit), (2, 0, 1, 3)).reshape(
            nc, depth, nd * unit
        )

    def everywhere(array):
        return lax.all_gather(array, "dp", axis=0, tiled=True)

    qkv_piece = jnp.concatenate([by_head(wq, 1), by_head(wk, copies), by_head(wv, copies)], 2)
    w_qkv = everywhere(swap_ctx(qkv_piece).reshape(nc * depth, -1))
    plane = nc * wo.shape[0]
    span = QUERY_HEADS * HEAD_SIZE // nc
    need = span // wo.shape[0]
    by_plane = everywhere(wo).reshape(nd, wo.shape[0], width)
    wanted = jnp.stack([by_plane[i * span // plane] for i in range(nc)])
    arrived = swap_ctx(wanted)
    first_source = (me * span % plane) // wo.shape[0]
    w_o = lax.dynamic_slice_in_dim(arrived, first_source, need, 0).reshape(span, width)
    w_gu = everywhere(
        swap_ctx(jnp.concatenate([by_unit(w_gate), by_unit(w_up)], 2)).reshape(nc * depth, -1)
    )
    w_d = everywhere(w_down)
    gain_all = lax.all_gather(gains, ("dp", "ctx"), axis=0, tiled=True).astype(F32)
    gain_one = gain_all[:width]
    gain_two = gain_all[width : 2 * width]
    gain_q = gain_all[2 * width : 2 * width + HEAD_SIZE]
    gain_k = gain_all[2 * width + HEAD_SIZE :]

    def whole(array):
        return lax.all_gather(array, "ctx", axis=0, tiled=True)

    def own_sum(partial):
        return lax.psum_scatter(partial.astype(BF), "ctx", scatter_dimension=0, tiled=True).astype(
            F32
        )

    pos = jnp.arange(seq, dtype=jnp.int32)
    visible = (pos[None, :] <= pos[:, None]) | (pos[None, :] < prefix[0])
    freqs = ROPE_BASE ** (-(jnp.arange(HEAD_SIZE // 2, dtype=F32) * 2.0 / HEAD_SIZE))
    angles = pos.astype(F32)[:, None] * freqs[None, :]
    cosine = jnp.cos(angles)[:, None, :]
    sine = jnp.sin(angles)[:, None, :]

    def prepare_heads(raw, gain):
        return rotate(rms_scale(raw, gain), cosine, sine)

    inputs = layer_input[0].astype(F32)
    n1, back_one = jax.vjp(rms_scale, inputs, gain_one)
    n1_all = whole(n1.astype(BF))
    dy_all = whole(cotangent[0])
    qkv = mm(n1_all, w_qkv)
    q_raw = qkv[:, : heads * HEAD_SIZE].reshape(seq, heads, HEAD_SIZE)
    k_raw = qkv[:, heads * HEAD_SIZE : (heads + kv_heads) * HEAD_SIZE].reshape(
        seq, kv_heads, HEAD_SIZE
    )
    v = qkv[:, (heads + kv_heads) * HEAD_SIZE :].astype(BF).reshape(seq, kv_heads, HEAD_SIZE)
    q_rot, back_q = jax.vjp(prepare_heads, q_raw, gain_q)
    k_rot, back_k = jax.vjp(prepare_heads, k_raw, gain_k)
    q_rot = q_rot.astype(BF).reshape(seq, kv_heads, -1, HEAD_SIZE)
    k_rot = k_rot.astype(BF)
    scores = jnp.einsum("tkgd,skd->kgts", q_rot, k_rot, preferred_element_type=F32) * scale
    scores = jnp.where(visible[None, None], scores, -1e30)
    top = jnp.max(scores, -1, keepdims=True)
    expo = jnp.exp(scores - top)
    total = jnp.sum(expo, -1, keepdims=True)
    probs = expo / total
    probs_bf = probs.astype(BF)
    o = jnp.einsum("kgts,skd->tkgd", probs_bf, v, preferred_element_type=F32).astype(BF)
    o = o.reshape(seq, heads * HEAD_SIZE)
    hidden = inputs + own_sum(mm(o, w_o))
    n2, back_two = jax.vjp(rms_scale, hidden, gain_two)
    n2_all = whole(n2.astype(BF))
    gu = mm(n2_all, w_gu)
    gate, up = gu[:, : nd * unit], gu[:, nd * unit :]
    active, back_gated = jax.vjp(gated_unit, gate, up)
    active = active.astype(BF)
    output = (hidden + own_sum(mm(active, w_d))).astype(BF)
    def row_sum(term):
        return lax.psum_scatter(term.astype(BF), "dp", scatter_dimension=0, tiled=True)

    down_grad = row_sum(mm_tn(active, dy_all)).astype(F32)
    d_gate, d_up = back_gated(mm_nt(dy_all, w_d))
    d_gu = jnp.concatenate([d_gate.astype(BF), d_up.astype(BF)], 1)
    gu_sum = swap_ctx(row_sum(mm_tn(n2_all, d_gu)).reshape(nc, depth, -1)).astype(F32)
    gu_sum = gu_sum.reshape(nc, depth, 2, nd, unit)
    gu_sum = jnp.transpose(gu_sum, (2, 1, 3, 0, 4)).reshape(2, depth, -1)
    gate_grad, up_grad = gu_sum[0], gu_sum[1]
    upstream = cotangent[0].astype(F32)
    d_hidden_part, d_gain_two = back_two(own_sum(mm_nt(d_gu, w_gu)))
    d_hidden = upstream + d_hidden_part
    d_attn = whole(d_hidden.astype(BF))
    wo_term = mm_tn(o, d_attn).astype(BF).reshape(need, wo.shape[0], width)
    slots = jnp.zeros((nc, wo.shape[0], width), BF)
    slots = lax.dynamic_update_slice_in_dim(slots, wo_term, first_source, 0)
    back_home = swap_ctx(slots)
    mine = []
    for plane_index in range(nd):
        total_plane = 0
        for i in range(nc):
            if i * span // plane == plane_index:
                total_plane = total_plane + back_home[i].astype(F32)
        mine.append(total_plane)
    wo_grad = lax.psum_scatter(
        jnp.stack(mine).astype(BF), "dp", scatter_dimension=0, tiled=True
    )[0].astype(F32)
    d_o = mm_nt(d_attn, w_o).astype(BF).reshape(seq, kv_heads, -1, HEAD_SIZE)
    d_probs = jnp.einsum("tkgd,skd->kgts", d_o, v, preferred_element_type=F32)
    d_v = jnp.einsum("kgts,tkgd->skd", probs_bf, d_o, preferred_element_type=F32).astype(BF)
    d_scores = (probs * (d_probs - jnp.sum(d_probs * probs, -1, keepdims=True))).astype(BF)
    d_q = jnp.einsum("kgts,skd->tkgd", d_scores, k_rot, preferred_element_type=F32) * scale
    d_k = jnp.einsum("kgts,tkgd->skd", d_scores, q_rot, preferred_element_type=F32) * scale
    d_q, d_gain_q = back_q(d_q.reshape(seq, heads, HEAD_SIZE))
    d_k, d_gain_k = back_k(d_k)
    d_qkv = jnp.concatenate(
        [a.reshape(seq, -1).astype(BF) for a in (d_q, d_k, d_v)], 1
    )
    qkv_sum = swap_ctx(row_sum(mm_tn(n1_all, d_qkv)).reshape(nc, depth, -1)).astype(F32)
    at_k, at_v = heads * HEAD_SIZE, (heads + kv_heads) * HEAD_SIZE

    def columns_back(part, repeat):
        part = part.reshape(nc // repeat, repeat, depth, -1).sum(1)
        return jnp.moveaxis(part, 0, 1).reshape(depth, -1)

    wq_grad = columns_back(qkv_sum[:, :, :at_k], 1)
    wk_grad = columns_back(qkv_sum[:, :, at_k:at_v], copies)
    wv_grad = columns_back(qkv_sum[:, :, at_v:], copies)
    d_input_part, d_gain_one = back_one(own_sum(mm_nt(d_qkv, w_qkv)))
    x_grad = (d_hidden + d_input_part).astype(BF)
    gain_term = jnp.concatenate([d_gain_one, d_gain_two, d_gain_q, d_gain_k])
    gains_grad = lax.psum_scatter(gain_term, ("dp", "ctx"), scatter_dimension=0, tiled=True)
    return (
        output[None], x_grad[None], wq_grad, wk_grad, wv_grad, wo_grad,
        gate_grad, up_grad, down_grad, gains_grad,
    )


MESH = pl.DeviceIdType.MESH
BLOCK = 128
VMEM_BYTES = 64 << 20


class Copies:
    def __init__(self, sends, receives):
        self.sends, self.receives = sends, receives
        self.used = 0

    def take(self, count=1):
        first = self.used
        self.used += count
        if self.used > SLOTS:
            raise ValueError("more semaphores")
        return first

    def to(self, src, dst, device, slot, receive_slot=None):
        receive_slot = slot if receive_slot is None else receive_slot
        return pltpu.make_async_remote_copy(
            src_ref=src,
            dst_ref=dst,
            send_sem=self.sends.at[slot],
            recv_sem=self.receives.at[receive_slot],
            device_id=device,
            device_id_type=MESH,
        )

    def here(self, src, dst, slot):
        return pltpu.make_async_copy(src, dst, self.sends.at[slot])


class Place:
    def __init__(self):
        self.d = lax.axis_index("dp")
        self.c = lax.axis_index("ctx")
        self.z = self.c // 2
        self.p = lax.rem(self.c, 2)

    def at(self, d, c):
        return (d, c)


def meet():
    barrier = pltpu.get_barrier_semaphore()
    d, c = lax.axis_index("dp"), lax.axis_index("ctx")
    partners = [(d, c ^ rel) for rel in range(1, 8)]
    partners += [(d ^ rel, c ^ twin) for rel in range(1, 4) for twin in range(2)]
    for partner in partners:
        pl.semaphore_signal(barrier, inc=1, device_id=partner, device_id_type=MESH)
    pl.semaphore_wait(barrier, len(partners))


def when(condition, then):
    if isinstance(condition, bool):
        if condition:
            then()
    else:
        pl.when(condition)(then)


def rows_at(start, size):
    return pl.ds(pl.multiple_of(start, 16), size)


class Gather:
    def __init__(self, copies, place, buf, parts=2, after=None):
        self.k, self.g, self.buf, self.parts = copies, place, buf, parts
        self.size = BLOCK // parts
        if after is None:
            self.right = copies.take(3 * parts)
            self.left = copies.take(3 * parts)
            self.twin = copies.take(7 * parts)
        else:
            self.right, self.left, self.twin = after.right, after.left, after.twin

    def piece(self, z, p, part):
        return self.buf.at[rows_at((2 * z + p) * BLOCK + part * self.size, self.size)]

    def line(self, step, part, rightwards):
        g = self.g
        z = g.z - step if rightwards else g.z + step
        slot = (self.right if rightwards else self.left) + step * self.parts + part
        piece = self.piece(z, g.p, part)
        to = g.c + 2 if rightwards else g.c - 2
        return self.k.to(piece, piece, (g.d, to), slot)

    def wait_line(self, step, part, rightwards):
        piece = self.piece(self.g.z, self.g.p, part)
        slot = (self.right if rightwards else self.left) + step * self.parts + part
        self.k.to(piece, piece, (self.g.d, self.g.c ^ 1), slot).wait_recv()

    def twins(self, order, z, part):
        piece = self.piece(z, self.g.p, part)
        return self.k.to(piece, piece, (self.g.d, self.g.c ^ 1), self.twin + order * self.parts + part)

    def can_send(self, step, rightwards):
        z = self.g.z
        return (z >= step) & (z < 3) if rightwards else (z + step <= 3) & (z > 0)

    def gets(self, step, rightwards):
        z = self.g.z
        return z >= step + 1 if rightwards else z + step + 1 <= 3

    def start(self):
        for part in range(self.parts):
            self.start_part(part)

    def start_part(self, part):
        for rightwards in (True, False):

            @pl.when(self.can_send(0, rightwards))
            def _():
                self.line(0, part, rightwards).start()

        self.twins(0, self.g.z, part).start()

    def start_line(self, right, left):
        for part in range(self.parts):
            for now, rightwards in ((right, True), (left, False)):

                @pl.when(now & self.can_send(0, rightwards))
                def _():
                    self.line(0, part, rightwards).start()

    def start_twin(self):
        for part in range(self.parts):
            self.twins(0, self.g.z, part).start()

    def step(self, step):
        for part in range(self.parts):
            self.step_part(step, part)

    def step_part(self, step, part):
        for side, rightwards in enumerate((True, False)):
            z = self.g.z - 1 - step if rightwards else self.g.z + 1 + step

            @pl.when(self.gets(step, rightwards))
            def _():
                self.wait_line(step, part, rightwards)

                def on():
                    @pl.when(self.can_send(step + 1, rightwards))
                    def _():
                        self.line(step + 1, part, rightwards).start()

                when(step < 2, on)
                self.twins(1 + 2 * step + side, z, part).start()

    def twin_own(self):
        for part in range(self.parts):
            self.twins(0, self.g.z, part).wait_recv()

    def twin_step(self, step):
        for part in range(self.parts):
            for side, rightwards in enumerate((True, False)):

                @pl.when(self.gets(step, rightwards))
                def _():
                    self.twins(1 + 2 * step + side, self.g.z, part).wait_recv()

    def drain(self):
        for part in range(self.parts):
            self.twins(0, self.g.z, part).wait_send()
            for step in range(3):
                for side, rightwards in enumerate((True, False)):

                    @pl.when(self.can_send(step, rightwards))
                    def _():
                        self.line(step, part, rightwards).wait_send()

                    @pl.when(self.gets(step, rightwards))
                    def _():
                        self.twins(1 + 2 * step + side, self.g.z, part).wait_send()


def add_rows(dst, dst_row, a, a_row, b, b_row, count):
    def body(i, carry):
        at = i * 32
        total = a[rows_at(a_row + at, 32), :].astype(F32) + b[rows_at(b_row + at, 32), :].astype(F32)
        dst[rows_at(dst_row + at, 32), :] = total.astype(dst.dtype)
        return carry

    lax.fori_loop(0, count // 32, body, 0)


class Scatter:
    def __init__(self, copies, place, partial, from_twin, from_left, from_right, parts=2, after=None):
        self.k, self.g = copies, place
        self.partial, self.from_twin = partial, from_twin
        self.from_line = {True: from_left, False: from_right}
        self.parts, self.size = parts, BLOCK // parts
        if after is None:
            self.twin = copies.take(4)
            self.slots = {True: copies.take(3 * parts), False: copies.take(3 * parts)}
        else:
            self.twin, self.slots = after.twin, after.slots

    def row(self, z, p):
        return (2 * z + p) * BLOCK

    def twins(self, z, slot):
        g = self.g
        src = self.partial.at[rows_at(self.row(z, 1 - g.p), BLOCK)]
        dst = self.from_twin.at[rows_at(z * BLOCK, BLOCK)]
        return self.k.to(src, dst, (g.d, g.c ^ 1), self.twin + slot)

    def send_twin(self, z):
        self.twins(z, z).start()

    def take_twin(self, z):
        self.twins(z, z).wait_recv()
        at = self.row(z, self.g.p)
        add_rows(self.partial, at, self.partial, at, self.from_twin, z * BLOCK, BLOCK)

    def target(self, step, rightwards):
        return self.g.z + 3 - step if rightwards else self.g.z - 3 + step

    def can_send(self, step, rightwards):
        z = self.g.z
        return z <= step if rightwards else 3 - z <= step

    def gets(self, step, rightwards):
        z = self.g.z
        return (z >= 1) & (z - 1 <= step) if rightwards else (z <= 2) & (2 - z <= step)

    def line(self, step, rightwards, part):
        g = self.g
        at = self.row(self.target(step, rightwards), g.p) + part * self.size
        src = self.partial.at[rows_at(at, self.size)]
        dst = self.from_line[rightwards].at[rows_at(step * BLOCK + part * self.size, self.size)]
        slot = self.slots[rightwards] + step * self.parts + part
        return self.k.to(src, dst, (g.d, g.c + 2 if rightwards else g.c - 2), slot)

    def wait_line(self, step, rightwards, part):
        src = self.partial.at[pl.ds(0, self.size)]
        dst = self.from_line[rightwards].at[rows_at(step * BLOCK + part * self.size, self.size)]
        slot = self.slots[rightwards] + step * self.parts + part
        self.k.to(src, dst, (self.g.d, self.g.c ^ 1), slot).wait_recv()

    def send(self, step, part):
        for rightwards in (True, False):

            @pl.when(self.can_send(step, rightwards))
            def _():
                self.line(step, rightwards, part).start()

    def start(self):
        for part in range(self.parts):
            self.send(0, part)

    def advance(self, step):
        for part in range(self.parts):
            for rightwards in (True, False):

                @pl.when(self.gets(step, rightwards))
                def _():
                    self.wait_line(step, rightwards, part)

                    def add():
                        z = self.g.z + 2 - step if rightwards else self.g.z - 2 + step
                        at = self.row(z, self.g.p) + part * self.size
                        add_rows(
                            self.partial, at, self.partial, at, self.from_line[rightwards],
                            step * BLOCK + part * self.size, self.size,
                        )

                    when(step < 2, add)

            when(step < 2, lambda: self.send(step + 1, part))

    def finish(self, done, slot=2, part=None):
        g = self.g
        own = self.row(g.z, g.p)
        first, count = (0, BLOCK) if part is None else (part * self.size, self.size)

        def body(i, carry):
            at = first + i * 16
            total = self.partial[rows_at(own + at, 16), :].astype(F32)
            a = self.from_line[True][rows_at(slot * BLOCK + at, 16), :].astype(F32)
            b = self.from_line[False][rows_at(slot * BLOCK + at, 16), :].astype(F32)
            total = total + jnp.where(g.z >= 1, a, 0.0) + jnp.where(g.z <= 2, b, 0.0)
            done(at, total)
            return carry

        lax.fori_loop(0, count // 16, body, 0)

    def send_ends(self, part, *steps):
        for rightwards in (True, False):

            @pl.when(self.g.z == (0 if rightwards else 3))
            def _():
                for step in steps:
                    self.line(step, rightwards, part).start()

    def relay(self, step, part):
        for rightwards in (True, False):

            @pl.when(self.gets(step, rightwards))
            def _():
                self.wait_line(step, rightwards, part)
                z = self.g.z + 2 - step if rightwards else self.g.z - 2 + step
                at = self.row(z, self.g.p) + part * self.size
                add_rows(
                    self.partial, at, self.partial, at, self.from_line[rightwards],
                    step * BLOCK + part * self.size, self.size,
                )
                self.line(step + 1, rightwards, part).start()

    def last(self, done, part):
        for rightwards in (True, False):

            @pl.when(self.gets(2, rightwards))
            def _():
                self.wait_line(2, rightwards, part)

        self.finish(done, part=part)

    def drain(self):
        for z in range(4):
            self.twins(z, z).wait_send()
        for step in range(3):
            for part in range(self.parts):
                for rightwards in (True, False):

                    @pl.when(self.can_send(step, rightwards))
                    def _():
                        self.line(step, rightwards, part).wait_send()


class Spread:
    def __init__(self, copies, place, piece):
        self.k, self.g, self.piece = copies, place, piece
        self.slots = copies.take(6)

    def direct(self, half, rel):
        g = self.g
        piece = self.piece(g.d, half)
        return self.k.to(piece, piece, (g.d ^ rel, g.c), self.slots + 2 * (rel - 1) + half)

    def passed(self, rel):
        g = self.g
        piece = self.piece(g.d ^ (3 - rel), rel - 1)
        return self.k.to(piece, piece, (g.d ^ rel, g.c), self.slots + 4 + rel - 1)

    def start(self):
        for half, rel in ((0, 1), (1, 2), (1, 1), (0, 2)):
            self.direct(half, rel).start()

    def forward(self):
        self.direct(1, 1).wait_recv()
        self.passed(2).start()
        self.direct(0, 2).wait_recv()
        self.passed(1).start()

    def finish(self):
        self.direct(0, 1).wait_recv()
        self.direct(1, 2).wait_recv()
        self.passed(1).wait_recv()
        self.passed(2).wait_recv()

    def drain(self):
        for half, rel in ((0, 1), (1, 2), (1, 1), (0, 2)):
            self.direct(half, rel).wait_send()
        self.passed(1).wait_send()
        self.passed(2).wait_send()


class Direct:
    def __init__(self, copies, place, piece):
        self.k, self.g, self.piece = copies, place, piece
        self.slots = copies.take(3)

    def copy(self, rel):
        piece = self.piece(self.g.d)
        return self.k.to(piece, piece, (self.g.d ^ rel, self.g.c), self.slots + rel - 1)

    def start(self):
        for rel in (1, 2, 3):
            self.copy(rel).start()

    def finish(self):
        for rel in (1, 2, 3):
            self.copy(rel).wait_recv()

    def drain(self):
        for rel in (1, 2, 3):
            self.copy(rel).wait_send()


class Fold:
    def __init__(self, copies, place, piece, got, stage):
        self.k, self.g, self.piece, self.got, self.stage = copies, place, piece, got, stage
        self.slots = copies.take(6)
        self.loads = copies.take(6)

    def first(self, half, passed):
        g = self.g
        rel = 1 + half
        src = self.piece(g.d ^ (3 if passed else rel), half)
        i = 2 * half + passed
        return self.k.to(src, self.got(i), (g.d ^ rel, g.c), self.slots + i)

    def second(self, half):
        g = self.g
        rel = 2 - half
        return self.k.to(
            self.piece(g.d ^ rel, half), self.got(4 + half), (g.d ^ rel, g.c), self.slots + 4 + half
        )

    def load(self, i):
        return self.k.here(self.got(i), self.stage(i), self.loads + i)

    def start(self):
        for passed in (1, 0):
            for half in range(2):
                self.first(half, passed).start()

    def middle(self, add):
        for half in range(2):
            self.first(half, 1).wait_recv()
            self.load(2 * half + 1).start()
        for half in range(2):
            self.load(2 * half + 1).wait()
            add(self.piece(self.g.d ^ (2 - half), half), (self.stage(2 * half + 1),))
            self.second(half).start()

    def final(self, add):
        for half in range(2):
            self.first(half, 0).wait_recv()
            self.load(2 * half).start()
        for half in range(2):
            self.second(half).wait_recv()
            self.load(4 + half).start()
        for half in range(2):
            self.load(2 * half).wait()
            self.load(4 + half).wait()
            add(self.piece(self.g.d, half), (self.stage(2 * half), self.stage(4 + half)))

    def drain(self):
        for half in range(2):
            for passed in range(2):
                self.first(half, passed).wait_send()
            self.second(half).wait_send()


def down_to_units(place, copies, src, dst):
    g, p, d = place, place.p, place.d
    send, receive = copies.take(8), copies.take(12)
    odd = lax.rem(d, 2)
    wide = (src.at[rows_at(p * 64, 128)], dst.at[rows_at(wide_row(p, d), 128)])
    thin = (src.at[rows_at((1 - p) * 128, 64)], dst.at[rows_at(thin_row(d, p), 64)])
    stays = odd == p

    def thin_to(rel, core):
        return copies.to(
            *thin, (d ^ rel, 2 * g.z + odd), send + 4 + rel, receive + 4 + 2 * rel + core
        )

    def start_thin():
        for rel in (1, 2, 3):
            thin_to(rel, p).start()

        @pl.when(stays)
        def _():
            copies.here(*thin, send + 4).start()

        @pl.when(jnp.logical_not(stays))
        def _():
            thin_to(0, p).start()

    copies.here(*wide, send).start()
    spread = Spread(
        copies, g, lambda e, half: dst.at[rows_at(wide_row(p, e) + half * 64, 64)]
    )

    def start_wide():
        copies.here(*wide, send).wait()
        spread.start()

    def finish():
        spread.finish()

        @pl.when(stays)
        def _():
            copies.here(*thin, send + 4).wait()

        @pl.when(jnp.logical_not(stays))
        def _():
            thin_to(0, p).wait_send()

        for rel in (1, 2, 3):
            thin_to(rel, p).wait_send()
        for rel in range(4):

            @pl.when(lax.rem(d ^ rel, 2) == p)
            def _():
                if rel:
                    thin_to(rel, p).wait_recv()
                thin_to(rel, 1 - p).wait_recv()

    return start_thin, start_wide, spread, finish


def unit_row(core, plane):
    return (plane // 2) * 384 + (lax.rem(plane, 2) ^ core) * 256


def wide_row(core, plane):
    return unit_row(core, plane) + core * lax.rem(plane, 2) * 128


def thin_row(plane, core):
    odd = lax.rem(plane, 2)
    return unit_row(odd, plane) + (1 - odd) * 128 + core * 64


def down_to_owners(place, copies, src, dst):
    g, p, d = place, place.p, place.d
    send, receive = copies.take(12), copies.take(8)

    def wide(rel):
        plane = d ^ rel
        a = src.at[rows_at(wide_row(p, plane), 128)]
        b = dst.at[rel, rows_at(p * 64, 128)]
        if rel == 0:
            return copies.here(a, b, send)
        return copies.to(a, b, (plane, g.c), send + rel, receive + rel)

    def thin(rel, core):
        plane = d ^ rel
        a = src.at[rows_at(thin_row(plane, core), 64)]
        b = dst.at[rel, rows_at((1 - core) * 128, 64)]
        return copies.to(
            a, b, (plane, 2 * g.z + core), send + 4 + 2 * rel + core, receive + 4 + rel
        )

    def thin_own():
        a = src.at[rows_at(thin_row(d, p), 64)]
        return copies.here(a, dst.at[0, rows_at((1 - p) * 128, 64)], send + 4 + p)

    def holds(rel):
        return lax.rem(d ^ rel, 2) == p

    def start_wide():
        for rel in (1, 2, 3, 0):
            wide(rel).start()

    def start_thin():
        for rel in (1, 2, 3, 0):

            @pl.when(holds(rel))
            def _():
                if rel:
                    thin(rel, p).start()
                else:
                    thin_own().start()
                thin(rel, 1 - p).start()

    def finish():
        wide(0).wait()
        for rel in (1, 2, 3):
            wide(rel).wait()
        for rel in range(4):

            @pl.when(holds(rel))
            def _():
                if rel:
                    thin(rel, p).wait_send()
                else:
                    thin_own().wait()
                thin(rel, 1 - p).wait_send()

        @pl.when(jnp.logical_not(holds(0)))
        def _():
            thin(0, p).wait_recv()

        for rel in (1, 2, 3):
            thin(rel, p).wait_recv()

    return start_wide, start_thin, finish


UNIT_PARTS = ((0, 256), (256, 128), (384, 256), (640, 128))


def unit_column(j, z, core):
    plane = 2 * (j // 2) + (core if j % 2 == 0 else 1 - core)
    return plane * 1536 + z * 384 + core * (128 if j % 2 == 0 else 256)


def lanes(start, size):
    return pl.ds(pl.multiple_of(start, 128), size)


def nt(left, right):
    return lax.dot_general(left, right, (((1,), (1,)), ((), ())), preferred_element_type=F32)


def tn(left, right):
    return lax.dot_general(left, right, (((0,), (0,)), ((), ())), preferred_element_type=F32)


def layer_kernel(
    x, prefix, wq, wk, wv, wo, wg, wu, wd, gains, cosine, sine, dy,
    output, x_grad, gain_out, out_q, out_k, out_v, out_o, out_g, out_u, out_d,
    n1_kept, got_gu, got_d, got_qkv,
    xs, n1, ys, partial, partial2, from_twin, from_left, from_right, from_twin2, from_left2, from_right2,
    w_qkv, w_o, w_gu, w_d, qkv, raw, o, lse, act, d_gu, hidden, d_hidden, x_own, d_kv, d_qkv,
    wo_mid, wo_back, got_o, gain_buf, gain_acc, gain_one, gain_two, gain_qk, gain_vec, gain_ctx, gain_dp,
    sends, receives,
):
    g = Place()
    k = Copies(sends, receives)
    d, c, z, p = g.d, g.c, g.z, g.p
    meet()
    own = rows_at(c * BLOCK, BLOCK)
    shard = rows_at(d * 512, 512)
    mine = rows_at(d * 512 + c * 64, 64)

    gain_buf[d, c] = gains[...]
    gain_slots = k.take(12)

    def gain_over_ctx(rel):
        return k.to(gain_buf.at[d, c], gain_buf.at[d, c], (d, c ^ rel), gain_slots + rel)

    def gain_over_dp(rel):
        return k.to(gain_buf.at[d], gain_buf.at[d], (d ^ rel, c), gain_slots + 8 + rel)

    for rel in range(1, 8):
        gain_over_ctx(rel).start()

    own_slots = k.take(3)
    own_copies = [
        k.here(x, xs.at[own], own_slots),
        k.here(x, x_own, own_slots + 1),
        k.here(dy, ys.at[own], own_slots + 2),
    ]
    for copy in own_copies:
        copy.start()

    qkv_slots = k.take(8)

    def qkv_to(rel, j):
        other = c ^ rel
        width = 256 if j == 0 else 128
        src = (wq, wk, wv)[j].at[:, lanes(other * width, width)]
        dst = w_qkv.at[mine, pl.ds((0, 256, 384)[j], width)]
        slot = qkv_slots + rel
        return k.to(src, dst, (d, other), slot) if rel else k.here(src, dst, slot)

    def qkv_pieces(rel):
        whole = w_qkv.at[mine]
        slot = qkv_slots + rel
        return k.to(whole, whole, (d, c ^ rel), slot) if rel else k.here(whole, whole, slot)

    for rel in range(8):
        for j in range(3):
            qkv_to(rel, j).start()
    own_copies[0].wait()
    tokens = Gather(k, g, xs)
    tokens.start()
    at_end = (z == 0) | (z == 3)
    gu_slots = k.take(16)

    def gu_to(which, rel, j):
        place, count = UNIT_PARTS[j]
        column = unit_column(j, z ^ (rel // 2), p ^ (rel % 2))
        src = (wg, wu)[which].at[:, lanes(column, count)]
        dst = w_gu.at[mine, pl.ds(which * 768 + place, count)]
        slot = gu_slots + which * 8 + rel
        return k.to(src, dst, (d, c ^ rel), slot) if rel else k.here(src, dst, slot)

    def gu_start(*groups):
        for which in range(2):
            for group in groups:
                for rel in (2 * group, 2 * group + 1):
                    for j in range(4):
                        gu_to(which, rel, j).start()

    @pl.when(at_end)
    def _():
        gu_start(1)


    wo_slots = k.take(20)
    far = c // 4

    def wo_over_dp(rel):
        src, dst = wo.at[rows_at((d ^ rel) * 16, 16)], wo_mid.at[d]
        slot = wo_slots + rel
        return k.to(src, dst, (d ^ rel, c), slot) if rel else k.here(src, dst, slot)

    def wo_over_ctx(rel):
        src, dst = wo_mid.at[z ^ rel], w_o.at[lax.rem(c, 4), rows_at(d * 16, 16)]
        return k.to(
            src, dst, (d, 2 * (z ^ rel) + far), wo_slots + 4 + rel, wo_slots + 8 + lax.rem(c, 4)
        )

    def wo_stay():
        return k.here(
            wo_mid.at[z], w_o.at[lax.rem(c, 4), rows_at(d * 16, 16)], wo_slots + 4
        )

    wo_stays = far == p
    for rel in range(4):
        wo_over_dp(rel).start()

    start_thin, start_wide, spread_wide, finish_down = down_to_units(g, k, wd, w_d)

    for rel in range(1, 8):
        gain_over_ctx(rel).wait_recv()
    for rel in range(1, 4):
        gain_over_dp(rel).start()
    start_thin()
    for rel in range(1, 4):
        gain_over_dp(rel).wait_recv()
    gain_acc[...] = jnp.zeros_like(gain_acc)
    for i in range(32):
        row = gain_buf[i // 8, i % 8][0:8, :].astype(F32)
        row = jnp.concatenate([row, jnp.zeros((8, 128), F32)], 1)
        shift = (8 * i) % 128
        if shift:
            row = pltpu.roll(row, shift, 1)
        first = 136 * i - shift
        gain_acc[:, first : first + 384] += row

    def normalize(block):
        def body(i, carry):
            at = rows_at(block * BLOCK + i * 16, 16)
            v = xs[at, :].astype(F32)
            r = lax.rsqrt(jnp.mean(v * v, -1, keepdims=True) + EPSILON)
            n1[at, :] = (v * r * gain_acc[0:1, 0:2048]).astype(BF)
            return carry

        lax.fori_loop(0, BLOCK // 16, body, 0)

    normalize(c)
    qkv_pieces(0).wait()
    for rel in range(1, 8):
        qkv_pieces(rel).wait_recv()
    spread_qkv = Spread(k, g, lambda e, half: w_qkv.at[rows_at(e * 512 + half * 256, 256)])
    spread_qkv.start()
    tokens.twin_own()
    normalize(c ^ 1)

    def each_side(step, use):
        def side(i, carry):
            chip = jnp.where(i == 0, z - 1 - step, z + 1 + step)

            @pl.when((chip >= 0) & (chip <= 3))
            def _():
                use(chip)

            return carry

        lax.fori_loop(0, 2, side, 0)

    def normalize_chip(chip):
        normalize(2 * chip)
        normalize(2 * chip + 1)

    gain_q, gain_k = gain_acc[0:1, 4096:4224], gain_acc[0:1, 4224:4352]

    def rotated(value, gain, at):
        r = lax.rsqrt(jnp.mean(value * value, -1, keepdims=True) + EPSILON)
        value = value * r * gain
        return value * cosine[at, :] + pltpu.roll(value, 64, 1) * sine[at, :]

    def project(chip):
        at = rows_at(chip * 256, 256)
        product = jnp.dot(n1[at, :], w_qkv[...], preferred_element_type=F32)
        raw[at, :] = product[:, :384]
        for j, gain in ((0, gain_q), (1, gain_q), (2, gain_k)):
            qkv[at, j * 128 : j * 128 + 128] = rotated(
                product[:, j * 128 : j * 128 + 128], gain, at
            ).astype(BF)
        qkv[at, 384:512] = product[:, 384:].astype(BF)

    def project_all(first, last):
        def body(i, carry):
            step = first + i // 2
            chip = jnp.where(lax.rem(i, 2) == 0, z - 1 - step, z + 1 + step)

            @pl.when((chip >= 0) & (chip <= 3) & ((step >= 0) | (lax.rem(i, 2) == 0)))
            def _():
                project(chip)

            return carry

        lax.fori_loop(0, 2 * (last - first), body, 0)

    tokens.step(0)

    @pl.when(jnp.logical_not(at_end))
    def _():
        gu_start(3)

    for rel in range(4):
        if rel == 0:
            wo_over_dp(0).wait()
        else:
            wo_over_dp(rel).wait_recv()
    for rel in range(1, 4):
        wo_over_ctx(rel).start()

    @pl.when(wo_stays)
    def _():
        wo_stay().start()

    @pl.when(jnp.logical_not(wo_stays))
    def _():
        wo_over_ctx(0).start()

    tokens.twin_step(0)
    each_side(0, normalize_chip)
    tokens.step(1)
    own_copies[2].wait()
    upstream = Gather(k, g, ys)
    upstream.start_line(z == 2, z == 1)
    spread_qkv.forward()
    tokens.twin_step(1)
    each_side(1, normalize_chip)
    for i in range(4):

        @pl.when(jnp.logical_not(c == 4 * p + i))
        def _():
            src, dst = wo_mid.at[0], w_o.at[0, rows_at(0, 16)]
            k.to(src, dst, (d, c ^ 1), wo_slots + 4, wo_slots + 8 + i).wait_recv()

    @pl.when(wo_stays)
    def _():
        wo_stay().wait()

    spread_o = Direct(k, g, lambda e: w_o.at[:, rows_at(e * 16, 16)])
    spread_o.start()
    start_wide()
    spread_qkv.finish()
    project_all(-1, 1)
    tokens.step(2)
    tokens.twin_step(2)
    each_side(2, normalize_chip)

    def gu_pieces(which, rel):
        whole = w_gu.at[mine, pl.ds(which * 768, 768)]
        slot = gu_slots + which * 8 + rel
        return k.to(whole, whole, (d, c ^ rel), slot) if rel else k.here(whole, whole, slot)

    def gu_take(which):
        gu_pieces(which, 0).wait()
        for rel in range(1, 8):
            gu_pieces(which, rel).wait_recv()

    @pl.when(at_end)
    def _():
        gu_start(0, 2, 3)

    project_all(1, 3)
    keep_slots = k.take(2)
    keep = k.here(n1, n1_kept, keep_slots)
    keep.start()

    limit = prefix[0]
    scale = HEAD_SIZE**-0.5

    def head_scores(head, at, first_row):
        scores = nt(qkv[at, head * 128 : head * 128 + 128], qkv[:, 256:384]) * scale
        row = first_row + lax.broadcasted_iota(jnp.int32, (256, 1), 0)
        column = lax.broadcasted_iota(jnp.int32, (1, 1024), 1)
        return jnp.where(column < jnp.maximum(row + 1, limit), scores, -1e30)

    def attend(head):
        def body(i, carry):
            at = rows_at(i * 256, 256)
            scores = head_scores(head, at, i * 256)
            top = jnp.max(scores, -1, keepdims=True)
            expo = jnp.exp(scores - top)
            total = jnp.sum(expo, -1, keepdims=True)
            probs = (expo * (1.0 / total)).astype(BF)
            value = jnp.dot(probs, qkv[:, 384:512], preferred_element_type=F32)
            o[at, head * 128 : head * 128 + 128] = value.astype(BF)
            lse[head, at, :] = jnp.broadcast_to(top + jnp.log(total), (256, 128))
            return carry

        lax.fori_loop(0, 4, body, 0)

    attend(0)
    attend(1)

    @pl.when(jnp.logical_not(at_end))
    def _():
        gu_start(0, 1, 2)

    spread_wide.forward()
    tokens.drain()
    spread_o.finish()
    sum_one = Scatter(k, g, partial, from_twin, from_left, from_right)
    for chip in (3, 0, 2, 1):

        def columns(j, carry):
            cols = lanes(j * 512, 512)
            rows = pl.ds(chip * 256, 256)
            value = jnp.dot(
                o[rows, :], w_o[:, :, cols].reshape(256, 512), preferred_element_type=F32
            )
            partial[rows, cols] = value.astype(BF)
            return carry

        lax.fori_loop(0, 4, columns, 0)
        sum_one.send_twin(chip)
    d_hidden[...] = ys[own, :].astype(F32)

    def upstream_goes(step):
        upstream.start_line((step == z) & (z < 2), (step == 3 - z) & (z > 1))


    sum_one.take_twin(3)
    sum_one.take_twin(0)
    sum_one.send_ends(0, 0)
    sum_one.take_twin(2)
    sum_one.take_twin(1)
    sum_one.send_ends(0, 1, 2)
    sum_one.send_ends(1, 0, 1, 2)
    gu_take(0)
    spread_gate = Spread(
        k, g, lambda e, half: w_gu.at[rows_at(e * 512 + half * 256, 256), pl.ds(0, 768)]
    )
    spread_gate.start()
    sum_one.relay(0, 0)
    gu_take(1)
    spread_up = Spread(
        k, g, lambda e, half: w_gu.at[rows_at(e * 512 + half * 256, 256), pl.ds(768, 768)]
    )
    spread_up.start()
    sum_one.relay(1, 0)
    own_copies[1].wait()

    def done_one(at, value):
        rows = rows_at(at, 16)
        h = x_own[rows, :].astype(F32) + value
        r = lax.rsqrt(jnp.mean(h * h, -1, keepdims=True) + EPSILON)
        hidden[rows, :] = h
        xs[rows_at(c * BLOCK + at, 16), :] = (h * r * gain_acc[0:1, 2048:4096]).astype(BF)

    seconds = Gather(k, g, xs, after=tokens)
    sum_one.last(done_one, 0)
    seconds.start_part(0)
    sum_one.relay(0, 1)
    spread_gate.forward()
    sum_one.relay(1, 1)
    seconds.step_part(0, 0)
    sum_one.last(done_one, 1)
    seconds.start_part(1)
    spread_up.forward()
    upstream_goes(0)
    upstream.start_twin()
    seconds.step_part(1, 0)
    seconds.step_part(0, 1)
    upstream_goes(1)
    spread_gate.finish()
    finish_down()
    sum_one.drain()
    keep.wait()
    spread_up.finish()
    sum_two = Scatter(k, g, partial2, from_twin, from_left, from_right, after=sum_one)
    sum_out = Scatter(k, g, partial, from_twin2, from_left2, from_right2, parts=1)

    def feed_forward(chip):
        at = rows_at(chip * 256, 256)

        def units(j, carry):
            cols, up_cols = lanes(j * 256, 256), lanes(768 + j * 256, 256)
            gate = jnp.dot(xs[at, :], w_gu[:, cols], preferred_element_type=F32)
            up = jnp.dot(xs[at, :], w_gu[:, up_cols], preferred_element_type=F32)
            act[at, cols] = (gate * up * (1.0 / (1.0 + jnp.exp(-gate)))).astype(BF)
            d_gu[at, cols] = gate.astype(BF)
            d_gu[at, up_cols] = up.astype(BF)
            return carry

        lax.fori_loop(0, 3, units, 0)

        def columns(j, carry):
            cols = lanes(j * 512, 512)
            partial[at, cols] = jnp.dot(
                act[at, :], w_d[:, cols], preferred_element_type=F32
            ).astype(BF)
            return carry

        lax.fori_loop(0, 4, columns, 0)
        sum_out.send_twin(chip)

    def feed_back(chip):
        at = rows_at(chip * 256, 256)

        def units(j, carry):
            cols, up_cols = lanes(j * 256, 256), lanes(768 + j * 256, 256)
            d_act = nt(ys[at, :], w_d[rows_at(j * 256, 256), :])
            gate, up = d_gu[at, cols].astype(F32), d_gu[at, up_cols].astype(F32)
            sig = 1.0 / (1.0 + jnp.exp(-gate))
            d_gu[at, cols] = (d_act * up * sig * (1.0 + gate * (1.0 - sig))).astype(BF)
            d_gu[at, up_cols] = (d_act * gate * sig).astype(BF)
            return carry

        lax.fori_loop(0, 3, units, 0)

        def columns(j, carry):
            rows = rows_at(j * 512, 512)
            partial2[at, lanes(j * 512, 512)] = nt(d_gu[at, :], w_gu[rows, :]).astype(BF)
            return carry

        lax.fori_loop(0, 4, columns, 0)
        sum_two.send_twin(chip)

    def visit(gather, use, between=None, taken=(0, 0), used=None):
        inner = jnp.where(z <= 1, 1, -1)

        def body(step, carry):
            @pl.when(step == 0)
            def _():
                gather.twin_own()

            @pl.when(step > 0)
            @jax.named_scope("twin")
            def _():
                gather.twin_step(step - 1)

            def side(i, carry):
                chip = jnp.where(i == 0, z + inner * step, z - inner * step)

                @pl.when((chip >= 0) & (chip <= 3) & ((i == 0) | (step > 0)))
                @jax.named_scope("use")
                def _():
                    use(chip)

                if used is not None:

                    @pl.when(i == 0)
                    def _():
                        used(step)

                for part in range(gather.parts):

                    @pl.when((i == 0) & (step >= taken[part]) & (step < 3))
                    @jax.named_scope("arrive")
                    def _():
                        gather.step_part(step, part)

                if between is not None:

                    @pl.when(i == 0)
                    @jax.named_scope("between")
                    def _():
                        between(step)

                return carry

            lax.fori_loop(0, 2, side, 0)
            return carry

        lax.fori_loop(0, 4, body, 0)

    def upstream_passes(step):
        @pl.when(step == 1)
        def _():
            upstream_goes(2)

        @pl.when((step == 2) & jnp.logical_not(at_end))
        def _():
            upstream.step(0)

    visit(seconds, feed_forward, taken=(2, 1), between=upstream_passes)

    @pl.when(at_end)
    def _():
        upstream.step(0)

    for i in (3, 0):
        sum_out.take_twin(i)
    sum_out.start()
    for i in (2, 1):
        sum_out.take_twin(i)

    @pl.when(at_end)
    def _():
        sum_out.advance(0)

    def out_goes(step):
        @pl.when((step == 3) & jnp.logical_not(at_end))
        def _():
            sum_out.advance(0)

    visit(upstream, feed_back, taken=(1, 1), between=out_goes)
    sum_two.take_twin(3)
    sum_two.take_twin(0)
    sum_two.send_ends(0, 0)
    sum_two.take_twin(2)
    sum_two.take_twin(1)
    sum_two.send_ends(0, 1, 2)
    sum_two.send_ends(1, 0, 1)
    for spread in (spread_qkv, spread_o, spread_wide, spread_gate, spread_up):
        spread.drain()
    upstream.drain()
    seconds.drain()
    for rel in range(1, 8):
        qkv_pieces(rel).wait_send()
        for which in range(2):
            gu_pieces(which, rel).wait_send()

    def fold_gu(which):
        cols = pl.ds(which * 768, 768)

        def stage(i):
            block = (0, 4, 1, 5, 2, 3)[i]
            return ys.at[pl.ds((block // 2) * 256, 256), pl.ds((block % 2) * 768, 768)]

        return Fold(
            k, g, lambda e, half: w_gu.at[rows_at(e * 512 + half * 256, 256), cols],
            lambda i: got_gu.at[i, :, cols], stage,
        )

    folds = [fold_gu(0), fold_gu(1)]

    def add_stages(piece, stages):
        def body(i, carry):
            rows = pl.ds(pl.multiple_of(i * 16, 16), 16)
            value = piece[rows, :].astype(F32)
            for stage in stages:
                value = value + stage[rows, :].astype(F32)
            piece[rows, :] = value.astype(BF)
            return carry

        lax.fori_loop(0, 16, body, 0)

    def gu_gradient(which):
        def body(j, carry):
            cols = lanes(j * 512, 512)
            w_gu[rows_at(j * 512, 512), which * 768 : which * 768 + 768] = tn(
                xs[:, cols], d_gu[:, which * 768 : which * 768 + 768]
            ).astype(BF)
            return carry

        lax.fori_loop(0, 4, body, 0)
        folds[which].start()

    def down_gradient(j, carry):
        rows = rows_at(j * 256, 256)
        for i in range(2):
            cols = slice(i * 1024, i * 1024 + 1024)
            w_d[rows, cols] = tn(act[:, lanes(j * 256, 256)], ys[:, cols]).astype(BF)
        return carry

    gu_gradient(0)
    gu_gradient(1)
    load = k.here(n1_kept, xs, keep_slots + 1)
    load.start()
    lax.fori_loop(0, 3, down_gradient, 0)
    start_wide_back, start_thin_back, finish_down_back = down_to_owners(g, k, w_d, got_d)
    sum_two.relay(0, 0)
    folds[0].middle(add_stages)
    sum_two.relay(1, 0)
    gain_two[...] = jnp.zeros_like(gain_two)

    def done_two(at, value):
        rows = rows_at(at, 16)
        there = rows_at(c * BLOCK + at, 16)
        h = hidden[rows, :]
        r = lax.rsqrt(jnp.mean(h * h, -1, keepdims=True) + EPSILON)
        scaled = value * gain_acc[0:1, 2048:4096]
        mean = jnp.mean(h * scaled, -1, keepdims=True)
        d_h = d_hidden[rows, :] + r * scaled - h * (r * r * r * mean)
        part = value * h * r
        gain_two[...] += part[0:8, :] + part[8:16, :]
        d_hidden[rows, :] = d_h
        n1[there, :] = d_h.astype(BF)

    thirds = Gather(k, g, n1, after=tokens)
    sum_two.last(done_two, 0)
    thirds.start_part(0)
    sum_two.send_ends(1, 2)
    sum_two.relay(0, 1)
    sum_two.relay(1, 1)
    thirds.step_part(0, 0)
    sum_two.last(done_two, 1)
    thirds.start_part(1)

    @pl.when(at_end)
    def _():
        sum_out.advance(1)


    folds[1].middle(add_stages)
    start_wide_back()
    thirds.step_part(1, 0)
    thirds.step_part(0, 1)

    sum_two.drain()
    d_kv[...] = jnp.zeros_like(d_kv)
    gain_qk[...] = jnp.zeros_like(gain_qk)

    def unrotated(gradient, value, gain, at):
        gradient = gradient * cosine[at, :] + pltpu.roll(gradient * sine[at, :], 64, 1)
        r = lax.rsqrt(jnp.mean(value * value, -1, keepdims=True) + EPSILON)
        part = gradient * value * r
        gradient = gradient * gain
        mean = jnp.mean(gradient * value, -1, keepdims=True)
        result = gradient * r - value * (r * r * r * mean)
        return result, jnp.sum(part.reshape(-1, 8, 128), 0)

    def attend_back(chip):
        at = rows_at(chip * 256, 256)
        d_o = nt(n1[at, :], w_o[...].reshape(256, 2048)).astype(BF)
        for head in range(2):
            cols = slice(head * 128, head * 128 + 128)
            probs = jnp.exp(head_scores(head, at, chip * 256) - lse[head, at, 0:1])
            d_probs = nt(d_o[:, cols], qkv[:, 384:512])
            delta = jnp.sum(d_probs * probs, -1, keepdims=True)
            d_scores = (probs * (d_probs - delta)).astype(BF)
            d_q = jnp.dot(d_scores, qkv[:, 256:384], preferred_element_type=F32) * scale
            d_kv[:, 0:128] += tn(d_scores, qkv[at, cols]) * scale
            d_kv[:, 128:256] += tn(probs.astype(BF), d_o[:, cols])
            d_q, part = unrotated(d_q, raw[at, cols], gain_q, at)
            d_qkv[at, cols] = d_q.astype(BF)
            gain_qk[:, 0:128] += part

    stage_slots = k.take(14)

    def gu_home(which, rel, j):
        place, count = UNIT_PARTS[j]
        src = w_gu.at[rows_at(d * 512 + (c ^ rel) * 64, 64), pl.ds(which * 768 + place, count)]
        dst = (out_g, out_u)[which].at[:, lanes(unit_column(j, z, p), count)]
        slot = gu_slots + which * 8 + rel
        return k.to(src, dst, (d, c ^ rel), slot) if rel else k.here(src, dst, slot)

    def sum_gu(which):
        folds[which].final(add_stages)
        for rel in range(8):
            for j in range(4):
                gu_home(which, rel, j).start()

    def meanwhile(step):
        @pl.when(step == 1)
        def _():
            @pl.when(jnp.logical_not(at_end))
            def _():
                sum_out.advance(1)

            sum_gu(0)

        @pl.when(step == 2)
        def _():
            sum_gu(1)

    visit(thirds, attend_back, taken=(2, 1), between=meanwhile)

    attn_slots = k.take(8)

    def qkv_rows(e, first, count):
        return d_gu.at[rows_at(lax.rem(e, 2) * 512 + first, count), lanes((e // 2) * 512, 512)]

    def qkv_over_dp(rel):
        return k.to(
            qkv_rows(d ^ rel, 0, 512), got_qkv.at[rel - 1], (d ^ rel, c), attn_slots + rel - 1
        )

    def wo_grad_over_dp(rel):
        src = w_o.at[:, rows_at((d ^ rel) * 16, 16)]
        return k.to(src, got_o.at[rel - 1], (d ^ rel, c), attn_slots + 3 + rel)

    def wo_gradient(j, carry):
        cols = lanes(j * 512, 512)
        w_o[:, :, cols] = tn(o[...], n1[:, cols]).astype(BF).reshape(4, 64, 512)
        return carry

    lax.fori_loop(0, 4, wo_gradient, 0)
    for rel in (1, 2, 3):
        wo_grad_over_dp(rel).start()

    def finish_keys(i, carry):
        at = rows_at(i * 256, 256)
        d_k, part = unrotated(d_kv[at, 0:128], raw[at, 256:384], gain_k, at)
        d_qkv[at, 256:384] = d_k.astype(BF)
        d_qkv[at, 384:512] = d_kv[at, 128:256].astype(BF)
        gain_qk[:, 128:256] += part
        return carry

    lax.fori_loop(0, 4, finish_keys, 0)
    load.wait()

    sum_three = Scatter(k, g, partial2, from_twin, from_left, from_right, after=sum_one)
    for chip in (3, 0, 2, 1):

        def columns(j, carry):
            cols = lanes(j * 512, 512)
            rows = pl.ds(chip * 256, 256)
            value = nt(d_qkv[rows, :], w_qkv[rows_at(j * 512, 512), :])
            partial2[rows, cols] = value.astype(BF)
            return carry

        lax.fori_loop(0, 4, columns, 0)
        sum_three.send_twin(chip)
    sum_three.take_twin(3)
    sum_three.take_twin(0)
    sum_three.start()
    sum_three.take_twin(2)
    sum_three.take_twin(1)
    def qkv_gradient(e, carry):
        cols = lanes(e * 512, 512)
        rows, place = rows_at(lax.rem(e, 2) * 512, 512), lanes((e // 2) * 512, 512)
        d_gu[rows, place] = tn(xs[:, cols], d_qkv[...]).astype(BF)
        return carry

    lax.fori_loop(0, 4, qkv_gradient, 0)
    for rel in (1, 2, 3):
        qkv_over_dp(rel).start()
    start_thin_back()

    def gain_columns(e, carry):
        rows, place = rows_at(lax.rem(e, 2) * 512, 512), lanes((e // 2) * 512, 512)
        product = d_gu[rows, place].astype(F32) * w_qkv[rows_at(e * 512, 512), :].astype(F32)
        gain_one[:, lanes(e * 512, 512)] = nt(jnp.ones((8, 512), BF), product.astype(BF))
        return carry

    lax.fori_loop(0, 4, gain_columns, 0)
    gain_vec[:, 0:2048] = gain_one[0:1, :] / gain_acc[0:1, 0:2048]
    gain_vec[:, 2048:4096] = jnp.sum(gain_two[...], 0, keepdims=True)
    gain_vec[:, 4096:4352] = jnp.sum(gain_qk[...], 0, keepdims=True)
    sum_slots = k.take(12)

    def gain_sum_over_ctx(rel):
        return k.to(gain_vec, gain_ctx.at[rel - 1], (d, c ^ rel), sum_slots + rel)

    def gain_sum_over_dp(rel):
        return k.to(gain_out, gain_dp.at[rel - 1], (d ^ rel, c), sum_slots + 8 + rel)

    for rel in range(1, 8):
        gain_sum_over_ctx(rel).start()
    for rel in (1, 2, 3):
        wo_grad_over_dp(rel).wait()
    for i in range(4):
        rows = rows_at(d * 16, 16)
        value = w_o[i, rows, :].astype(F32)
        for j in range(3):
            value = value + got_o[j, i].astype(F32)
        w_o[i, rows, :] = value.astype(BF)
    back_slots = k.take(20)

    def wo_back_ctx(i):
        src, dst = w_o.at[i, rows_at(d * 16, 16)], wo_back.at[z]
        return k.to(src, dst, (d, 4 * p + i), back_slots + i, back_slots + 4 + z)

    def wo_back_here(i):
        return k.here(w_o.at[i, rows_at(d * 16, 16)], wo_back.at[z], back_slots + i)

    def wo_home(rel):
        src, dst = wo_back.at[d ^ rel], out_o.at[rows_at(d * 16, 16)]
        slot = back_slots + 8 + rel
        return k.to(src, dst, (d ^ rel, c), slot) if rel else k.here(src, dst, slot)

    for i in range(4):

        @pl.when(c == 4 * p + i)
        def _():
            wo_back_here(i).start()

        @pl.when(c != 4 * p + i)
        def _():
            wo_back_ctx(i).start()

    sum_three.advance(0)


    sum_three.advance(1)


    def qkv_home(rel, j):
        other = c ^ rel
        width = 256 if j == 0 else 128
        src = d_gu.at[
            rows_at(lax.rem(d, 2) * 512 + other * 64, 64),
            lanes((d // 2) * 512 + (0, 256, 384)[j], width),
        ]
        dst = (out_q, out_k, out_v)[j].at[:, lanes(c * width, width)]
        slot = qkv_slots + rel
        return k.to(src, dst, (d, other), slot) if rel else k.here(src, dst, slot)

    for rel in (1, 2, 3):
        qkv_over_dp(rel).wait()
    qkv_stage = [
        k.here(
            got_qkv.at[i],
            ys.at[pl.ds(512, 512), pl.ds(i * 512, 512)],
            stage_slots + 11 + i,
        )
        for i in range(3)
    ]
    for copy in qkv_stage:
        copy.start()
    for copy in qkv_stage:
        copy.wait()

    def add_qkv(i, carry):
        at = i * 16
        rows, place = rows_at(lax.rem(d, 2) * 512 + at, 16), lanes((d // 2) * 512, 512)
        value = d_gu[rows, place].astype(F32)
        for j in range(3):
            value = value + ys[rows_at(512 + at, 16), j * 512 : j * 512 + 512].astype(F32)
        d_gu[rows, place] = value.astype(BF)
        return carry

    lax.fori_loop(0, 32, add_qkv, 0)
    for rel in range(8):
        for j in range(3):
            qkv_home(rel, j).start()
    for j in range(4):

        @pl.when(jnp.logical_not((j == z) & wo_stays))
        def _():
            src, dst = w_o.at[0, rows_at(0, 16)], wo_back.at[0]
            k.to(src, dst, (d, c ^ 1), back_slots, back_slots + 4 + j).wait_recv()

    for i in range(4):

        @pl.when(c == 4 * p + i)
        def _():
            wo_back_here(i).wait()

        @pl.when(c != 4 * p + i)
        def _():
            wo_back_ctx(i).wait_send()

    for rel in range(4):
        wo_home(rel).start()

    total = gain_vec[...]
    for rel in range(1, 8):
        gain_sum_over_ctx(rel).wait()
        total = total + gain_ctx[rel - 1]
    gain_out[...] = total
    for rel in range(1, 4):
        gain_sum_over_dp(rel).start()

    sum_out.advance(2)

    def done_out(at, value):
        rows = rows_at(at, 16)
        output[rows, :] = (hidden[rows, :] + value).astype(BF)

    sum_out.finish(done_out)

    finish_down_back()
    stages = [
        k.here(got_d.at[i], ys.at[pl.ds(i * 192, 192)], stage_slots + 6 + i) for i in range(4)
    ]
    for copy in stages:
        copy.start()
    for copy in stages:
        copy.wait()

    def add_down(i, carry):
        at = i * 16
        value = 0.0
        for j in range(4):
            value = value + ys[rows_at(j * 192 + at, 16), :].astype(F32)
        ys[rows_at(at, 16), :] = value.astype(BF)
        return carry

    lax.fori_loop(0, 12, add_down, 0)
    down_home = k.here(ys.at[pl.ds(0, 192)], out_d, stage_slots + 10)
    down_home.start()

    sum_three.advance(2)

    def done_three(at, value):
        rows = rows_at(at, 16)
        v = x_own[rows, :].astype(F32)
        r = lax.rsqrt(jnp.mean(v * v, -1, keepdims=True) + EPSILON)
        scaled = value * gain_acc[0:1, 0:2048]
        mean = jnp.mean(v * scaled, -1, keepdims=True)
        x_grad[rows, :] = (d_hidden[rows, :] + r * scaled - v * (r * r * r * mean)).astype(BF)

    sum_three.finish(done_three)
    total = gain_out[...]
    for rel in range(1, 4):
        gain_sum_over_dp(rel).wait()
        total = total + gain_dp[rel - 1]
    gain_out[...] = total

    for rel in range(8):
        qkv_pieces(rel).wait()
        for which in range(2):
            gu_pieces(which, rel).wait()
        if rel:
            gain_over_ctx(rel).wait_send()
    for rel in range(4):
        wo_home(rel).wait()
        if rel:
            gain_over_dp(rel).wait_send()
            wo_over_dp(rel).wait_send()
            wo_over_ctx(rel).wait_send()

    @pl.when(jnp.logical_not(wo_stays))
    def _():
        wo_over_ctx(0).wait_send()

    down_home.wait()
    for fold in folds:
        fold.drain()
    thirds.drain()
    sum_out.drain()
    sum_three.drain()


def run_layer(x, prefix, wq, wk, wv, wo, wg, wu, wd, gains, cosine, sine, dy):
    width = 2048
    any_space, vmem = pl.BlockSpec(memory_space=pl.ANY), pl.BlockSpec(memory_space=pltpu.VMEM)
    shape, hold = jax.ShapeDtypeStruct, pltpu.VMEM
    return pl.pallas_call(
        layer_kernel,
        out_shape=(
            shape((BLOCK, width), BF), shape((BLOCK, width), BF), shape((1, 4352), F32),
            shape((64, 2048), BF), shape((64, 1024), BF), shape((64, 1024), BF), shape((64, 2048), BF),
            shape((64, 6144), BF), shape((64, 6144), BF), shape((192, 2048), BF),
            shape((1024, width), BF), shape((6, 256, 1536), BF), shape((4, 192, 2048), BF),
            shape((3, 512, 512), BF),
        ),
        in_specs=[any_space, pl.BlockSpec(memory_space=pltpu.SMEM)] + [any_space] * 7 + [vmem] * 3 + [any_space],
        out_specs=(vmem,) * 3 + (any_space,) * 11,
        scratch_shapes=[
            hold((1024, width), BF), hold((1024, width), BF), hold((1024, width), BF),
            hold((1024, width), BF), hold((1024, width), BF),
            hold((512, width), BF), hold((384, width), BF), hold((384, width), BF),
            hold((512, width), BF), hold((384, width), BF), hold((384, width), BF),
            hold((width, 512), BF), hold((4, 64, width), BF), hold((width, 1536), BF), hold((768, width), BF),
            hold((1024, 512), BF), hold((1024, 384), F32), hold((1024, 256), BF), hold((2, 1024, 128), F32),
            hold((1024, 768), BF), hold((1024, 1536), BF),
            hold((BLOCK, width), F32), hold((BLOCK, width), F32), hold((BLOCK, width), BF),
            hold((1024, 256), F32), hold((1024, 512), BF),
            hold((4, 16, width), BF), hold((4, 16, width), BF), hold((3, 4, 16, width), BF),
            hold((4, 8, 16, 256), BF), hold((8, 4608), F32), hold((8, width), F32), hold((8, width), F32),
            hold((8, 256), F32), hold((1, 4352), F32), hold((7, 1, 4352), F32), hold((3, 1, 4352), F32),
            pltpu.SemaphoreType.DMA((SLOTS,)), pltpu.SemaphoreType.DMA((SLOTS,)),
        ],
        compiler_params=pltpu.CompilerParams(
            collective_id=0, has_side_effects=True, vmem_limit_bytes=VMEM_BYTES
        ),
        name="layer",
    )(x, prefix, wq, wk, wv, wo, wg, wu, wd, gains, cosine, sine, dy)


SLOTS = 284


def widen_kernel(*refs):
    narrow, wide = refs[:9], refs[9:18]
    held, turned, sems = refs[18:27], refs[27:34], refs[34]
    loads = [pltpu.make_async_copy(a, b, sems.at[i]) for i, (a, b) in enumerate(zip(narrow, held))]
    stores = [
        pltpu.make_async_copy(a, b, sems.at[9 + i])
        for i, (a, b) in enumerate(zip(turned + held[7:], wide))
    ]
    for copy in loads:
        copy.start()
    for load, store, a, b in zip(loads, stores, held, turned):
        load.wait()

        def body(i, carry):
            rows = rows_at(i * 32, 32)
            b[rows, :] = a[rows, :].astype(F32)
            return carry

        lax.fori_loop(0, a.shape[0] // 32, body, 0)
        store.start()
    for i in (7, 8):
        loads[i].wait()
        stores[i].start()
    for copy in stores:
        copy.wait()


def widen(narrow, same):
    place, shape, hold = pl.BlockSpec(memory_space=pltpu.HBM), jax.ShapeDtypeStruct, pltpu.VMEM
    return pl.pallas_call(
        widen_kernel,
        out_shape=tuple(shape(a.shape, F32) for a in narrow) + tuple(shape(a.shape, BF) for a in same),
        in_specs=[place] * 9,
        out_specs=(place,) * 9,
        scratch_shapes=[hold(a.shape, BF) for a in narrow + same]
        + [hold(a.shape, F32) for a in narrow]
        + [pltpu.SemaphoreType.DMA((18,))],
        compiler_params=pltpu.CompilerParams(vmem_limit_bytes=VMEM_BYTES),
        name="widen",
    )(*narrow, *same)


def rope_tables(length):
    freqs = ROPE_BASE ** (-(np.arange(HEAD_SIZE // 2, dtype=np.float32) * 2.0 / HEAD_SIZE))
    angles = np.arange(length, dtype=np.float32)[:, None] * freqs.astype(np.float32)[None, :]
    cosine, sine = np.cos(angles), np.sin(angles)
    return np.concatenate([cosine, cosine], 1), np.concatenate([-sine, sine], 1)


def with_kernel(layer_input, prefix, wq, wk, wv, wo, w_gate, w_up, w_down, gains, cotangent):
    cosine, sine = rope_tables(layer_input.shape[1] * 8)
    results = run_layer(
        layer_input[0], prefix, wq, wk, wv, wo, w_gate, w_up, w_down,
        jnp.pad(gains.reshape(1, 136), ((0, 15), (0, 120))),
        cosine, sine, cotangent[0],
    )
    output, x_grad, gain_sum = results[:3]
    first = (lax.axis_index("dp") * 8 + lax.axis_index("ctx")) * 136
    gains_grad = lax.dynamic_slice_in_dim(gain_sum[0], first, 136, 0)
    big_first = (8, 7, 9, 3, 6, 4, 5)
    final = widen([results[i] for i in big_first], [output, x_grad])
    wide = tuple(final[big_first.index(i)] for i in range(3, 10))
    return (final[7][None], final[8][None]) + wide + (gains_grad,)


def solution(mesh):
    tokens = P("dp", "ctx", None)
    matrix = P(("dp", "ctx"), None)
    vector = P(("dp", "ctx"))
    small = mesh.shape["dp"] == 4 and mesh.shape["ctx"] == 8
    return jax.shard_map(
        with_kernel if small else general,
        mesh=mesh,
        in_specs=(tokens, P("dp")) + (matrix,) * 7 + (vector, tokens),
        out_specs=(tokens, tokens) + (matrix,) * 7 + (vector,),
        check_vma=False,
    )
```
